128 devices in a mesh: ctx: 32 (over y, z_lo, x), wsh: 4 (over z_hi, core).
Axes of the slice: x: 4, y: 4, z: 4 (z_hi: 2, z_lo: 2; z = z_hi * 2 + z_lo), core: 2. Of those that a mesh axis runs over, the one named last changes fastest.
Arguments:
- tokens: bfloat16 [4, 4096, 1536], P('wsh', 'ctx'), may hold values from -6 to 6
- lengths: int32 [4, 4], replicated, may hold values from 1 to 2048, as said below
- deal: int32 [4, 64], replicated, may hold values from 0 to 63, as said below
- expert_ids: int32 [4, 4096, 2], P('wsh', 'ctx'), may hold values from 0 to 15, all different within a row; in each aligned block of 128 rows (0 to 127, 128 to 255, ..., all dimensions but the last counted through in order) at most 32 rows name the same one
- gain_attn: float32 [1536], P('wsh'), may hold values from 0.5 to 1.5
- w_qkv: float32 [1536, 2560], P('wsh'), may hold values from -0.15625 to 0.15625
- w_out: float32 [1536, 1536], P('wsh'), may hold values from -1.25 to 1.25
- gain_moe: float32 [1536], P('wsh'), may hold values from 0.5 to 1.5
- w_router: float32 [1536, 16], P('wsh'), may hold values from -0.109375 to 0.109375
- w_gate: float32 [32, 1536, 512], P('ctx', 'wsh'), may hold values from -0.15625 to 0.15625
- w_up: float32 [32, 1536, 512], P('ctx', 'wsh'), may hold values from -0.15625 to 0.15625
- w_down: float32 [32, 512, 1536], P('ctx', None, 'wsh'), may hold values from -0.375 to 0.375
- cotangent: bfloat16 [4, 4096, 1536], P('wsh', 'ctx'), may hold values from -6 to 6
Outputs:
- block_output: bfloat16 [4, 4096, 1536], P('wsh', 'ctx')
- d_tokens: bfloat16 [4, 4096, 1536], P('wsh', 'ctx')
- d_gain_attn: float32 [1536], P('wsh')
- d_w_qkv: float32 [1536, 2560], P('wsh')
- d_w_out: float32 [1536, 1536], P('wsh')
- d_gain_moe: float32 [1536], P('wsh')
- d_w_router: float32 [1536, 16], P('wsh')
- d_w_gate: float32 [32, 1536, 512], P('ctx', 'wsh')
- d_w_up: float32 [32, 1536, 512], P('ctx', 'wsh')
- d_w_down: float32 [32, 512, 1536], P('ctx', None, 'wsh')
The draws below stay inside these ranges and needn't reach their ends.
Inputs may be any that keep to these rules, and one draw needn't show every extreme that they name: `lengths`: each row adds up to 4096, and its largest entry is 2048. `deal`: each row is a permutation of 0 to 63 in which the entries at 2 i and 2 i + 1 add up to 63. `expert_ids`: each row names 2 different experts; within the rows of one device (aligned blocks of 128 rows along the first two dimensions) no expert is named by more than 32 rows, and in some blocks one is named by exactly 32.
All inputs are finite; a program needn't handle non-finite values.
Results may differ from the reference program's by a relative error of at most 0.03.
Values may be sent and summed in bfloat16 or wider, within the bound.
A program may use at most 192 MiB of HBM per device.

```python
import math
import jax
import jax.numpy as jnp
import numpy as np
from jax import lax

D = 1536
QUERY_HEADS = 24
KEY_VALUE_HEADS = 8
HEAD_SIZE = 64
FF = 1024
TOP = 2
TOK_DEV = 128
EXPERTS = 16
STREAMS = 4
TOKENS_PER_LANE = 4096
BLK = 64
NBLK = 64
LONGEST = 2048
NSEQ = 4
CAP = 32
FFH = 512
QKV = 2560
N_CTX = 32


def draw_lengths(key, part):
    key = jax.random.fold_in(key, 11)
    rest_total = TOKENS_PER_LANE - LONGEST
    pieces = NSEQ - 1

    def one_row(row_key):
        flip_key, cut_key = jax.random.split(row_key)
        longest_entry = jnp.full((1,), LONGEST, jnp.int32)
        if pieces == 0:
            return longest_entry
        if pieces == 1:
            others = jnp.full((1,), rest_total, jnp.int32)
        else:
            cut_points = jax.random.permutation(cut_key, rest_total - 1)[:pieces - 1].astype(jnp.int32) + 1
            bounds = jnp.concatenate([jnp.zeros((1,), jnp.int32), jnp.sort(cut_points), jnp.full((1,), rest_total, jnp.int32)])
            others = bounds[1:] - bounds[:-1]
        first_long = jax.random.randint(flip_key, (), 0, 2)
        at_front = jnp.concatenate([longest_entry, others])
        at_back = jnp.concatenate([others, longest_entry])
        return jnp.where(first_long == 1, at_front, at_back)
    return jax.vmap(one_row)(jax.random.split(key, STREAMS))


def draw_deal(key, part):
    key = jax.random.fold_in(key, 23)
    half_count = NBLK // 2

    def one_row(row_key):
        order_key, flip_key = jax.random.split(row_key)
        chosen = jax.random.permutation(order_key, half_count).astype(jnp.int32)
        flip_bits = jax.random.randint(flip_key, (half_count,), 0, 2)
        partner = NBLK - 1 - chosen
        first_block = jnp.where(flip_bits == 1, partner, chosen)
        second_block = jnp.where(flip_bits == 1, chosen, partner)
        return jnp.stack([first_block, second_block], axis=1).reshape(NBLK)
    return jax.vmap(one_row)(jax.random.split(key, STREAMS))


def level_of(rng, shape, shards, least, high):
    def one(position, shards_of):
        draws = jax.random.uniform(jax.random.fold_in(jax.random.fold_in(rng, 6), position), (shards_of,), jnp.float32, least / len(shards), high / len(shards))
        return jnp.repeat(jnp.exp(draws), shape[position] // shards_of).reshape((-1,) + (1,) * (len(shape) - position - 1))

    loudness = one(*shards[0])
    for cut in shards[1:]:
        loudness = loudness * one(*cut)
    return loudness


def assign_block(stream_key, own, number, rows, count, top, reach, slope):
    sequence = jax.random.permutation(stream_key, count)
    heavy_load, common = shares(count, rows * top, reach, slope, True), shares(count, rows * top, reach, slope, False)
    places = jnp.arange(count)

    def named(sizes, turn):
        used = int((sizes > 0).sum())
        fixed = max(1, used // 4)
        passed = fixed + (places - fixed + turn * (used - fixed)) % max(1, count - fixed)
        return jnp.zeros((count,), jnp.int32).at[sequence[jnp.where(places < fixed, places, passed)]].set(jnp.asarray(sizes, jnp.int32))

    sizes = jnp.where(number % 4 == 0, named(heavy_load, number // 4), named(common, number - number // 4 - 1))
    mixed = jax.random.permutation(jax.random.fold_in(own, 3), count)
    giver, receiver = mixed[0:count // 2 * 2:2], mixed[1:count // 2 * 2:2]
    room = jnp.minimum(sizes[giver] - 1, reach - sizes[receiver]) // 2
    room = jnp.where((giver == sequence[0]) | (receiver == sequence[0]) | (sizes[receiver] == 0), 0, jnp.maximum(room, 0))
    passed = jax.random.randint(jax.random.fold_in(own, 4), (count // 2,), 0, 1 << 20) % (room + 1)
    sizes = sizes.at[giver].add(-passed).at[receiver].add(passed)
    labels = jnp.searchsorted(jnp.cumsum(sizes), jnp.arange(rows * top), side="right").astype(jnp.int32)
    listing = labels.reshape(top, rows).T
    listing = listing[jax.random.permutation(jax.random.fold_in(own, 1), rows)]
    turn = jax.random.randint(jax.random.fold_in(own, 2), (rows, 1), 0, top)
    return jnp.take_along_axis(listing, (jnp.arange(top)[None, :] + turn) % top, axis=1)


def shares(count, total, most, slope, full):
    loads = [(1 << 20) // math.isqrt(grade ** slope) + 1 for grade in range(1, count + 1)]
    largest = most if full else min(most, max(-(-total // count), total * loads[0] // sum(loads)))
    least = 1 if total - largest >= count - 1 else 0
    counts, rest = [largest] + [least] * (count - 1), total - largest - least * (count - 1)
    while rest > 0:
        movable = [i for i in range(1, count) if counts[i] < largest] or [i for i in range(1, count) if counts[i] < most]
        pool, budget = sum([loads[i] for i in movable]), rest
        for i in movable:
            more = min(most - counts[i], max(1, budget * loads[i] // pool), rest)
            counts[i] = counts[i] + more
            rest = rest - more
    return np.array(counts)


def scatter_about(own_key, dims, width, limit, cuts=(), kind=jnp.bfloat16):
    level = level_of(own_key, dims, cuts, -0.22, 0.18) if cuts else 1.0
    entries = jax.random.normal(own_key, dims, jnp.float32) * width * level
    return jnp.minimum(jnp.maximum(entries, -limit), limit).astype(kind)


def setup_inputs(seed: int = 0) -> dict:
    keys = jax.random.split(jax.random.key(seed), 14)
    tokens = scatter_about(keys[0], (STREAMS, TOKENS_PER_LANE, D), 1.0, 6.0, ((0, 4), (1, 32)))
    lengths = draw_lengths(jax.random.fold_in(keys[13], 71), 0)
    deal = draw_deal(jax.random.fold_in(keys[13], 71), 0)
    expert_ids_keys = jax.random.split(jax.random.fold_in(keys[3], 1), STREAMS * TOKENS_PER_LANE // TOK_DEV)
    expert_ids_turns = jax.random.permutation(jax.random.fold_in(keys[3], 3), STREAMS * TOKENS_PER_LANE // TOK_DEV)
    expert_ids = jax.vmap(lambda own, number: assign_block(jax.random.fold_in(keys[3], 2), own, number, TOK_DEV, EXPERTS, TOP, CAP, 1))(expert_ids_keys, expert_ids_turns).reshape((STREAMS, TOKENS_PER_LANE, TOP))
    gain_attn = jnp.clip(1.0 + 0.1 * jax.random.normal(keys[4], (D,), jnp.float32), 0.5, 1.5)
    w_qkv = scatter_about(keys[5], (D, QKV), D ** -0.5, 0.15625, ((0, 4),), jnp.float32)
    w_out = scatter_about(keys[6], (QUERY_HEADS * HEAD_SIZE, D), (max(1, QUERY_HEADS * HEAD_SIZE // 64)) ** -0.5, 1.25, ((0, 4),), jnp.float32)
    gain_moe = jnp.clip(1.0 + 0.1 * jax.random.normal(keys[7], (D,), jnp.float32), 0.5, 1.5)
    w_router = scatter_about(keys[8], (D, EXPERTS), (2 * D) ** -0.5, 0.109375, ((0, 4),), jnp.float32)
    w_gate = scatter_about(keys[9], (2 * EXPERTS, D, FFH), D ** -0.5, 0.15625, ((0, 32), (1, 4)), jnp.float32)
    w_up = scatter_about(keys[10], (2 * EXPERTS, D, FFH), D ** -0.5, 0.15625, ((0, 32), (1, 4)), jnp.float32)
    w_down = scatter_about(keys[11], (2 * EXPERTS, FFH, D), (max(1, FF // 4)) ** -0.5, 0.375, ((0, 32), (2, 4)), jnp.float32)
    cotangent = scatter_about(keys[12], (STREAMS, TOKENS_PER_LANE, D), 1.0, 6.0, ((0, 4), (1, 32)))
    return {"tokens": tokens, "lengths": lengths, "deal": deal, "expert_ids": expert_ids, "gain_attn": gain_attn, "w_qkv": w_qkv, "w_out": w_out, "gain_moe": gain_moe, "w_router": w_router, "w_gate": w_gate, "w_up": w_up, "w_down": w_down, "cotangent": cotangent}


EPSILON = 1e-05
NEG_BIG = -1e+30
PRECISE = lax.Precision.HIGHEST

@jax.custom_vjp
def low(v):
    return lax.optimization_barrier(v.astype(jnp.bfloat16)).astype(jnp.float32)

@jax.custom_vjp
def low_back(v):
    return v

def low_keep(v):
    return (low(v), None)

def low_pass(kept, grad):
    return (grad,)

def back_keep(v):
    return (v, None)

def back_low(kept, grad):
    return (low(grad),)
low.defvjp(low_keep, low_pass)
low_back.defvjp(back_keep, back_low)

def stream_positions(deal_row, lengths_row, block_rows):
    count_blocks = deal_row.shape[0]
    within = jnp.tile(jnp.arange(block_rows, dtype=jnp.int32), count_blocks)
    positions = jnp.repeat(deal_row * block_rows, block_rows) + within
    bounds = jnp.cumsum(lengths_row)
    documents = lax.optimization_barrier(jnp.sum((bounds[None, :] <= positions[:, None]).astype(jnp.int32), axis=1))
    return (positions, documents)

def rms_norm(values, gain_row):
    return values * lax.rsqrt(lax.optimization_barrier(jnp.mean(values * values, axis=-1, keepdims=True)) + EPSILON) * gain_row

def softmax_last(logits_in):
    top_value = lax.optimization_barrier(jnp.max(logits_in, axis=-1, keepdims=True))
    exponent_terms = jnp.exp(logits_in - top_value)
    return exponent_terms / lax.optimization_barrier(jnp.sum(exponent_terms, axis=-1, keepdims=True))

def attention_stream(query_head_rows, key_head_rows, value_head_rows, positions, documents):
    current_query_block = math.gcd(TOKENS_PER_LANE, 512)
    total_blocks = TOKENS_PER_LANE // current_query_block
    query_group_width = QUERY_HEADS // KEY_VALUE_HEADS

    def one_block(block_input):
        q_block, pos_block, doc_block = block_input
        scores = jnp.einsum('qhgd,khd->hgqk', q_block, key_head_rows, precision=PRECISE) * HEAD_SIZE ** (-0.5)
        scores = low_back(scores)
        allowed = (doc_block[:, None] == documents[None, :]) & (positions[None, :] <= pos_block[:, None])
        probs = low(softmax_last(jnp.where(allowed, scores, NEG_BIG)))
        return jnp.einsum('hgqk,khd->qhgd', probs, value_head_rows, precision=PRECISE)
    query_block_count = query_head_rows.reshape(total_blocks, current_query_block, KEY_VALUE_HEADS, query_group_width, HEAD_SIZE)
    outputs = lax.map(jax.checkpoint(one_block), (query_block_count, positions.reshape(total_blocks, current_query_block), documents.reshape(total_blocks, current_query_block)))
    return outputs.reshape(TOKENS_PER_LANE, QUERY_HEADS * HEAD_SIZE)

def expert_mix(act_moe, gates, ids_stream, gate_weight, up_weight, down_weight):
    per_block = TOK_DEV * TOP
    assign_ids = ids_stream.reshape(N_CTX, per_block)
    assign_hot = (assign_ids[:, :, None] == jnp.arange(EXPERTS, dtype=jnp.int32)[None, None, :]).astype(jnp.int32)
    ranks = lax.optimization_barrier(jnp.sum((jnp.cumsum(assign_hot, axis=1) - 1) * assign_hot, axis=2))
    sources = jnp.arange(N_CTX, dtype=jnp.int32)[:, None]
    slot_ids = ((assign_ids * N_CTX + sources) * CAP + ranks).reshape(-1).astype(jnp.int32)
    slot_total = EXPERTS * N_CTX * CAP
    sentinel = TOKENS_PER_LANE * TOP
    slot_assign = jnp.full((slot_total,), sentinel, jnp.int32).at[slot_ids].set(jnp.arange(sentinel, dtype=jnp.int32))
    slot_token = slot_assign // TOP
    act_pad = jnp.concatenate([act_moe, jnp.zeros((1, D), act_moe.dtype)], axis=0)
    expert_in = jnp.take(act_pad, slot_token, axis=0).reshape(EXPERTS, N_CTX * CAP, D)
    gate_pad = jnp.concatenate([gates.reshape(-1), jnp.zeros((1,), gates.dtype)])
    slot_gate = jnp.take(gate_pad, slot_assign).reshape(EXPERTS, N_CTX * CAP, 1)
    combined = jnp.zeros((EXPERTS, N_CTX * CAP, D), act_moe.dtype)
    for half_index in range(2):
        inputs = low_back(expert_in)
        pre_gate = low_back(jnp.einsum('erd,edf->erf', inputs, gate_weight[half_index::2], precision=PRECISE))
        pre_up = low_back(jnp.einsum('erd,edf->erf', inputs, up_weight[half_index::2], precision=PRECISE))
        hidden = low(pre_gate * jax.nn.sigmoid(pre_gate) * pre_up)
        combined = combined + low_back(low(jnp.einsum('erf,efd->erd', hidden, down_weight[half_index::2], precision=PRECISE)))
    weighted = (slot_gate * combined).reshape(slot_total, D)
    return jax.ops.segment_sum(weighted, slot_token, num_segments=TOKENS_PER_LANE + 1)[:TOKENS_PER_LANE]

def stream_forward(x_stream, lengths_row, deal_row, ids_stream, weights):
    gain_a, qkv_weight, out_weight, gain_m, router_weight, gate_weight, up_weight, down_weight = weights
    positions, documents = stream_positions(deal_row, lengths_row, BLK)
    act_attn = low(rms_norm(x_stream, gain_a))
    query_key_value = low_back(low(jnp.dot(act_attn, qkv_weight, precision=PRECISE)))
    query_group_width = QUERY_HEADS // KEY_VALUE_HEADS
    query_head_rows = query_key_value[:, :QUERY_HEADS * HEAD_SIZE].reshape(TOKENS_PER_LANE, KEY_VALUE_HEADS, query_group_width, HEAD_SIZE)
    key_head_rows = query_key_value[:, QUERY_HEADS * HEAD_SIZE:(QUERY_HEADS + KEY_VALUE_HEADS) * HEAD_SIZE].reshape(TOKENS_PER_LANE, KEY_VALUE_HEADS, HEAD_SIZE)
    value_head_rows = query_key_value[:, (QUERY_HEADS + KEY_VALUE_HEADS) * HEAD_SIZE:].reshape(TOKENS_PER_LANE, KEY_VALUE_HEADS, HEAD_SIZE)
    attn_low = low_back(low(attention_stream(query_head_rows, key_head_rows, value_head_rows, positions, documents)))
    middle = x_stream + low_back(jnp.dot(attn_low, out_weight, precision=PRECISE))
    act_moe = low(rms_norm(middle, gain_m))
    logits = low_back(jnp.dot(act_moe, router_weight, precision=PRECISE))
    gates = softmax_last(jnp.take_along_axis(logits, ids_stream, axis=1))
    return middle + expert_mix(act_moe, gates, ids_stream, gate_weight, up_weight, down_weight)

def reference(tokens, lengths, deal, expert_ids, gain_attn, w_qkv, w_out, gain_moe, w_router, w_gate, w_up, w_down, cotangent):

    def forward_floats(x_all, gain_a, qkv_w, out_w, gain_m, router_w, gate_w, up_w, down_w):
        weights = (low(gain_a), low(qkv_w), low(out_w), low(gain_m), low(router_w), low(gate_w), low(up_w), low(down_w))

        def one_stream(carry_value, stream_input):
            x_stream, lengths_row, deal_row, ids_stream = stream_input
            return (carry_value, stream_forward(x_stream, lengths_row, deal_row, ids_stream, weights))
        _, outputs = lax.scan(one_stream, jnp.zeros((), x_all.dtype), (x_all, lengths, deal, expert_ids))
        return outputs
    outputs, pullback = jax.vjp(forward_floats, tokens.astype(jnp.float32), gain_attn, w_qkv, w_out, gain_moe, w_router, w_gate, w_up, w_down)
    gradients = pullback(cotangent.astype(jnp.float32))
    return (outputs.astype(jnp.bfloat16), gradients[0].astype(jnp.bfloat16), gradients[1], gradients[2], gradients[3], gradients[4], gradients[5], gradients[6], gradients[7], gradients[8])
```

```python
import functools

import jax
import jax.numpy as jnp
from jax import lax
from jax.experimental import pallas as pl
from jax.experimental.pallas import tpu as pltpu
from jax.sharding import PartitionSpec as P

QUERY_HEADS = 24
KEY_VALUE_HEADS = 8
HEAD_SIZE = 64
GROUP = QUERY_HEADS // KEY_VALUE_HEADS
TOP = 2
BLOCK = 64
WIDTH = GROUP * HEAD_SIZE
HEAD_COLUMNS = WIDTH + 2 * HEAD_SIZE
CHUNK = 256

EPSILON = 1e-05
NEG_BIG = -1e30
BF = jnp.bfloat16
F32 = jnp.float32

ROW = [[y * 8 + r for r in range(8)] for y in range(4)]
COLUMN = [[y * 8 + r for y in range(4)] for r in range(8)]
NEAR = [[y * 8 + z * 4 + x for y in range(4) for z in range(2) for x in xs] for xs in ((0, 3), (1, 2))]
OWNERS = [[(2 * e + k) * 4 + w for k in range(2) for w in range(4)] for e in range(16)]
OTHER_HALF = [(c, c ^ 1) for c in range(32)]
OTHER_SIDE = [(w, w ^ 2) for w in range(4)]
OTHER_CORE = [(w, w ^ 1) for w in range(4)]
NEXT_Z = [(c * 4 + w, (c ^ 4) * 4 + (w ^ 2)) for c in range(32) for w in range(4)]
TERMS = [[(y * 8 + r) * 4 + w for y in range(4) for w in range(4)] for r in range(8)]
MOVES = [
    ((y * 8 + r) * 4 + w, ((r % 2) * 16 + y * 4 + w) * 4 + r // 2)
    for r in range(8)
    for y in range(4)
    for w in range(4)
]


def dot(a, b, dims=((1,), (0,))):
    return lax.dot_general(a, b, (dims, ((), ())), preferred_element_type=F32)


NT = ((1,), (1,))
TN = ((0,), (0,))


def block_range(meta, b):
    position = meta[BLOCK + b]
    base = position * BLOCK
    bounds = [meta[80 + i] for i in range(3)]
    lane = lax.broadcasted_iota(jnp.int32, (1, WIDTH), 1)
    query = base + (lane & (BLOCK - 1))
    start = jnp.zeros((1, WIDTH), jnp.int32)
    first = jnp.int32(0)
    for bound in bounds:
        start = jnp.where(query >= bound, bound, start)
        first = jnp.where(base >= bound, bound, first)
    first = (first // 128) * 128
    count = (base + BLOCK - first + CHUNK - 1) // CHUNK
    return query, start, first, count


def allowed_of(key_start, query, start):
    key = key_start + lax.broadcasted_iota(jnp.int32, (CHUNK, WIDTH), 0)
    return (key <= query) & (key >= start)


def stack_heads(rows):
    return jnp.concatenate([rows[:, g * HEAD_SIZE : (g + 1) * HEAD_SIZE] for g in range(GROUP)], axis=0)


def sort_blocks(meta, kv_ref, sorted_ref):
    total = kv_ref.shape[0]

    def one(p, carry):
        source = pl.multiple_of(meta[p] * BLOCK, BLOCK)
        target = pl.multiple_of(p * BLOCK, BLOCK)
        sorted_ref[pl.ds(target, BLOCK), :] = kv_ref[pl.ds(source, BLOCK), :]
        return carry

    lax.fori_loop(0, total // BLOCK, one, 0)
    sorted_ref[total:, :] = jnp.zeros((CHUNK, sorted_ref.shape[1]), sorted_ref.dtype)


def transpose_all(sorted_ref, turned_ref):
    steps = sorted_ref.shape[0] // CHUNK

    def one(i, carry):
        at = pl.multiple_of(i * CHUNK, CHUNK)
        turned_ref[:, pl.ds(at, CHUNK)] = sorted_ref[pl.ds(at, CHUNK), :].T
        return carry

    lax.fori_loop(0, steps, one, 0)


def attention_forward(meta, q_ref, kv_ref, o_ref, lse_ref, sorted_ref, turned_ref):
    sort_blocks(meta, kv_ref, sorted_ref)
    transpose_all(sorted_ref, turned_ref)
    zeros = jnp.zeros((WIDTH, HEAD_SIZE), BF)

    def tile(b, carry):
        query, start, first, count = block_range(meta, b)
        at = pl.multiple_of(b * BLOCK, BLOCK)
        rows = stack_heads(q_ref[pl.ds(at, BLOCK), :]) * jnp.asarray(HEAD_SIZE**-0.5, BF)
        padded = jnp.concatenate([rows, zeros], axis=1)

        def chunk(i, running):
            top, total, acc = running
            key_start = pl.multiple_of(first + i * CHUNK, 128)
            keys = sorted_ref[pl.ds(key_start, CHUNK), :]
            scores = dot(keys, padded, NT)
            scores = jnp.where(allowed_of(key_start, query, start), scores, NEG_BIG)
            top_new = jnp.maximum(top, jnp.max(scores, axis=0, keepdims=True))
            weights = jnp.exp(scores - top_new)
            fade = jnp.exp(top - top_new)
            total = total * fade + jnp.sum(weights, axis=0, keepdims=True)
            acc = acc * fade + dot(turned_ref[:, pl.ds(key_start, CHUNK)], weights.astype(BF))
            return top_new, total, acc

        top, total, acc = lax.fori_loop(
            0,
            count,
            chunk,
            (
                jnp.full((1, WIDTH), NEG_BIG, F32),
                jnp.zeros((1, WIDTH), F32),
                jnp.zeros((2 * HEAD_SIZE, WIDTH), F32),
            ),
        )
        lse_ref[pl.ds(b, 1), :] = top + jnp.log(total)
        result = (acc / total).T[:, HEAD_SIZE:].astype(BF)
        o_ref[pl.ds(at, BLOCK), :] = jnp.concatenate(
            [result[g * BLOCK : (g + 1) * BLOCK] for g in range(GROUP)], axis=1
        )
        return carry

    lax.fori_loop(0, q_ref.shape[0] // BLOCK, tile, 0)


def attention_backward(
    meta, q_ref, kv_ref, o_ref, lse_ref, do_ref, dq_ref, dkv_ref, sorted_ref, turned_ref, total_ref
):
    sort_blocks(meta, kv_ref, sorted_ref)
    transpose_all(sorted_ref, turned_ref)
    total_ref[...] = jnp.zeros_like(total_ref)
    zeros = jnp.zeros((WIDTH, HEAD_SIZE), BF)
    scaling = HEAD_SIZE**-0.5

    def tile(b, carry):
        query, start, first, count = block_range(meta, b)
        at = pl.multiple_of(b * BLOCK, BLOCK)
        rows = stack_heads(q_ref[pl.ds(at, BLOCK), :]) * jnp.asarray(scaling, BF)
        grad = stack_heads(do_ref[pl.ds(at, BLOCK), :])
        value = stack_heads(o_ref[pl.ds(at, BLOCK), :])
        delta = jnp.sum((grad.astype(F32) * value.astype(F32)).T, axis=0, keepdims=True)
        lse = lse_ref[pl.ds(b, 1), :]
        query_pad = jnp.concatenate([rows, zeros], axis=1)
        grad_pad = jnp.concatenate([zeros, grad], axis=1)
        both = jnp.concatenate([query_pad, grad_pad], axis=0)

        def chunk(i, acc):
            key_start = pl.multiple_of(first + i * CHUNK, 128)
            keys = sorted_ref[pl.ds(key_start, CHUNK), :]
            scores = dot(keys, query_pad, NT)
            probs = jnp.where(allowed_of(key_start, query, start), jnp.exp(scores - lse), 0.0)
            d_probs = dot(keys, grad_pad, NT)
            d_scores = (probs * (d_probs - delta)).astype(BF)
            joined = jnp.concatenate([d_scores, probs.astype(BF)], axis=1)
            total_ref[pl.ds(key_start, CHUNK), :] += dot(joined, both)
            return acc + dot(turned_ref[:, pl.ds(key_start, CHUNK)], d_scores)

        acc = lax.fori_loop(0, count, chunk, jnp.zeros((2 * HEAD_SIZE, WIDTH), F32))
        result = (acc * scaling).T[:, :HEAD_SIZE].astype(BF)
        dq_ref[pl.ds(at, BLOCK), :] = jnp.concatenate(
            [result[g * BLOCK : (g + 1) * BLOCK] for g in range(GROUP)], axis=1
        )
        return carry

    lax.fori_loop(0, q_ref.shape[0] // BLOCK, tile, 0)

    def back(p, carry):
        target = pl.multiple_of(meta[p] * BLOCK, BLOCK)
        source = pl.multiple_of(p * BLOCK, BLOCK)
        dkv_ref[pl.ds(target, BLOCK), :] = total_ref[pl.ds(source, BLOCK), :].astype(BF)
        return carry

    lax.fori_loop(0, kv_ref.shape[0] // BLOCK, back, 0)


def local_call(kernel, outs, n_vmem, scratch, name):
    return pl.pallas_call(
        kernel,
        out_shape=outs,
        in_specs=[pl.BlockSpec(memory_space=pltpu.SMEM)] + [pl.BlockSpec(memory_space=pltpu.VMEM)] * n_vmem,
        out_specs=tuple(pl.BlockSpec(memory_space=pltpu.VMEM) for _ in outs),
        scratch_shapes=scratch,
        compiler_params=pltpu.CompilerParams(vmem_limit_bytes=40 * 2**20),
        cost_estimate=pl.CostEstimate(flops=4 * 10**9, bytes_accessed=10**7, transcendentals=4 * 10**6),
        name=name,
    )


def run_forward(meta, q, kv):
    rows, keys = q.shape[0], kv.shape[0]
    return local_call(
        attention_forward,
        (jax.ShapeDtypeStruct((rows, WIDTH), BF), jax.ShapeDtypeStruct((rows // BLOCK, WIDTH), F32)),
        2,
        [pltpu.VMEM((keys + CHUNK, 2 * HEAD_SIZE), BF), pltpu.VMEM((2 * HEAD_SIZE, keys + CHUNK), BF)],
        "attention_forward",
    )(meta, q, kv)


def run_backward(meta, q, kv, o, lse, d_o):
    rows, keys = q.shape[0], kv.shape[0]
    return local_call(
        attention_backward,
        (jax.ShapeDtypeStruct((rows, WIDTH), BF), jax.ShapeDtypeStruct((keys, 2 * HEAD_SIZE), BF)),
        5,
        [
            pltpu.VMEM((keys + CHUNK, 2 * HEAD_SIZE), BF),
            pltpu.VMEM((2 * HEAD_SIZE, keys + CHUNK), BF),
            pltpu.VMEM((keys + CHUNK, 2 * HEAD_SIZE), F32),
        ],
        "attention_backward",
    )(meta, q, kv, o, lse, d_o)


def expert_forward_kernel(x_ref, w_ref, gate_ref, up_ref, hidden_ref, out_ref, acc_ref):
    step = pl.program_id(0)
    quarter = w_ref.shape[2]
    gate = up = 0.0
    for q in range(4):
        part = x_ref[:, q * quarter : (q + 1) * quarter]
        gate += dot(part, w_ref[q, 0])
        up += dot(part, w_ref[q, 1])
    gate_ref[...] = gate
    up_ref[...] = up
    hidden = (gate * jax.nn.sigmoid(gate) * up).astype(BF)
    hidden_ref[...] = hidden

    @pl.when(step == 0)
    def _():
        acc_ref[...] = jnp.zeros_like(acc_ref)

    for q in range(4):
        acc_ref[:, q * quarter : (q + 1) * quarter] += dot(hidden, w_ref[q, 2], NT)

    @pl.when(step == pl.num_programs(0) - 1)
    def _():
        out_ref[...] = acc_ref[...].astype(BF)


def expert_backward_kernel(g_ref, w_ref, gate_ref, up_ref, d_gate_ref, d_up_ref, out_ref, acc_ref):
    step = pl.program_id(0)
    quarter = w_ref.shape[2]
    d_hidden = 0.0
    for q in range(4):
        d_hidden += dot(g_ref[:, q * quarter : (q + 1) * quarter], w_ref[q, 2])
    gate, up = gate_ref[...], up_ref[...]
    sigmoid = jax.nn.sigmoid(gate)
    d_gate = (d_hidden * up * sigmoid * (1.0 + gate * (1.0 - sigmoid))).astype(BF)
    d_up = (d_hidden * (gate * sigmoid)).astype(BF)
    d_gate_ref[...] = d_gate
    d_up_ref[...] = d_up

    @pl.when(step == 0)
    def _():
        acc_ref[...] = jnp.zeros_like(acc_ref)

    for q in range(4):
        acc_ref[:, q * quarter : (q + 1) * quarter] += dot(d_gate, w_ref[q, 0], NT) + dot(d_up, w_ref[q, 1], NT)

    @pl.when(step == pl.num_programs(0) - 1)
    def _():
        out_ref[...] = acc_ref[...].astype(BF)


def expert_gradients_kernel(core_ref, x_ref, g_ref, hidden_ref, d_gate_ref, d_up_ref, out_ref):
    x = x_ref[...].T
    out_ref[0, 0, 0] = dot(x, d_gate_ref[...]).astype(BF)
    out_ref[0, 0, 1] = dot(x, d_up_ref[...]).astype(BF)
    out_ref[0, 0, 2] = dot(g_ref[...].T, hidden_ref[...]).astype(BF)


FF_STEP = 256


def expert_specs(rows, width, weights):
    halves = weights.shape[3] // FF_STEP
    whole = pl.BlockSpec((rows, width), lambda i: (0, 0))
    part = pl.BlockSpec((rows, FF_STEP), lambda i: (0, i))
    weight = pl.BlockSpec((4, 3, weights.shape[2], FF_STEP), lambda i: (i // halves, 0, 0, i % halves))
    return 2 * halves, whole, part, weight


def expert_forward(x, weights):
    rows, width = x.shape
    steps, whole, part, weight = expert_specs(rows, width, weights)
    wide = jax.ShapeDtypeStruct((rows, steps * FF_STEP), F32)
    return pl.pallas_call(
        expert_forward_kernel,
        out_shape=(wide, wide, jax.ShapeDtypeStruct(wide.shape, BF), jax.ShapeDtypeStruct(x.shape, BF)),
        grid=(steps,),
        in_specs=[whole, weight],
        out_specs=(part, part, part, whole),
        scratch_shapes=[pltpu.VMEM((rows, width), F32)],
        compiler_params=pltpu.CompilerParams(vmem_limit_bytes=40 * 2**20),
        cost_estimate=pl.CostEstimate(flops=5 * 10**9, bytes_accessed=16 * 10**6, transcendentals=10**6),
        name="expert_forward",
    )(x, weights)


def expert_backward(g, weights, gate, up):
    rows, width = g.shape
    steps, whole, part, weight = expert_specs(rows, width, weights)
    low = jax.ShapeDtypeStruct(gate.shape, BF)
    return pl.pallas_call(
        expert_backward_kernel,
        out_shape=(low, low, jax.ShapeDtypeStruct(g.shape, BF)),
        grid=(steps,),
        in_specs=[whole, weight, part, part],
        out_specs=(part, part, whole),
        scratch_shapes=[pltpu.VMEM((rows, width), F32)],
        compiler_params=pltpu.CompilerParams(vmem_limit_bytes=40 * 2**20),
        cost_estimate=pl.CostEstimate(flops=5 * 10**9, bytes_accessed=16 * 10**6, transcendentals=10**6),
        name="expert_backward",
    )(g, weights, gate, up)


def expert_gradients(core, x, g, hidden, d_gate, d_up):
    rows, width = x.shape
    half = hidden.shape[1] // 2
    quarter = width // 4
    part = pl.BlockSpec((rows, quarter), lambda k, z, core: (0, 2 * z + core[0]))
    row = pl.BlockSpec((rows, half), lambda k, z, core: (0, k))
    return pl.pallas_call(
        expert_gradients_kernel,
        out_shape=jax.ShapeDtypeStruct((2, 2, 3, quarter, half), BF),
        grid_spec=pltpu.PrefetchScalarGridSpec(
            num_scalar_prefetch=1,
            grid=(2, 2),
            in_specs=[part, part, row, row, row],
            out_specs=pl.BlockSpec((1, 1, 3, quarter, half), lambda k, z, core: (k, z, 0, 0, 0)),
        ),
        compiler_params=pltpu.CompilerParams(vmem_limit_bytes=40 * 2**20),
        cost_estimate=pl.CostEstimate(flops=3 * 10**9, bytes_accessed=8 * 10**6, transcendentals=0),
        name="expert_gradients",
    )(core.reshape(1).astype(jnp.int32), x, g, hidden, d_gate, d_up)


def assemble_kernel(by_row_ref, by_head_ref, qkv_ref, out_ref, rest_ref):
    heads = [by_row_ref[0, h].astype(F32) for h in range(8)]
    ends = (0, WIDTH, WIDTH + HEAD_SIZE, HEAD_COLUMNS)
    qkv_ref[...] = jnp.concatenate([t[:, a:b] for a, b in zip(ends[:-1], ends[1:]) for t in heads], axis=1)
    tail = heads[0]
    for t in heads[1:]:
        tail = tail + t
    rest_ref[...] = tail[:, HEAD_COLUMNS + WIDTH :]
    for parity in range(2):
        parts = [by_head_ref[parity, y, 0, :, HEAD_COLUMNS : HEAD_COLUMNS + WIDTH].astype(F32).T for y in range(4)]
        out_ref[parity * WIDTH : (parity + 1) * WIDTH, :] = jnp.concatenate(parts, axis=1)


def assemble(gathered):
    _, piece, columns = gathered.shape
    shard = 4 * piece
    return pl.pallas_call(
        assemble_kernel,
        out_shape=(
            jax.ShapeDtypeStruct((shard, 8 * HEAD_COLUMNS), F32),
            jax.ShapeDtypeStruct((2 * WIDTH, 4 * shard), F32),
            jax.ShapeDtypeStruct((shard, columns - HEAD_COLUMNS - WIDTH), F32),
        ),
        grid=(4,),
        in_specs=[
            pl.BlockSpec((1, 8, piece, columns), lambda i: (i, 0, 0, 0)),
            pl.BlockSpec((2, 4, 1, piece, columns), lambda i: (0, 0, i, 0, 0)),
        ],
        out_specs=(
            pl.BlockSpec((piece, 8 * HEAD_COLUMNS), lambda i: (i, 0)),
            pl.BlockSpec((2 * WIDTH, shard), lambda i: (0, i)),
            pl.BlockSpec((piece, columns - HEAD_COLUMNS - WIDTH), lambda i: (i, 0)),
        ),
        compiler_params=pltpu.CompilerParams(vmem_limit_bytes=40 * 2**20),
        name="assemble",
    )(gathered.reshape(4, 8, piece, columns), gathered.reshape(2, 4, 4, piece, columns))


MESH = pl.DeviceIdType.MESH
ANY = pl.BlockSpec(memory_space=pl.ANY)


class Copies:
    def __init__(self, send, recv, local):
        self.send, self.recv, self.local = send, recv, local
        self.remote_count = self.local_count = 0
        self.started, self.kept = [], []

    def to(self, source, target, device):
        k = self.remote_count
        self.remote_count += 1
        copy = pltpu.make_async_remote_copy(
            source, target, self.send.at[k], self.recv.at[k], device_id=device, device_id_type=MESH
        )
        copy.start()
        self.started.append(copy)
        return copy

    def keep(self, source, middle, target):
        k = self.local_count
        self.local_count += 2
        first = pltpu.make_async_copy(source, middle, self.local.at[k])
        first.start()
        self.kept.append((first, pltpu.make_async_copy(middle, target, self.local.at[k + 1])))

    def move_kept(self):
        for first, second in self.kept:
            first.wait()
            second.start()

    def finish(self, arrived):
        for copy in self.started:
            copy.wait_send()
            if not any(copy is other for other in arrived):
                copy.wait_recv()
        for _, second in self.kept:
            second.wait()


def meet(devices):
    barrier = pltpu.get_barrier_semaphore()
    for device in devices:
        pl.semaphore_signal(barrier, inc=1, device_id=device, device_id_type=MESH)
    pl.semaphore_wait(barrier, len(devices))


def gather_rows_kernel(
    tok_ref, wp_ref, gain_ref, wo_ref, tok_out, wp_out, gain_out, wo_out, v_tok, v_wp, v_gain, v_wo, send, recv, local
):
    place, stream = lax.axis_index("ctx"), lax.axis_index("wsh")
    x, z = place % 4, (place // 4) % 2
    right, left = {"ctx": place - x + (x + 1) % 4}, {"ctx": place - x + (x + 3) % 4}
    across = place + 4 - 8 * z
    other = {"wsh": stream + 1 - 2 * (stream % 2)}
    far = {"ctx": across, "wsh": (stream + 2) % 4}
    meet([right, left, {"ctx": across}, other, far])
    copies = Copies(send, recv, local)
    half = tok_ref.shape[0] // 2
    own, own_z = z * 4 + x, (1 - z) * 4 + x
    left_id, right_id = z * 4 + (x + 3) % 4, z * 4 + (x + 1) % 4
    left_z, right_z = (1 - z) * 4 + (x + 3) % 4, (1 - z) * 4 + (x + 1) % 4

    def rows(ref, h):
        return ref.at[pl.ds(h * half, half)]

    def spot(block, h):
        return tok_out.at[block, pl.ds(h * half, half)]

    head = place % 8
    far_wp = copies.to(wp_ref.at[across % 8], wp_out.at[stream], far)
    far_gain = copies.to(gain_ref, gain_out.at[stream], far)
    cross = [copies.to(rows(tok_ref, h), spot(own, h), {"ctx": across}) for h in range(2)]
    to_right = [copies.to(rows(tok_ref, h), spot(own, h), right) for h in (0, 1)]
    to_left = [copies.to(rows(tok_ref, h), spot(own, h), left) for h in (1, 0)]
    copies.to(wp_ref.at[head], wp_out.at[stream], other)
    copies.to(gain_ref, gain_out.at[stream], other)
    third = wo_ref.shape[0] // 3
    parts = [pl.ds(i * third, third) for i in range(3)]
    far_wo = [copies.to(wo_ref.at[p], wo_out.at[stream, p], far) for p in parts]
    copies.to(wo_ref, wo_out.at[stream], other)
    copies.keep(tok_ref, v_tok, tok_out.at[own])
    copies.keep(wp_ref.at[head], v_wp, wp_out.at[stream])
    copies.keep(gain_ref, v_gain, gain_out.at[stream])
    copies.keep(wo_ref, v_wo, wo_out.at[stream])
    copies.move_kept()

    arrived = []

    def arrive(copy):
        copy.wait_recv()
        arrived.append(copy)

    far_stream = (stream + 2) % 4
    arrive(far_wp)
    copies.to(wp_out.at[far_stream], wp_out.at[far_stream], other)
    arrive(far_gain)
    copies.to(gain_out.at[far_stream], gain_out.at[far_stream], other)
    arrive(to_right[0])
    copies.to(spot(left_id, 0), spot(left_id, 0), right)
    arrive(to_left[0])
    copies.to(spot(right_id, 1), spot(right_id, 1), left)
    arrive(cross[0])
    arrive(cross[1])
    z_right = [copies.to(spot(own_z, h), spot(own_z, h), right) for h in (0, 1)]
    z_left = [copies.to(spot(own_z, h), spot(own_z, h), left) for h in (1, 0)]
    arrive(z_right[0])
    copies.to(spot(left_z, 0), spot(left_z, 0), right)
    arrive(z_left[0])
    copies.to(spot(right_z, 1), spot(right_z, 1), left)
    for p, copy in zip(parts, far_wo):
        arrive(copy)
        copies.to(wo_out.at[far_stream, p], wo_out.at[far_stream, p], other)
    copies.finish(arrived)


def gather_rows(tok, wp, gain, wo):
    return pl.pallas_call(
        gather_rows_kernel,
        out_shape=(
            jax.ShapeDtypeStruct((8,) + tok.shape, BF),
            jax.ShapeDtypeStruct((4,) + wp.shape[1:], BF),
            jax.ShapeDtypeStruct((4,) + gain.shape, BF),
            jax.ShapeDtypeStruct((4,) + wo.shape, BF),
        ),
        in_specs=[ANY] * 4,
        out_specs=(ANY,) * 4,
        scratch_shapes=[
            pltpu.VMEM(tok.shape, BF),
            pltpu.VMEM(wp.shape[1:], BF),
            pltpu.VMEM(gain.shape, BF),
            pltpu.VMEM(wo.shape, BF),
            pltpu.SemaphoreType.DMA((27,)),
            pltpu.SemaphoreType.DMA((27,)),
            pltpu.SemaphoreType.DMA((8,)),
        ],
        compiler_params=pltpu.CompilerParams(collective_id=1, has_side_effects=True, vmem_limit_bytes=40 * 2**20),
        name="gather_rows",
    )(tok, wp, gain, wo)


def gather_keys_kernel(kv_ref, kv_out, v_kv, send, recv, local):
    place = lax.axis_index("ctx")
    y = place // 8
    up, down = {"ctx": (place + 8) % 32}, {"ctx": (place + 24) % 32}
    meet([up, down])
    copies = Copies(send, recv, local)
    half = kv_ref.shape[0] // 2

    def rows(h):
        return kv_ref.at[pl.ds(h * half, half)]

    def spot(block, h):
        return kv_out.at[block, pl.ds(h * half, half)]

    to_up = [copies.to(rows(h), spot(y, h), up) for h in (0, 1)]
    to_down = [copies.to(rows(h), spot(y, h), down) for h in (1, 0)]
    copies.keep(kv_ref, v_kv, kv_out.at[y])
    copies.move_kept()
    to_up[0].wait_recv()
    copies.to(spot((y + 3) % 4, 0), spot((y + 3) % 4, 0), up)
    to_down[0].wait_recv()
    copies.to(spot((y + 1) % 4, 1), spot((y + 1) % 4, 1), down)
    copies.finish([to_up[0], to_down[0]])


def gather_keys(kv):
    return pl.pallas_call(
        gather_keys_kernel,
        out_shape=jax.ShapeDtypeStruct((4,) + kv.shape, BF),
        in_specs=[ANY],
        out_specs=ANY,
        scratch_shapes=[
            pltpu.VMEM(kv.shape, BF),
            pltpu.SemaphoreType.DMA((6,)),
            pltpu.SemaphoreType.DMA((6,)),
            pltpu.SemaphoreType.DMA((2,)),
        ],
        compiler_params=pltpu.CompilerParams(collective_id=2, has_side_effects=True, vmem_limit_bytes=40 * 2**20),
        name="gather_keys",
    )(kv)


def prepare_kernel(qkv_ref, router_ref, wo_ref, wp_out, wo_out):
    rows = qkv_ref.shape[0]
    experts = router_ref.shape[1]
    wo_out[...] = wo_ref[...].astype(BF)
    router = router_ref[...].astype(BF)
    tail = jnp.zeros((rows, wp_out.shape[2] - HEAD_COLUMNS - experts), BF)
    k_at, v_at = QUERY_HEADS * HEAD_SIZE, (QUERY_HEADS + KEY_VALUE_HEADS) * HEAD_SIZE
    for h in range(KEY_VALUE_HEADS):
        wp_out[h] = jnp.concatenate(
            [
                qkv_ref[:, h * WIDTH : (h + 1) * WIDTH].astype(BF),
                qkv_ref[:, k_at + h * HEAD_SIZE : k_at + (h + 1) * HEAD_SIZE].astype(BF),
                qkv_ref[:, v_at + h * HEAD_SIZE : v_at + (h + 1) * HEAD_SIZE].astype(BF),
                router,
                tail,
            ],
            axis=1,
        )


def prepare(w_qkv, w_router, w_out):
    shard = w_qkv.shape[0]
    step = shard // 3

    def block(n):
        return pl.BlockSpec((step, n), lambda i: (i, 0))

    return pl.pallas_call(
        prepare_kernel,
        out_shape=(
            jax.ShapeDtypeStruct((KEY_VALUE_HEADS, shard, 384), BF),
            jax.ShapeDtypeStruct(w_out.shape, BF),
        ),
        grid=(3,),
        in_specs=[block(w_qkv.shape[1]), block(w_router.shape[1]), block(w_out.shape[1])],
        out_specs=(
            pl.BlockSpec((KEY_VALUE_HEADS, step, 384), lambda i: (0, i, 0)),
            block(w_out.shape[1]),
        ),
        compiler_params=pltpu.CompilerParams(vmem_limit_bytes=40 * 2**20),
        name="prepare",
    )(w_qkv, w_router, w_out)


def input_gradient_kernel(stream_ref, d_qkv_ref, p0, p1, p2, p3, x_ref, d_mid_ref, gain_ref, out_ref, acc_ref):
    step = pl.program_id(0)
    stream = stream_ref[0]

    @pl.when(step == 0)
    def _():
        acc_ref[...] = jnp.zeros_like(acc_ref)

    grad = d_qkv_ref[0]
    for j, piece in enumerate((p0, p1, p2, p3)):
        acc_ref[stream ^ j] += dot(grad, piece[0, :, :HEAD_COLUMNS], NT)

    @pl.when(step == pl.num_programs(0) - 1)
    def _():
        x = x_ref[...].astype(F32)
        scale = rms_scale(x)
        quarter = acc_ref.shape[2]
        inner = 0.0
        for q in range(4):
            at = slice(q * quarter, (q + 1) * quarter)
            inner += jnp.sum(acc_ref[q] * gain_ref[:, at] * x[:, at], axis=-1, keepdims=True)
        inner = inner * (1.0 / x.shape[1])
        for q in range(4):
            at = slice(q * quarter, (q + 1) * quarter)
            out_ref[:, at] = (
                d_mid_ref[:, at] + scale * (acc_ref[q] * gain_ref[:, at]) - x[:, at] * scale**3 * inner
            ).astype(BF)


def input_gradient(stream, d_qkv, pieces, x, d_middle, gain):
    heads, rows, _ = d_qkv.shape
    width = x.shape[1]

    def whole(a):
        return pl.BlockSpec(a.shape, lambda h, s: (0, 0))

    def by_head(a):
        return pl.BlockSpec((1,) + a.shape[1:], lambda h, s: (h, 0, 0))

    gain = gain.reshape(1, width)
    return pl.pallas_call(
        input_gradient_kernel,
        out_shape=jax.ShapeDtypeStruct(x.shape, BF),
        grid_spec=pltpu.PrefetchScalarGridSpec(
            num_scalar_prefetch=1,
            grid=(heads,),
            in_specs=[by_head(d_qkv)] + [by_head(p) for p in pieces] + [whole(x), whole(d_middle), whole(gain)],
            out_specs=whole(x),
            scratch_shapes=[pltpu.VMEM((4, rows, width // 4), F32)],
        ),
        compiler_params=pltpu.CompilerParams(vmem_limit_bytes=40 * 2**20),
        cost_estimate=pl.CostEstimate(flops=10**9, bytes_accessed=12 * 10**6, transcendentals=0),
        name="input_gradient",
    )(stream.reshape(1).astype(jnp.int32), d_qkv, *pieces, x, d_middle, gain)


def swap(x, groups, axis="ctx"):
    return lax.all_to_all(x, axis, 0, 0, axis_index_groups=groups, tiled=True)


def spread(x, groups, count, axis="ctx"):
    return swap(jnp.broadcast_to(x[None], (count,) + x.shape), groups, axis)


def rms_scale(values):
    return lax.rsqrt(jnp.mean(values * values, axis=-1, keepdims=True) + EPSILON)


def body(
    tokens,
    lengths,
    deal,
    expert_ids,
    gain_attn,
    w_qkv,
    w_out,
    gain_moe,
    w_router,
    w_gate,
    w_up,
    w_down,
    cotangent,
):
    stream = lax.axis_index("wsh")
    place = lax.axis_index("ctx")
    rows, width = tokens.shape[1], tokens.shape[2]
    shard = w_qkv.shape[0]
    experts = w_router.shape[1]
    capacity = 2 * rows * TOP // experts
    head = place % 8
    head_row = place // 8
    lengths_row = lax.dynamic_index_in_dim(lengths, stream, 0, keepdims=False)
    deal_row = lax.dynamic_index_in_dim(deal, stream, 0, keepdims=False)
    blocks = deal_row.shape[0]
    block_ids = jnp.arange(blocks, dtype=jnp.int32)
    inverse = jnp.sum(jnp.where(deal_row[None, :] == block_ids[:, None], block_ids[None, :], 0), axis=1)
    own_blocks = lax.dynamic_slice_in_dim(deal_row, head_row * 16, 16)
    meta = jnp.concatenate([inverse, own_blocks, jnp.cumsum(lengths_row)]).astype(jnp.int32)

    q_columns = QUERY_HEADS * HEAD_SIZE
    by_head, own_out = prepare(w_qkv, w_router, w_out)
    own_gains = jnp.concatenate(
        [gain_attn.astype(BF)[None], gain_moe.astype(BF)[None], jnp.zeros((14, shard), BF)], axis=0
    )
    group_tokens, head_full, gains, full_out = gather_rows(tokens[0], by_head, own_gains, own_out)
    head_full = head_full.reshape(width, -1)
    head_weight = head_full[:, :HEAD_COLUMNS]
    full_router = head_full[:, HEAD_COLUMNS : HEAD_COLUMNS + experts]
    gain_first = gains[:, 0].reshape(width).astype(F32)
    gain_second = gains[:, 1].reshape(width).astype(F32)
    full_out = full_out.reshape(q_columns, width)

    w_gate, w_up, w_down, _ = lax.optimization_barrier((w_gate, w_up, w_down, gains))
    expert_shard = jnp.stack([w_gate[0].astype(BF), w_up[0].astype(BF), w_down[0].T.astype(BF)])
    expert_all = lax.all_gather(expert_shard, ("ctx", "wsh"), axis_index_groups=OWNERS)
    far_qkv = lax.ppermute(by_head, ("ctx", "wsh"), NEXT_Z)
    qkv_pieces = [
        by_head,
        lax.ppermute(by_head, "wsh", OTHER_CORE),
        far_qkv,
        lax.ppermute(far_qkv, "wsh", OTHER_CORE),
    ]

    group_x = group_tokens.reshape(8 * rows, width).astype(F32)
    group_act = (group_x * rms_scale(group_x) * gain_first).astype(BF)
    head_qkv = dot(group_act, head_weight).astype(BF)
    kv_all = gather_keys(head_qkv[:, WIDTH:]).reshape(32 * rows, 2 * HEAD_SIZE)
    head_q = head_qkv[:, :WIDTH]
    head_attn, lse = run_forward(meta, head_q, kv_all)
    attn_low = swap(head_attn.reshape(8, rows, WIDTH), ROW).transpose(1, 0, 2).reshape(rows, q_columns)

    x_first = tokens[0].astype(F32)
    middle = x_first + dot(attn_low, full_out)
    scale_second = rms_scale(middle)
    act_moe = (middle * scale_second * gain_second).astype(BF)
    logits = dot(act_moe, full_router)
    choice = expert_ids[0]
    expert_range = jnp.arange(experts, dtype=jnp.int32)
    picked_hot = choice[:, :, None] == expert_range[None, None, :]
    picked = jnp.sum(jnp.where(picked_hot, logits[:, None, :], 0.0), axis=-1)
    picked_exp = jnp.exp(picked - jnp.max(picked, axis=-1, keepdims=True))
    gates = picked_exp / jnp.sum(picked_exp, axis=-1, keepdims=True)
    flat_ids = choice.reshape(-1)
    assign_hot = (flat_ids[:, None] == expert_range[None, :]).astype(jnp.int32)
    ranks = jnp.sum((jnp.cumsum(assign_hot, axis=0) - 1) * assign_hot, axis=1)
    slots = (flat_ids * capacity + ranks).reshape(rows, TOP)
    slot_range = jnp.arange(experts * capacity, dtype=jnp.int32)
    hot = [slots[:, j][:, None] == slot_range[None, :] for j in range(TOP)]
    hot_low = [h.astype(BF) for h in hot]
    hot_any = hot_low[0] + hot_low[1]
    slot_gate = sum(jnp.sum(jnp.where(hot[j], gates[:, j][:, None], 0.0), axis=0) for j in range(TOP))

    send_rows = dot(hot_any, act_moe, TN).astype(BF).reshape(experts, capacity, width)
    send_grads = (slot_gate[:, None] * dot(hot_any, cotangent[0], TN)).astype(BF)
    inputs = swap(send_rows, NEAR).reshape(-1, width)
    inputs, send_grads, expert_all = lax.optimization_barrier((inputs, send_grads, expert_all))
    recv_grads = swap(send_grads.reshape(experts, capacity, width), NEAR).reshape(-1, width)
    pre_gate, pre_up, hidden, expert_out = expert_forward(inputs, expert_all)
    expert_out, recv_grads = lax.optimization_barrier((expert_out, recv_grads))
    back_rows = swap(expert_out.reshape(experts, capacity, width), NEAR).reshape(-1, width)
    d_pre_gate, d_pre_up, d_inputs = expert_backward(recv_grads, expert_all, pre_gate, pre_up)
    d_inputs, d_pre_gate, back_rows, qkv_pieces = lax.optimization_barrier(
        (d_inputs, d_pre_gate, back_rows, qkv_pieces)
    )
    returned = swap(d_inputs.reshape(experts, capacity, width), NEAR).reshape(-1, width)
    core = stream % 2
    send_terms = expert_gradients(1 - core, inputs, recv_grads, hidden, d_pre_gate, d_pre_up)
    recv_terms = lax.ppermute(send_terms, "wsh", OTHER_CORE)
    keep_terms = expert_gradients(core, inputs, recv_grads, hidden, d_pre_gate, d_pre_up)
    returned, keep_terms, recv_terms = lax.optimization_barrier((returned, keep_terms, recv_terms))
    expert_terms = (keep_terms.astype(F32) + recv_terms.astype(F32)).astype(BF)
    half = place % 2
    recv_terms = lax.ppermute(
        lax.dynamic_index_in_dim(expert_terms, 1 - half, 0, keepdims=False), "ctx", OTHER_HALF
    )
    keep_terms = lax.dynamic_index_in_dim(expert_terms, half, 0, keepdims=False)
    expert_terms = (keep_terms.astype(F32) + recv_terms.astype(F32)).astype(BF)
    side = stream // 2
    recv_terms = lax.ppermute(
        lax.dynamic_index_in_dim(expert_terms, 1 - side, 0, keepdims=False), "wsh", OTHER_SIDE
    )
    expert_own = lax.dynamic_index_in_dim(expert_terms, side, 0, keepdims=False).astype(F32) + recv_terms.astype(F32)

    both = [dot(hot_low[j], back_rows) for j in range(TOP)]
    output_rows = (middle + gates[:, :1] * both[0] + gates[:, 1:] * both[1]).astype(BF)
    d_out = cotangent[0].astype(F32)
    d_gates = jnp.stack([jnp.sum(d_out * both[j], axis=-1) for j in range(TOP)], axis=1)
    d_picked = gates * (d_gates - jnp.sum(gates * d_gates, axis=-1, keepdims=True))
    d_logits = jnp.sum(jnp.where(picked_hot, d_picked[:, :, None], 0.0), axis=1).astype(BF)
    d_act_moe = dot(hot_any, returned) + dot(d_logits, full_router, NT)
    d_router_local = dot(act_moe, d_logits, TN)
    d_gain_second = jnp.sum(d_act_moe * middle * scale_second, axis=0)
    scaled = d_act_moe * gain_second
    d_middle = (
        d_out
        + scale_second * scaled
        - middle * scale_second**3 * jnp.mean(scaled * middle, axis=-1, keepdims=True)
    )
    d_branch = d_middle.astype(BF)

    d_attn = dot(d_branch, full_out, NT).astype(BF)
    head_d_attn = swap(d_attn.reshape(rows, 8, WIDTH).transpose(1, 0, 2), ROW).reshape(8 * rows, WIDTH)
    group_branch = lax.all_gather(d_branch, "ctx", axis_index_groups=ROW).reshape(8 * rows, width)
    d_q, d_kv = run_backward(meta, head_q, kv_all, head_attn, lse, head_d_attn)
    d_kv_own = jnp.sum(swap(d_kv.reshape(4, 8 * rows, 2 * HEAD_SIZE), COLUMN).astype(F32), axis=0).astype(BF)
    head_d_qkv = jnp.concatenate([d_q, d_kv_own], axis=1)
    d_qkv = swap(head_d_qkv.reshape(8, rows, HEAD_COLUMNS), ROW)
    d_tokens = input_gradient(stream, d_qkv, qkv_pieces, tokens[0], d_middle, gain_first)

    term = jnp.concatenate(
        [
            dot(group_act, head_d_qkv, TN).astype(BF),
            dot(group_branch, head_attn, TN).astype(BF),
            d_router_local.astype(BF),
            d_gain_second.astype(BF)[:, None],
            jnp.zeros((width, 111), BF),
        ],
        axis=1,
    )
    columns = term.shape[1]
    piece = shard // 4
    term = term.reshape(4, 4, piece, columns).transpose(1, 0, 2, 3).reshape(16, piece, columns)
    summed = jnp.sum(swap(term, TERMS, ("ctx", "wsh")).astype(F32), axis=0).astype(BF)
    out_piece = lax.ppermute(summed[:, HEAD_COLUMNS : HEAD_COLUMNS + WIDTH], ("ctx", "wsh"), MOVES)
    summed = jnp.concatenate([summed[:, :HEAD_COLUMNS], out_piece, summed[:, HEAD_COLUMNS + WIDTH :]], axis=1)
    summed, expert_own = lax.optimization_barrier((summed, expert_own))
    gathered = spread(summed, None, 32)
    d_w_qkv, d_w_out, rest = assemble(gathered)
    d_gain_first = jnp.sum(d_w_qkv * w_qkv.astype(BF).astype(F32), axis=1) / gain_attn.astype(BF).astype(F32)
    return (
        output_rows[None],
        d_tokens[None],
        d_gain_first,
        d_w_qkv,
        d_w_out,
        rest[:, experts],
        rest[:, :experts],
        expert_own[0][None],
        expert_own[1][None],
        expert_own[2].T[None],
    )


def solution(mesh):
    placed = (
        P("wsh", "ctx", None),
        P(),
        P(),
        P("wsh", "ctx", None),
        P("wsh"),
        P("wsh", None),
        P("wsh", None),
        P("wsh"),
        P("wsh", None),
        P("ctx", "wsh", None),
        P("ctx", "wsh", None),
        P("ctx", None, "wsh"),
        P("wsh", "ctx", None),
    )
    return jax.shard_map(
        body,
        mesh=mesh,
        in_specs=placed,
        out_specs=(
            P("wsh", "ctx", None),
            P("wsh", "ctx", None),
            P("wsh"),
            P("wsh", None),
            P("wsh", None),
            P("wsh"),
            P("wsh", None),
            P("ctx", "wsh", None),
            P("ctx", "wsh", None),
            P("ctx", None, "wsh"),
        ),
        check_vma=False,
    )
```

```python
import functools

import jax
import jax.numpy as jnp
from jax import lax
from jax.experimental import pallas as pl
from jax.experimental.pallas import tpu as pltpu
from jax.sharding import PartitionSpec as P

QUERY_HEADS = 24
KEY_VALUE_HEADS = 8
HEAD_SIZE = 64
GROUP = QUERY_HEADS // KEY_VALUE_HEADS
TOP = 2
BLOCK = 64
WIDTH = GROUP * HEAD_SIZE
HEAD_COLUMNS = WIDTH + 2 * HEAD_SIZE
CHUNK = 512
LANES = 3
TURN = 256

EPSILON = 1e-05
NEG_BIG = -1e30
BF = jnp.bfloat16
F32 = jnp.float32

def turned(index):
    return index % 4 * 8 + index // 4 % 2 * 4 + index // 8


ROW = [[turned(y * 8 + r) for r in range(8)] for y in range(4)]
OWNERS = [[(2 * e + k) * 4 + w for k in range(2) for w in range(4)] for e in range(16)]
OTHER_HALF = [(c, c ^ 1) for c in range(32)]
OTHER_SIDE = [(w, w ^ 2) for w in range(4)]
OTHER_CORE = [(w, w ^ 1) for w in range(4)]
NEXT_Z = [(c * 4 + w, (c ^ 4) * 4 + (w ^ 2)) for c in range(32) for w in range(4)]
MOVES = [
    (turned(y * 8 + r) * 4 + w, turned((r % 2) * 16 + y * 4 + w) * 4 + r // 2)
    for r in range(8)
    for y in range(4)
    for w in range(4)
]


def dot(a, b, dims=((1,), (0,))):
    return lax.dot_general(a, b, (dims, ((), ())), preferred_element_type=F32)


NT = ((1,), (1,))
TN = ((0,), (0,))


def block_range(meta, b):
    base = meta[BLOCK + b] * BLOCK
    lane = lax.broadcasted_iota(jnp.int32, (1, WIDTH), 1)
    query = base + (lane & (BLOCK - 1))
    start = jnp.zeros((1, WIDTH), jnp.int32)
    first = jnp.int32(0)
    for i in range(3):
        bound = meta[80 + i]
        start = jnp.where(query >= bound, bound, start)
        first = jnp.where(base >= bound, bound, first)
    first = (first // 128) * 128
    count = (base + BLOCK - first + CHUNK - 1) // CHUNK
    return query, start, first, count


def list_work(meta, blocks, block_s, key_s):
    def one(b, n):
        _, _, first, count = block_range(meta, b)

        def put(i, n):
            block_s[n] = b
            key_s[n] = first + i * CHUNK
            return n + 1

        return lax.fori_loop(0, count, put, n)

    total = lax.fori_loop(0, blocks, one, jnp.int32(0))
    for i in range(LANES):
        block_s[total + i] = blocks
        key_s[total + i] = 0
    return (total + LANES - 1) // LANES


def allowed_of(key_start, query, start):
    key = key_start + lax.broadcasted_iota(jnp.int32, (CHUNK, WIDTH), 0)
    return (key <= query) & (key >= start)


def stack_heads(rows):
    return jnp.concatenate([rows[:, g * HEAD_SIZE : (g + 1) * HEAD_SIZE] for g in range(GROUP)], axis=0)


def sort_blocks(meta, kv_ref, sorted_ref):
    total = kv_ref.shape[0]

    def one(p, carry):
        source = pl.multiple_of(meta[p] * BLOCK, BLOCK)
        target = pl.multiple_of(p * BLOCK, BLOCK)
        sorted_ref[pl.ds(target, BLOCK), :] = kv_ref[pl.ds(source, BLOCK), :]
        return carry

    lax.fori_loop(0, total // BLOCK, one, 0, unroll=8)
    sorted_ref[total:, :] = jnp.zeros((CHUNK, sorted_ref.shape[1]), sorted_ref.dtype)


def transpose_all(sorted_ref, turned_ref):
    steps = sorted_ref.shape[0] // TURN

    def one(i, carry):
        at = pl.multiple_of(i * TURN, TURN)
        turned_ref[:, pl.ds(at, TURN)] = sorted_ref[pl.ds(at, TURN), :].T
        return carry

    lax.fori_loop(0, steps, one, 0)


def attention_forward(
    meta, q_ref, kv_ref, o_ref, lse_ref,
    sorted_ref, turned_ref, pad_ref, query_ref, start_ref, top_ref, total_ref, acc_ref, block_s, key_s,
):
    blocks = q_ref.shape[0] // BLOCK
    sort_blocks(meta, kv_ref, sorted_ref)
    transpose_all(sorted_ref, turned_ref)
    share = list_work(meta, blocks, block_s, key_s)
    zeros = jnp.zeros((WIDTH, HEAD_SIZE), BF)
    top_ref[...] = jnp.full(top_ref.shape, NEG_BIG, F32)
    total_ref[...] = jnp.zeros_like(total_ref)
    acc_ref[...] = jnp.zeros_like(acc_ref)
    query_ref[blocks] = jnp.full((1, WIDTH), -1, jnp.int32)
    start_ref[blocks] = jnp.zeros((1, WIDTH), jnp.int32)
    pad_ref[blocks] = jnp.zeros((WIDTH, 2 * HEAD_SIZE), BF)

    def prepare_block(b, carry):
        query_ref[b], start_ref[b], _, _ = block_range(meta, b)
        at = pl.multiple_of(b * BLOCK, BLOCK)
        rows = stack_heads(q_ref[pl.ds(at, BLOCK), :]) * jnp.asarray(HEAD_SIZE**-0.5, BF)
        pad_ref[b] = jnp.concatenate([rows, zeros], axis=1)
        return carry

    lax.fori_loop(0, blocks, prepare_block, 0, unroll=4)

    def work(i, carry):
        blocks_now = [block_s[lane * share + i] for lane in range(LANES)]
        starts_now = [pl.multiple_of(key_s[lane * share + i], 128) for lane in range(LANES)]
        results = []
        for b, key_start in zip(blocks_now, starts_now):
            scores = dot(sorted_ref[pl.ds(key_start, CHUNK), :], pad_ref[b], NT)
            scores = jnp.where(allowed_of(key_start, query_ref[b], start_ref[b]), scores, NEG_BIG)
            top = top_ref[b]
            top_new = jnp.maximum(top, jnp.max(scores, axis=0, keepdims=True))
            weights = jnp.exp(scores - top_new)
            fade = jnp.exp(top - top_new)
            total = total_ref[b] * fade + jnp.sum(weights, axis=0, keepdims=True)
            values = turned_ref[HEAD_SIZE:, pl.ds(key_start, CHUNK)]
            results.append((top_new, total, acc_ref[b] * fade + dot(values, weights.astype(BF))))
        for b, (top, total, acc) in zip(blocks_now, results):
            top_ref[b] = top
            total_ref[b] = total
            acc_ref[b] = acc
        return carry

    lax.fori_loop(0, share, work, 0)

    def finish_block(b, carry):
        at = pl.multiple_of(b * BLOCK, BLOCK)
        total = total_ref[b]
        lse_ref[b] = top_ref[b] + jnp.log(total)
        result = (acc_ref[b] / total).T.astype(BF)
        o_ref[pl.ds(at, BLOCK), :] = jnp.concatenate(
            [result[g * BLOCK : (g + 1) * BLOCK] for g in range(GROUP)], axis=1
        )
        return carry

    lax.fori_loop(0, blocks, finish_block, 0, unroll=4)


def attention_backward(
    meta, q_ref, kv_ref, o_ref, lse_ref, do_ref, dq_ref, dkv_ref,
    sorted_ref, turned_ref, total_ref, both_ref, query_ref, start_ref, delta_ref, acc_ref, block_s, key_s,
):
    blocks = q_ref.shape[0] // BLOCK
    sort_blocks(meta, kv_ref, sorted_ref)
    transpose_all(sorted_ref, turned_ref)
    share = list_work(meta, blocks, block_s, key_s)
    total_ref[...] = jnp.zeros_like(total_ref)
    acc_ref[...] = jnp.zeros_like(acc_ref)
    query_ref[blocks] = jnp.full((1, WIDTH), -1, jnp.int32)
    start_ref[blocks] = jnp.zeros((1, WIDTH), jnp.int32)
    delta_ref[blocks] = jnp.zeros((1, WIDTH), F32)
    both_ref[blocks] = jnp.zeros((2 * WIDTH, 2 * HEAD_SIZE), BF)
    zeros = jnp.zeros((WIDTH, HEAD_SIZE), BF)
    scaling = HEAD_SIZE**-0.5

    def prepare_block(b, carry):
        query_ref[b], start_ref[b], _, _ = block_range(meta, b)
        at = pl.multiple_of(b * BLOCK, BLOCK)
        rows = stack_heads(q_ref[pl.ds(at, BLOCK), :]) * jnp.asarray(scaling, BF)
        grad = stack_heads(do_ref[pl.ds(at, BLOCK), :])
        value = stack_heads(o_ref[pl.ds(at, BLOCK), :])
        delta_ref[b] = jnp.sum((grad.astype(F32) * value.astype(F32)).T, axis=0, keepdims=True)
        both_ref[b, :WIDTH] = jnp.concatenate([rows, zeros], axis=1)
        both_ref[b, WIDTH:] = jnp.concatenate([zeros, grad], axis=1)
        return carry

    lax.fori_loop(0, blocks, prepare_block, 0, unroll=4)

    def work(i, carry):
        blocks_now = [block_s[lane * share + i] for lane in range(LANES)]
        starts_now = [pl.multiple_of(key_s[lane * share + i], 128) for lane in range(LANES)]
        results = []
        for b, key_start in zip(blocks_now, starts_now):
            keys = sorted_ref[pl.ds(key_start, CHUNK), :]
            scores = dot(keys, both_ref[b, :WIDTH], NT)
            d_probs = dot(keys, both_ref[b, WIDTH:], NT)
            allowed = allowed_of(key_start, query_ref[b], start_ref[b])
            probs = jnp.where(allowed, jnp.exp(scores - lse_ref[b]), 0.0)
            d_scores = (probs * (d_probs - delta_ref[b])).astype(BF)
            joined = jnp.concatenate([d_scores, probs.astype(BF)], axis=1)
            turned = turned_ref[:HEAD_SIZE, pl.ds(key_start, CHUNK)]
            results.append((acc_ref[b] + dot(turned, d_scores), dot(joined, both_ref[b])))
        for b, key_start, (acc, d_keys) in zip(blocks_now, starts_now, results):
            acc_ref[b] = acc
            total_ref[pl.ds(key_start, CHUNK), :] += d_keys
        return carry

    lax.fori_loop(0, share, work, 0)

    def finish_block(b, carry):
        at = pl.multiple_of(b * BLOCK, BLOCK)
        result = (acc_ref[b] * scaling).T.astype(BF)
        dq_ref[pl.ds(at, BLOCK), :] = jnp.concatenate(
            [result[g * BLOCK : (g + 1) * BLOCK] for g in range(GROUP)], axis=1
        )
        return carry

    lax.fori_loop(0, blocks, finish_block, 0, unroll=4)

    def back(p, carry):
        target = pl.multiple_of(meta[p] * BLOCK, BLOCK)
        source = pl.multiple_of(p * BLOCK, BLOCK)
        dkv_ref[pl.ds(target, BLOCK), :] = total_ref[pl.ds(source, BLOCK), :].astype(BF)
        return carry

    lax.fori_loop(0, kv_ref.shape[0] // BLOCK, back, 0, unroll=8)


def local_call(kernel, outs, n_vmem, scratch, name):
    return pl.pallas_call(
        kernel,
        out_shape=outs,
        in_specs=[pl.BlockSpec(memory_space=pltpu.SMEM)] + [pl.BlockSpec(memory_space=pltpu.VMEM)] * n_vmem,
        out_specs=tuple(pl.BlockSpec(memory_space=pltpu.VMEM) for _ in outs),
        scratch_shapes=scratch,
        compiler_params=pltpu.CompilerParams(vmem_limit_bytes=40 * 2**20),
        cost_estimate=pl.CostEstimate(flops=4 * 10**9, bytes_accessed=10**7, transcendentals=4 * 10**6),
        name=name,
    )


def work_scratch(rows, keys):
    blocks = rows // BLOCK
    most = blocks * (keys // CHUNK + 1) + LANES
    return [pltpu.SMEM((most,), jnp.int32), pltpu.SMEM((most,), jnp.int32)]


def run_forward(meta, q, kv):
    rows, keys = q.shape[0], kv.shape[0]
    blocks = rows // BLOCK
    line = (blocks + 1, 1, WIDTH)
    return local_call(
        attention_forward,
        (jax.ShapeDtypeStruct((rows, WIDTH), BF), jax.ShapeDtypeStruct(line, F32)),
        2,
        [
            pltpu.VMEM((keys + CHUNK, 2 * HEAD_SIZE), BF),
            pltpu.VMEM((2 * HEAD_SIZE, keys + CHUNK), BF),
            pltpu.VMEM((blocks + 1, WIDTH, 2 * HEAD_SIZE), BF),
            pltpu.VMEM(line, jnp.int32),
            pltpu.VMEM(line, jnp.int32),
            pltpu.VMEM(line, F32),
            pltpu.VMEM(line, F32),
            pltpu.VMEM((blocks + 1, HEAD_SIZE, WIDTH), F32),
        ]
        + work_scratch(rows, keys),
        "attention_forward",
    )(meta, q, kv)


def run_backward(meta, q, kv, o, lse, d_o):
    rows, keys = q.shape[0], kv.shape[0]
    blocks = rows // BLOCK
    line = (blocks + 1, 1, WIDTH)
    return local_call(
        attention_backward,
        (jax.ShapeDtypeStruct((rows, WIDTH), BF), jax.ShapeDtypeStruct((keys, 2 * HEAD_SIZE), BF)),
        5,
        [
            pltpu.VMEM((keys + CHUNK, 2 * HEAD_SIZE), BF),
            pltpu.VMEM((2 * HEAD_SIZE, keys + CHUNK), BF),
            pltpu.VMEM((keys + CHUNK, 2 * HEAD_SIZE), F32),
            pltpu.VMEM((blocks + 1, 2 * WIDTH, 2 * HEAD_SIZE), BF),
            pltpu.VMEM(line, jnp.int32),
            pltpu.VMEM(line, jnp.int32),
            pltpu.VMEM(line, F32),
            pltpu.VMEM((blocks + 1, HEAD_SIZE, WIDTH), F32),
        ]
        + work_scratch(rows, keys),
        "attention_backward",
    )(meta, q, kv, o, lse, d_o)


def exchange_terms_kernel(kv_ref, out_ref, kv_to, out_to, v_kv, v_out, send, recv, local):
    place, stream = turned(lax.axis_index("ctx")), lax.axis_index("wsh")
    y = place // 8
    peers = []
    for k in range(1, 16):
        peers.append(((y + k // 4) % 4, (stream + k % 4) % 4))
    meet([{"ctx": turned(place % 8 + 8 * py), "wsh": pw} for py, pw in peers])
    copies = Copies(send, recv, local)
    for k in (8, 4, 12):
        py, _ = peers[k - 1]
        copies.to(kv_ref.at[py], kv_to.at[y], {"ctx": turned(place % 8 + 8 * py)})
    for py, pw in peers:
        copies.to(out_ref.at[py, pw], out_to.at[y, stream], {"ctx": turned(place % 8 + 8 * py), "wsh": pw})
    copies.keep(kv_ref.at[y], v_kv, kv_to.at[y])
    copies.keep(out_ref.at[y, stream], v_out, out_to.at[y, stream])
    copies.move_kept()
    copies.finish([])


def exchange_terms(kv, out):
    return pl.pallas_call(
        exchange_terms_kernel,
        out_shape=(jax.ShapeDtypeStruct(kv.shape, BF), jax.ShapeDtypeStruct(out.shape, BF)),
        in_specs=[ANY, ANY],
        out_specs=(ANY, ANY),
        scratch_shapes=[
            pltpu.VMEM(kv.shape[1:], BF),
            pltpu.VMEM(out.shape[2:], BF),
            pltpu.SemaphoreType.DMA((18,)),
            pltpu.SemaphoreType.DMA((18,)),
            pltpu.SemaphoreType.DMA((4,)),
        ],
        compiler_params=pltpu.CompilerParams(collective_id=3, has_side_effects=True, vmem_limit_bytes=40 * 2**20),
        name="exchange_terms",
    )(kv, out)


def weight_terms_kernel(act_ref, dq_ref, kv_ref, small_ref, grad_out, term_out, grad_ref):
    rows = dq_ref.shape[0]

    @pl.when(pl.program_id(0) == 0)
    def _():
        total = kv_ref[0].astype(F32)
        for i in range(1, 4):
            total = total + kv_ref[i].astype(F32)
        grad = jnp.concatenate([dq_ref[...], total.astype(BF)], axis=1)
        grad_ref[...] = grad
        padded = jnp.concatenate([grad, jnp.zeros((rows, 64), BF)], axis=1)
        grad_out[...] = padded.reshape(grad_out.shape)

    term = dot(act_ref[...].T, grad_ref[...]).astype(BF)
    term = jnp.concatenate([term, small_ref[...]], axis=1)
    piece = term_out.shape[2]
    for y in range(4):
        term_out[y, 0] = term[y * piece : (y + 1) * piece]


def weight_terms(act, dq, kv, small):
    rows, width = act.shape
    shard = width // 4
    return pl.pallas_call(
        weight_terms_kernel,
        out_shape=(
            jax.ShapeDtypeStruct((8, rows // 8, 384), BF),
            jax.ShapeDtypeStruct((4, 4, shard // 4, 384), BF),
        ),
        grid=(4,),
        in_specs=[
            pl.BlockSpec((rows, shard), lambda w: (0, w)),
            pl.BlockSpec(dq.shape, lambda w: (0, 0)),
            pl.BlockSpec(kv.shape, lambda w: (0, 0, 0)),
            pl.BlockSpec((shard, 64), lambda w: (w, 0)),
        ],
        out_specs=(
            pl.BlockSpec((8, rows // 8, 384), lambda w: (0, 0, 0)),
            pl.BlockSpec((4, 1, shard // 4, 384), lambda w: (0, w, 0, 0)),
        ),
        scratch_shapes=[pltpu.VMEM((rows, HEAD_COLUMNS), BF)],
        compiler_params=pltpu.CompilerParams(vmem_limit_bytes=40 * 2**20),
        cost_estimate=pl.CostEstimate(flops=10**9, bytes_accessed=8 * 10**6, transcendentals=0),
        name="weight_terms",
    )(act, dq, kv, small)


def return_terms_kernel(grad_ref, term_ref, grad_to, term_to, v_grad, v_term, send, recv, local):
    place, stream = turned(lax.axis_index("ctx")), lax.axis_index("wsh")
    y, r = place // 8, place % 8
    peers = [((y + k // 4) % 4, (stream + k % 4) % 4) for k in range(1, 16)]
    in_row = [(r + k) % 8 for k in range(1, 8)]
    meet(
        [{"ctx": turned(r + 8 * py), "wsh": pw} for py, pw in peers] + [{"ctx": turned(8 * y + pr)} for pr in in_row]
    )
    copies = Copies(send, recv, local)
    for py, pw in peers:
        copies.to(term_ref.at[py, pw], term_to.at[y, stream], {"ctx": turned(r + 8 * py), "wsh": pw})
    for pr in in_row:
        copies.to(grad_ref.at[pr], grad_to.at[r], {"ctx": turned(8 * y + pr)})
    copies.keep(grad_ref.at[r], v_grad, grad_to.at[r])
    copies.keep(term_ref.at[y, stream], v_term, term_to.at[y, stream])
    copies.move_kept()
    copies.finish([])


def return_terms(grad, term):
    return pl.pallas_call(
        return_terms_kernel,
        out_shape=(jax.ShapeDtypeStruct(grad.shape, BF), jax.ShapeDtypeStruct(term.shape, BF)),
        in_specs=[ANY, ANY],
        out_specs=(ANY, ANY),
        scratch_shapes=[
            pltpu.VMEM(grad.shape[1:], BF),
            pltpu.VMEM(term.shape[2:], BF),
            pltpu.SemaphoreType.DMA((22,)),
            pltpu.SemaphoreType.DMA((22,)),
            pltpu.SemaphoreType.DMA((4,)),
        ],
        compiler_params=pltpu.CompilerParams(collective_id=4, has_side_effects=True, vmem_limit_bytes=40 * 2**20),
        name="return_terms",
    )(grad, term)


def gather_sums_kernel(term_ref, piece_ref, all_out, own_ref, send, recv, local):
    place = turned(lax.axis_index("ctx"))
    y, r = place // 8, place % 8
    x, z = r % 4, r // 4
    right, left = {"ctx": turned(place - x + (x + 1) % 4)}, {"ctx": turned(place - x + (x + 3) % 4)}
    across = {"ctx": turned(place + 4 - 8 * z)}
    up, down, beyond = ({"ctx": turned((place + 8 * k) % 32)} for k in (1, 3, 2))
    total = term_ref[0, 0].astype(F32)
    for i in range(1, 16):
        total = total + term_ref[i // 4, i % 4].astype(F32)
    own_ref[:, : total.shape[1]] = total.astype(BF)
    own_ref[:, total.shape[1] :] = piece_ref[...]
    meet([right, left, across, up, down, beyond])
    copies = Copies(send, recv, local)
    half = own_ref.shape[0] // 2
    first, last = pl.ds(0, half), pl.ds(half, half)
    r_z = (1 - z) * 4 + x
    r_left, r_right = z * 4 + (x + 3) % 4, z * 4 + (x + 1) % 4
    z_left, z_right = (1 - z) * 4 + (x + 3) % 4, (1 - z) * 4 + (x + 1) % 4
    arrived = []

    def arrive(*which):
        for copy in which:
            copy.wait_recv()
            arrived.append(copy)

    def on(device, *at):
        return copies.to(all_out.at[at], all_out.at[at], device)

    keep = pltpu.make_async_copy(own_ref, all_out.at[y, r], local.at[0])
    keep.start()
    a_right = copies.to(own_ref.at[first], all_out.at[y, r, first], right)
    a_left = copies.to(own_ref.at[first], all_out.at[y, r, first], left)
    a_cross = copies.to(own_ref.at[first], all_out.at[y, r, first], across)
    b_up = copies.to(own_ref.at[last], all_out.at[y, r, last], up)
    b_down = copies.to(own_ref.at[last], all_out.at[y, r, last], down)
    b_beyond = copies.to(own_ref.at[last], all_out.at[y, r, last], beyond)
    keep.wait()
    arrive(a_cross)
    a_z_right = on(right, y, r_z, first)
    a_z_left = on(left, y, r_z, first)
    arrive(a_right)
    a_on = on(right, y, r_left, first)
    arrive(b_up, b_down, b_beyond)
    lower, upper, every = pl.ds(0, 2), pl.ds(2, 2), pl.ds(0, 4)
    b_right = on(right, every, r, last)
    b_left = on(left, every, r, last)
    b_cross = on(across, every, r, last)
    arrive(a_z_left, a_left)
    a_z_on = on(left, y, z_right, first)
    arrive(a_z_right, a_on, a_z_on)
    low_r, high_r = pl.ds(0, 4), pl.ds(4, 4)
    c_up = [on(up, y, low_r, first), on(up, y, high_r, first)]
    c_down = [on(down, y, high_r, first), on(down, y, low_r, first)]
    arrive(b_right)
    on(right, lower, r_left, last)
    arrive(b_left)
    on(left, upper, r_right, last)
    arrive(b_cross)
    b_z_right = on(right, every, r_z, last)
    b_z_left = on(left, every, r_z, last)
    arrive(c_up[0])
    on(up, (y + 3) % 4, low_r, first)
    arrive(c_down[0])
    on(down, (y + 1) % 4, high_r, first)
    arrive(b_z_right)
    on(right, lower, z_left, last)
    arrive(b_z_left)
    on(left, upper, z_right, last)
    copies.finish(arrived)


def gather_sums(term, piece):
    rows, columns = piece.shape[0], term.shape[3] + piece.shape[1]
    vmem = pl.BlockSpec(memory_space=pltpu.VMEM)
    return pl.pallas_call(
        gather_sums_kernel,
        out_shape=jax.ShapeDtypeStruct((4, 8, rows, columns), BF),
        in_specs=[vmem, vmem],
        out_specs=ANY,
        scratch_shapes=[
            pltpu.VMEM((rows, columns), BF),
            pltpu.SemaphoreType.DMA((25,)),
            pltpu.SemaphoreType.DMA((25,)),
            pltpu.SemaphoreType.DMA((1,)),
        ],
        compiler_params=pltpu.CompilerParams(collective_id=5, has_side_effects=True, vmem_limit_bytes=40 * 2**20),
        name="gather_sums",
    )(term, piece)


def assemble_kernel(by_row_ref, by_head_ref, qkv_ref, out_ref, rest_ref):
    heads = [by_row_ref[0, h].astype(F32) for h in range(8)]
    ends = (0, WIDTH, WIDTH + HEAD_SIZE, HEAD_COLUMNS)
    qkv_ref[...] = jnp.concatenate([t[:, a:b] for a, b in zip(ends[:-1], ends[1:]) for t in heads], axis=1)
    tail = heads[0]
    for t in heads[1:]:
        tail = tail + t
    rest_ref[...] = tail[:, HEAD_COLUMNS:384]
    for parity in range(2):
        parts = [by_head_ref[parity, y, 0, :, 384:].astype(F32).T for y in range(4)]
        out_ref[parity * WIDTH : (parity + 1) * WIDTH, :] = jnp.concatenate(parts, axis=1)


def assemble(gathered):
    _, _, piece, columns = gathered.shape
    shard = 4 * piece
    return pl.pallas_call(
        assemble_kernel,
        out_shape=(
            jax.ShapeDtypeStruct((shard, 8 * HEAD_COLUMNS), F32),
            jax.ShapeDtypeStruct((2 * WIDTH, 4 * shard), F32),
            jax.ShapeDtypeStruct((shard, 64), F32),
        ),
        grid=(4,),
        in_specs=[
            pl.BlockSpec((1, 8, piece, columns), lambda i: (i, 0, 0, 0)),
            pl.BlockSpec((2, 4, 1, piece, columns), lambda i: (0, 0, i, 0, 0)),
        ],
        out_specs=(
            pl.BlockSpec((piece, 8 * HEAD_COLUMNS), lambda i: (i, 0)),
            pl.BlockSpec((2 * WIDTH, shard), lambda i: (0, i)),
            pl.BlockSpec((piece, 64), lambda i: (i, 0)),
        ),
        compiler_params=pltpu.CompilerParams(vmem_limit_bytes=40 * 2**20),
        name="assemble",
    )(gathered, gathered.reshape(2, 4, 4, piece, columns))


MESH = pl.DeviceIdType.MESH
ANY = pl.BlockSpec(memory_space=pl.ANY)


class Copies:
    def __init__(self, send, recv, local):
        self.send, self.recv, self.local = send, recv, local
        self.remote_count = self.local_count = 0
        self.started, self.kept = [], []

    def to(self, source, target, device):
        k = self.remote_count
        self.remote_count += 1
        copy = pltpu.make_async_remote_copy(
            source, target, self.send.at[k], self.recv.at[k], device_id=device, device_id_type=MESH
        )
        copy.start()
        self.started.append(copy)
        return copy

    def keep(self, source, middle, target):
        k = self.local_count
        self.local_count += 2
        first = pltpu.make_async_copy(source, middle, self.local.at[k])
        first.start()
        self.kept.append((first, pltpu.make_async_copy(middle, target, self.local.at[k + 1])))

    def move_kept(self):
        for first, second in self.kept:
            first.wait()
            second.start()

    def finish(self, arrived):
        for copy in self.started:
            copy.wait_send()
            if not any(copy is other for other in arrived):
                copy.wait_recv()
        for _, second in self.kept:
            second.wait()


def meet(devices):
    barrier = pltpu.get_barrier_semaphore()
    for device in devices:
        pl.semaphore_signal(barrier, inc=1, device_id=device, device_id_type=MESH)
    pl.semaphore_wait(barrier, len(devices))


def gather_rows_kernel(
    tok_ref, wp_ref, gain_ref, wo_ref, tok_out, wp_out, gain_out, wo_out, v_tok, v_wp, v_gain, v_wo, send, recv, local
):
    place, stream = turned(lax.axis_index("ctx")), lax.axis_index("wsh")
    x, z = place % 4, (place // 4) % 2
    right, left = {"ctx": turned(place - x + (x + 1) % 4)}, {"ctx": turned(place - x + (x + 3) % 4)}
    across = place + 4 - 8 * z
    other = {"wsh": stream + 1 - 2 * (stream % 2)}
    far = {"ctx": turned(across), "wsh": (stream + 2) % 4}
    meet([right, left, {"ctx": turned(across)}, other, far])
    copies = Copies(send, recv, local)
    half = tok_ref.shape[0] // 2
    own, own_z = z * 4 + x, (1 - z) * 4 + x
    left_id, right_id = z * 4 + (x + 3) % 4, z * 4 + (x + 1) % 4
    left_z, right_z = (1 - z) * 4 + (x + 3) % 4, (1 - z) * 4 + (x + 1) % 4

    def rows(ref, h):
        return ref.at[pl.ds(h * half, half)]

    def spot(block, h):
        return tok_out.at[block, pl.ds(h * half, half)]

    head = place % 8
    far_wp = copies.to(wp_ref.at[across % 8], wp_out.at[stream], far)
    far_gain = copies.to(gain_ref, gain_out.at[stream], far)
    cross = [copies.to(rows(tok_ref, h), spot(own, h), {"ctx": turned(across)}) for h in range(2)]
    to_right = [copies.to(rows(tok_ref, h), spot(own, h), right) for h in (0, 1)]
    to_left = [copies.to(rows(tok_ref, h), spot(own, h), left) for h in (1, 0)]
    copies.to(wp_ref.at[head], wp_out.at[stream], other)
    copies.to(gain_ref, gain_out.at[stream], other)
    third = wo_ref.shape[0] // 3
    parts = [pl.ds(i * third, third) for i in range(3)]
    far_wo = [copies.to(wo_ref.at[p], wo_out.at[stream, p], far) for p in parts]
    copies.to(wo_ref, wo_out.at[stream], other)
    copies.keep(tok_ref, v_tok, tok_out.at[own])
    copies.keep(wp_ref.at[head], v_wp, wp_out.at[stream])
    copies.keep(gain_ref, v_gain, gain_out.at[stream])
    copies.keep(wo_ref, v_wo, wo_out.at[stream])
    copies.move_kept()

    arrived = []

    def arrive(copy):
        copy.wait_recv()
        arrived.append(copy)

    far_stream = (stream + 2) % 4
    arrive(far_wp)
    copies.to(wp_out.at[far_stream], wp_out.at[far_stream], other)
    arrive(far_gain)
    copies.to(gain_out.at[far_stream], gain_out.at[far_stream], other)
    arrive(to_right[0])
    copies.to(spot(left_id, 0), spot(left_id, 0), right)
    arrive(to_left[0])
    copies.to(spot(right_id, 1), spot(right_id, 1), left)
    arrive(cross[0])
    arrive(cross[1])
    z_right = [copies.to(spot(own_z, h), spot(own_z, h), right) for h in (0, 1)]
    z_left = [copies.to(spot(own_z, h), spot(own_z, h), left) for h in (1, 0)]
    arrive(z_right[0])
    copies.to(spot(left_z, 0), spot(left_z, 0), right)
    arrive(z_left[0])
    copies.to(spot(right_z, 1), spot(right_z, 1), left)
    for p, copy in zip(parts, far_wo):
        arrive(copy)
        copies.to(wo_out.at[far_stream, p], wo_out.at[far_stream, p], other)
    copies.finish(arrived)


def gather_rows(tok, wp, gain, wo):
    return pl.pallas_call(
        gather_rows_kernel,
        out_shape=(
            jax.ShapeDtypeStruct((8,) + tok.shape, BF),
            jax.ShapeDtypeStruct((4,) + wp.shape[1:], BF),
            jax.ShapeDtypeStruct((4,) + gain.shape, BF),
            jax.ShapeDtypeStruct((4,) + wo.shape, BF),
        ),
        in_specs=[ANY] * 4,
        out_specs=(ANY,) * 4,
        scratch_shapes=[
            pltpu.VMEM(tok.shape, BF),
            pltpu.VMEM(wp.shape[1:], BF),
            pltpu.VMEM(gain.shape, BF),
            pltpu.VMEM(wo.shape, BF),
            pltpu.SemaphoreType.DMA((27,)),
            pltpu.SemaphoreType.DMA((27,)),
            pltpu.SemaphoreType.DMA((8,)),
        ],
        compiler_params=pltpu.CompilerParams(collective_id=1, has_side_effects=True, vmem_limit_bytes=40 * 2**20),
        name="gather_rows",
    )(tok, wp, gain, wo)


def gather_keys_kernel(kv_ref, kv_out, v_kv, send, recv, local):
    place = turned(lax.axis_index("ctx"))
    y = place // 8
    up, down = {"ctx": turned((place + 8) % 32)}, {"ctx": turned((place + 24) % 32)}
    meet([up, down])
    copies = Copies(send, recv, local)
    half = kv_ref.shape[0] // 2

    def rows(h):
        return kv_ref.at[pl.ds(h * half, half)]

    def spot(block, h):
        return kv_out.at[block, pl.ds(h * half, half)]

    to_up = [copies.to(rows(h), spot(y, h), up) for h in (0, 1)]
    to_down = [copies.to(rows(h), spot(y, h), down) for h in (1, 0)]
    copies.keep(kv_ref, v_kv, kv_out.at[y])
    copies.move_kept()
    to_up[0].wait_recv()
    copies.to(spot((y + 3) % 4, 0), spot((y + 3) % 4, 0), up)
    to_down[0].wait_recv()
    copies.to(spot((y + 1) % 4, 1), spot((y + 1) % 4, 1), down)
    copies.finish([to_up[0], to_down[0]])


def gather_keys(kv):
    return pl.pallas_call(
        gather_keys_kernel,
        out_shape=jax.ShapeDtypeStruct((4,) + kv.shape, BF),
        in_specs=[ANY],
        out_specs=ANY,
        scratch_shapes=[
            pltpu.VMEM(kv.shape, BF),
            pltpu.SemaphoreType.DMA((6,)),
            pltpu.SemaphoreType.DMA((6,)),
            pltpu.SemaphoreType.DMA((2,)),
        ],
        compiler_params=pltpu.CompilerParams(collective_id=2, has_side_effects=True, vmem_limit_bytes=40 * 2**20),
        name="gather_keys",
    )(kv)


FF_STEP = 256


def experts_kernel(
    rows_ref, grads_ref, w_ref, back_out, returned_out, terms_out,
    w_v, x_v, g_v, turned_x, turned_g, out_v, d_in_v, acc_v, gate_v, up_v, hidden_v, d_gate_v, d_up_v, sent_v, got_v,
    send, recv, local,
):
    index, stream = lax.axis_index("ctx"), lax.axis_index("wsh")
    x, mine = index % 4, index // 2
    inner = (x + 1) // 2 % 2

    def device(p):
        return {"ctx": p // 2 * 4 + (1 - inner) * (3 * (p % 2)) + inner * (1 + p % 2)}

    peers = [(mine + k) % 16 for k in range(1, 16)]
    core = stream % 2
    other = {"wsh": stream + 1 - 2 * core}
    meet([device(p) for p in peers] + [other])
    copies = Copies(send, recv, local)
    width, rows = turned_x.shape
    quarter = width // 4
    own = []

    def here(source, target):
        copy = pltpu.make_async_copy(source, target, local.at[len(own)])
        copy.start()
        own.append(copy)
        return copy

    came = [copies.to(rows_ref.at[p], x_v.at[mine], device(p)) for p in peers]
    own_x = here(rows_ref.at[mine], x_v.at[mine])
    weights = [
        here(w_ref.at[4 * k + q, m], w_v.at[k, m, pl.ds(q * quarter, quarter)])
        for k in range(2)
        for q in range(4)
        for m in range(3)
    ]
    came_g = [copies.to(grads_ref.at[p], g_v.at[mine], device(p)) for p in peers]
    own_g = here(grads_ref.at[mine], g_v.at[mine])
    arrived = []

    def arrive(several):
        for copy in several:
            copy.wait_recv()
            arrived.append(copy)

    for copy in weights:
        copy.wait()
    arrive(came)
    own_x.wait()
    steps = w_v.shape[3] // FF_STEP
    acc_v[...] = jnp.zeros_like(acc_v)

    def forward(i, carry):
        k, at = i // steps, pl.ds(pl.multiple_of(i % steps * FF_STEP, FF_STEP), FF_STEP)
        inputs = x_v[...].reshape(rows, width)
        gate = dot(inputs, w_v[k, 0, :, at])
        up = dot(inputs, w_v[k, 1, :, at])
        hidden = (gate * jax.nn.sigmoid(gate) * up).astype(BF)
        gate_v[i] = gate
        up_v[i] = up
        hidden_v[k, :, at] = hidden
        acc_v[...] += dot(hidden, w_v[k, 2, :, at], NT)
        return carry

    lax.fori_loop(0, 2 * steps, forward, 0)
    out_v[...] = acc_v[...].astype(BF).reshape(out_v.shape)
    for p in peers:
        copies.to(out_v.at[p], back_out.at[mine], device(p))
    own_back = here(out_v.at[mine], back_out.at[mine])
    for q in range(4):
        at = slice(q * quarter, (q + 1) * quarter)
        turned_x[at, :] = x_v[:, :, at].reshape(rows, quarter).T
    acc_v[...] = jnp.zeros_like(acc_v)
    arrive(came_g)
    own_g.wait()

    def backward(i, carry):
        k, at = i // steps, pl.ds(pl.multiple_of(i % steps * FF_STEP, FF_STEP), FF_STEP)
        d_hidden = dot(g_v[...].reshape(rows, width), w_v[k, 2, :, at])
        gate, up = gate_v[i], up_v[i]
        sigmoid = jax.nn.sigmoid(gate)
        d_gate = (d_hidden * up * sigmoid * (1.0 + gate * (1.0 - sigmoid))).astype(BF)
        d_up = (d_hidden * (gate * sigmoid)).astype(BF)
        d_gate_v[k, :, at] = d_gate
        d_up_v[k, :, at] = d_up
        acc_v[...] += dot(d_gate, w_v[k, 0, :, at], NT) + dot(d_up, w_v[k, 1, :, at], NT)
        return carry

    lax.fori_loop(0, 2 * steps, backward, 0)
    d_in_v[...] = acc_v[...].astype(BF).reshape(d_in_v.shape)
    for p in peers:
        copies.to(d_in_v.at[p], returned_out.at[mine], device(p))
    own_returned = here(d_in_v.at[mine], returned_out.at[mine])
    for q in range(4):
        at = slice(q * quarter, (q + 1) * quarter)
        turned_g[at, :] = g_v[:, :, at].reshape(rows, quarter).T

    def terms(k, z, c):
        at = pl.ds(pl.multiple_of((2 * z + c) * quarter, quarter), quarter)
        part = turned_x[at, :]
        return (
            dot(part, d_gate_v[k]),
            dot(part, d_up_v[k]),
            dot(turned_g[at, :], hidden_v[k]),
        )

    crossing = []
    for z in range(2):

        def other_term(k, carry, z=z):
            for m, term in enumerate(terms(k, z, 1 - core)):
                sent_v[z, k, m] = term.astype(BF)
            return carry

        lax.fori_loop(0, 2, other_term, 0)
        crossing.append(copies.to(sent_v.at[z], got_v.at[z], other))
    for z in range(2):

        def own_term(k, carry, z=z):
            for m, term in enumerate(terms(k, z, core)):
                terms_out[z, k, m] = (term + got_v[z, k, m].astype(F32)).astype(BF)
            return carry

        arrive([crossing[z]])
        lax.fori_loop(0, 2, own_term, 0)
    copies.finish(arrived)
    own_back.wait()
    own_returned.wait()


def experts(send_rows, send_grads, weights):
    groups, capacity, width = send_rows.shape
    rows = groups * capacity
    half = weights.shape[3]
    vmem = pltpu.VMEM
    steps = 2 * half // FF_STEP
    slots = vmem(send_rows.shape, BF)
    terms = (2, 2, 3, width // 4, half)
    return pl.pallas_call(
        experts_kernel,
        out_shape=(
            jax.ShapeDtypeStruct(send_rows.shape, BF),
            jax.ShapeDtypeStruct(send_rows.shape, BF),
            jax.ShapeDtypeStruct(terms, BF),
        ),
        in_specs=[ANY, ANY, ANY],
        out_specs=(ANY, ANY, pl.BlockSpec(memory_space=pltpu.VMEM)),
        scratch_shapes=[
            vmem((2, 3, width, half), BF),
            slots,
            slots,
            vmem((width, rows), BF),
            vmem((width, rows), BF),
            slots,
            slots,
            vmem((rows, width), F32),
            vmem((steps, rows, FF_STEP), F32),
            vmem((steps, rows, FF_STEP), F32),
            vmem((2, rows, half), BF),
            vmem((2, rows, half), BF),
            vmem((2, rows, half), BF),
            vmem(terms, BF),
            vmem(terms, BF),
            pltpu.SemaphoreType.DMA((62,)),
            pltpu.SemaphoreType.DMA((62,)),
            pltpu.SemaphoreType.DMA((28,)),
        ],
        compiler_params=pltpu.CompilerParams(collective_id=6, has_side_effects=True, vmem_limit_bytes=56 * 2**20),
        cost_estimate=pl.CostEstimate(flops=15 * 10**9, bytes_accessed=10**8, transcendentals=10**6),
        name="experts",
    )(send_rows, send_grads, weights)


def prepare_kernel(qkv_ref, router_ref, wo_ref, wp_out, wo_out):
    rows = qkv_ref.shape[0]
    experts = router_ref.shape[1]
    wo_out[...] = wo_ref[...].astype(BF)
    router = router_ref[...].astype(BF)
    tail = jnp.zeros((rows, wp_out.shape[2] - HEAD_COLUMNS - experts), BF)
    k_at, v_at = QUERY_HEADS * HEAD_SIZE, (QUERY_HEADS + KEY_VALUE_HEADS) * HEAD_SIZE
    for h in range(KEY_VALUE_HEADS):
        wp_out[h] = jnp.concatenate(
            [
                qkv_ref[:, h * WIDTH : (h + 1) * WIDTH].astype(BF),
                qkv_ref[:, k_at + h * HEAD_SIZE : k_at + (h + 1) * HEAD_SIZE].astype(BF),
                qkv_ref[:, v_at + h * HEAD_SIZE : v_at + (h + 1) * HEAD_SIZE].astype(BF),
                router,
                tail,
            ],
            axis=1,
        )


def prepare(w_qkv, w_router, w_out):
    shard = w_qkv.shape[0]
    step = shard // 3

    def block(n):
        return pl.BlockSpec((step, n), lambda i: (i, 0))

    return pl.pallas_call(
        prepare_kernel,
        out_shape=(
            jax.ShapeDtypeStruct((KEY_VALUE_HEADS, shard, 384), BF),
            jax.ShapeDtypeStruct(w_out.shape, BF),
        ),
        grid=(3,),
        in_specs=[block(w_qkv.shape[1]), block(w_router.shape[1]), block(w_out.shape[1])],
        out_specs=(
            pl.BlockSpec((KEY_VALUE_HEADS, step, 384), lambda i: (0, i, 0)),
            block(w_out.shape[1]),
        ),
        compiler_params=pltpu.CompilerParams(vmem_limit_bytes=40 * 2**20),
        name="prepare",
    )(w_qkv, w_router, w_out)


def input_gradient_kernel(stream_ref, d_qkv_ref, p0, p1, p2, p3, x_ref, d_mid_ref, gain_ref, out_ref, acc_ref):
    step = pl.program_id(0)
    stream = stream_ref[0]

    @pl.when(step == 0)
    def _():
        acc_ref[...] = jnp.zeros_like(acc_ref)

    grad = d_qkv_ref[0, :, :HEAD_COLUMNS]
    for j, piece in enumerate((p0, p1, p2, p3)):
        acc_ref[stream ^ j] += dot(grad, piece[0, :, :HEAD_COLUMNS], NT)

    @pl.when(step == pl.num_programs(0) - 1)
    def _():
        x = x_ref[...].astype(F32)
        scale = rms_scale(x)
        quarter = acc_ref.shape[2]
        inner = 0.0
        for q in range(4):
            at = slice(q * quarter, (q + 1) * quarter)
            inner += jnp.sum(acc_ref[q] * gain_ref[:, at] * x[:, at], axis=-1, keepdims=True)
        inner = inner * (1.0 / x.shape[1])
        for q in range(4):
            at = slice(q * quarter, (q + 1) * quarter)
            out_ref[:, at] = (
                d_mid_ref[:, at] + scale * (acc_ref[q] * gain_ref[:, at]) - x[:, at] * scale**3 * inner
            ).astype(BF)


def input_gradient(stream, d_qkv, pieces, x, d_middle, gain):
    heads, rows, _ = d_qkv.shape
    width = x.shape[1]

    def whole(a):
        return pl.BlockSpec(a.shape, lambda h, s: (0, 0))

    def by_head(a):
        return pl.BlockSpec((1,) + a.shape[1:], lambda h, s: (h, 0, 0))

    gain = gain.reshape(1, width)
    return pl.pallas_call(
        input_gradient_kernel,
        out_shape=jax.ShapeDtypeStruct(x.shape, BF),
        grid_spec=pltpu.PrefetchScalarGridSpec(
            num_scalar_prefetch=1,
            grid=(heads,),
            in_specs=[by_head(d_qkv)] + [by_head(p) for p in pieces] + [whole(x), whole(d_middle), whole(gain)],
            out_specs=whole(x),
            scratch_shapes=[pltpu.VMEM((4, rows, width // 4), F32)],
        ),
        compiler_params=pltpu.CompilerParams(vmem_limit_bytes=40 * 2**20),
        cost_estimate=pl.CostEstimate(flops=10**9, bytes_accessed=12 * 10**6, transcendentals=0),
        name="input_gradient",
    )(stream.reshape(1).astype(jnp.int32), d_qkv, *pieces, x, d_middle, gain)


def swap(x, groups, axis="ctx"):
    return lax.all_to_all(x, axis, 0, 0, axis_index_groups=groups, tiled=True)


def rms_scale(values):
    return lax.rsqrt(jnp.mean(values * values, axis=-1, keepdims=True) + EPSILON)


def body(
    tokens,
    lengths,
    deal,
    expert_ids,
    gain_attn,
    w_qkv,
    w_out,
    gain_moe,
    w_router,
    w_gate,
    w_up,
    w_down,
    cotangent,
):
    stream = lax.axis_index("wsh")
    index = lax.axis_index("ctx")
    place = turned(index)
    rows, width = tokens.shape[1], tokens.shape[2]
    shard = w_qkv.shape[0]
    experts_count = w_router.shape[1]
    capacity = 2 * rows * TOP // experts_count
    head = place % 8
    head_row = place // 8
    lengths_row = lax.dynamic_index_in_dim(lengths, stream, 0, keepdims=False)
    deal_row = lax.dynamic_index_in_dim(deal, stream, 0, keepdims=False)
    blocks = deal_row.shape[0]
    deal_row = deal_row.reshape(4, 2, 4, 2).transpose(2, 1, 0, 3).reshape(blocks)
    block_ids = jnp.arange(blocks, dtype=jnp.int32)
    inverse = jnp.sum(jnp.where(deal_row[None, :] == block_ids[:, None], block_ids[None, :], 0), axis=1)
    own_blocks = lax.dynamic_slice_in_dim(deal_row, head_row * 16, 16)
    meta = jnp.concatenate([inverse, own_blocks, jnp.cumsum(lengths_row)]).astype(jnp.int32)

    q_columns = QUERY_HEADS * HEAD_SIZE
    by_head, own_out = prepare(w_qkv, w_router, w_out)
    own_gains = jnp.concatenate(
        [gain_attn.astype(BF)[None], gain_moe.astype(BF)[None], jnp.zeros((14, shard), BF)], axis=0
    )
    group_tokens, head_full, gains, full_out = gather_rows(tokens[0], by_head, own_gains, own_out)
    head_full = head_full.reshape(width, -1)
    head_weight = head_full[:, :HEAD_COLUMNS]
    full_router = head_full[:, HEAD_COLUMNS : HEAD_COLUMNS + experts_count]
    gain_first = gains[:, 0].reshape(width).astype(F32)
    gain_second = gains[:, 1].reshape(width).astype(F32)
    full_out = full_out.reshape(q_columns, width)

    w_gate, w_up, w_down, _ = lax.optimization_barrier((w_gate, w_up, w_down, gains))
    expert_shard = jnp.stack([w_gate[0].astype(BF), w_up[0].astype(BF), w_down[0].T.astype(BF)])
    expert_all = lax.all_gather(expert_shard, ("ctx", "wsh"), axis_index_groups=OWNERS)
    far_qkv = lax.ppermute(by_head, ("ctx", "wsh"), NEXT_Z)
    qkv_pieces = [
        by_head,
        lax.ppermute(by_head, "wsh", OTHER_CORE),
        far_qkv,
        lax.ppermute(far_qkv, "wsh", OTHER_CORE),
    ]

    group_x = group_tokens.reshape(8 * rows, width).astype(F32)
    group_act = (group_x * rms_scale(group_x) * gain_first).astype(BF)
    head_qkv = dot(group_act, head_weight).astype(BF)
    kv_all = gather_keys(head_qkv[:, WIDTH:]).reshape(32 * rows, 2 * HEAD_SIZE)
    head_q = head_qkv[:, :WIDTH]
    head_attn, lse = run_forward(meta, head_q, kv_all)
    attn_low = swap(head_attn.reshape(8, rows, WIDTH), ROW).transpose(1, 0, 2).reshape(rows, q_columns)

    x_first = tokens[0].astype(F32)
    middle = x_first + dot(attn_low, full_out)
    scale_second = rms_scale(middle)
    act_moe = (middle * scale_second * gain_second).astype(BF)
    logits = dot(act_moe, full_router)
    choice = expert_ids[0]
    expert_range = jnp.arange(experts_count, dtype=jnp.int32)
    picked_hot = choice[:, :, None] == expert_range[None, None, :]
    picked = jnp.sum(jnp.where(picked_hot, logits[:, None, :], 0.0), axis=-1)
    picked_exp = jnp.exp(picked - jnp.max(picked, axis=-1, keepdims=True))
    gates = picked_exp / jnp.sum(picked_exp, axis=-1, keepdims=True)
    flat_ids = choice.reshape(-1)
    assign_hot = (flat_ids[:, None] == expert_range[None, :]).astype(jnp.int32)
    ranks = jnp.sum((jnp.cumsum(assign_hot, axis=0) - 1) * assign_hot, axis=1)
    slots = (flat_ids * capacity + ranks).reshape(rows, TOP)
    slot_range = jnp.arange(experts_count * capacity, dtype=jnp.int32)
    hot = [slots[:, j][:, None] == slot_range[None, :] for j in range(TOP)]
    hot_low = [h.astype(BF) for h in hot]
    hot_any = hot_low[0] + hot_low[1]
    slot_gate = sum(jnp.sum(jnp.where(hot[j], gates[:, j][:, None], 0.0), axis=0) for j in range(TOP))

    send_rows = dot(hot_any, act_moe, TN).astype(BF).reshape(experts_count, capacity, width)
    send_grads = (slot_gate[:, None] * dot(hot_any, cotangent[0], TN)).astype(BF)
    back_rows, returned, expert_terms = experts(send_rows, send_grads.reshape(experts_count, capacity, width), expert_all)
    back_rows, returned = (r.reshape(-1, width) for r in (back_rows, returned))

    both = [dot(hot_low[j], back_rows) for j in range(TOP)]
    output_rows = (middle + gates[:, :1] * both[0] + gates[:, 1:] * both[1]).astype(BF)
    d_out = cotangent[0].astype(F32)
    d_gates = jnp.stack([jnp.sum(d_out * both[j], axis=-1) for j in range(TOP)], axis=1)
    d_picked = gates * (d_gates - jnp.sum(gates * d_gates, axis=-1, keepdims=True))
    d_logits = jnp.sum(jnp.where(picked_hot, d_picked[:, :, None], 0.0), axis=1).astype(BF)
    d_act_moe = dot(hot_any, returned) + dot(d_logits, full_router, NT)
    d_router_local = dot(act_moe, d_logits, TN)
    d_gain_second = jnp.sum(d_act_moe * middle * scale_second, axis=0)
    scaled = d_act_moe * gain_second
    d_middle = (
        d_out
        + scale_second * scaled
        - middle * scale_second**3 * jnp.mean(scaled * middle, axis=-1, keepdims=True)
    )
    d_branch = d_middle.astype(BF)

    d_attn = dot(d_branch, full_out, NT).astype(BF)
    head_d_attn = swap(d_attn.reshape(rows, 8, WIDTH).transpose(1, 0, 2), ROW).reshape(8 * rows, WIDTH)
    group_branch = lax.all_gather(d_branch, "ctx", axis_index_groups=ROW).reshape(8 * rows, width)
    head_d_attn, expert_terms, qkv_pieces = lax.optimization_barrier((head_d_attn, expert_terms, qkv_pieces))
    side = stream // 2
    recv_terms = lax.ppermute(
        lax.dynamic_index_in_dim(expert_terms, 1 - side, 0, keepdims=False), "wsh", OTHER_SIDE
    )
    keep_terms = lax.dynamic_index_in_dim(expert_terms, side, 0, keepdims=False)
    pending_terms = (keep_terms, recv_terms)
    d_q, d_kv = run_backward(meta, head_q, kv_all, head_attn, lse, head_d_attn)
    out_term = dot(group_branch, head_attn, TN).astype(BF).reshape(4, 4, shard // 4, WIDTH).transpose(1, 0, 2, 3)
    small_term = jnp.concatenate(
        [d_router_local.astype(BF), d_gain_second.astype(BF)[:, None], jnp.zeros((width, 47), BF)], axis=1
    )
    kv_terms, out_terms = exchange_terms(d_kv.reshape(4, 8 * rows, 2 * HEAD_SIZE), out_term)
    (keep_terms, recv_terms), kv_terms = lax.optimization_barrier((pending_terms, kv_terms))
    expert_terms = (keep_terms.astype(F32) + recv_terms.astype(F32)).astype(BF)
    half = index % 2
    keep_terms = lax.dynamic_index_in_dim(expert_terms, half, 0, keepdims=False)
    recv_terms = lax.ppermute(
        lax.dynamic_index_in_dim(expert_terms, 1 - half, 0, keepdims=False), "ctx", OTHER_HALF
    )
    out_piece = lax.ppermute(
        jnp.sum(out_terms.astype(F32), axis=(0, 1)).astype(BF), ("ctx", "wsh"), MOVES
    )
    head_d_qkv, term = weight_terms(group_act, d_q, kv_terms, small_term)
    d_qkv, terms = return_terms(head_d_qkv, term)
    d_tokens = input_gradient(stream, d_qkv, qkv_pieces, tokens[0], d_middle, gain_first)
    terms, recv_terms = lax.optimization_barrier((terms, recv_terms))
    expert_own = keep_terms.astype(F32) + recv_terms.astype(F32)
    d_w_qkv, d_w_out, rest = assemble(gather_sums(terms, out_piece))
    d_gain_first = jnp.sum(d_w_qkv * w_qkv.astype(BF).astype(F32), axis=1) / gain_attn.astype(BF).astype(F32)
    return (
        output_rows[None],
        d_tokens[None],
        d_gain_first,
        d_w_qkv,
        d_w_out,
        rest[:, experts_count],
        rest[:, :experts_count],
        expert_own[0][None],
        expert_own[1][None],
        expert_own[2].T[None],
    )


def solution(mesh):
    placed = (
        P("wsh", "ctx", None),
        P(),
        P(),
        P("wsh", "ctx", None),
        P("wsh"),
        P("wsh", None),
        P("wsh", None),
        P("wsh"),
        P("wsh", None),
        P("ctx", "wsh", None),
        P("ctx", "wsh", None),
        P("ctx", None, "wsh"),
        P("wsh", "ctx", None),
    )
    return jax.shard_map(
        body,
        mesh=mesh,
        in_specs=placed,
        out_specs=(
            P("wsh", "ctx", None),
            P("wsh", "ctx", None),
            P("wsh"),
            P("wsh", None),
            P("wsh", None),
            P("wsh"),
            P("wsh", None),
            P("ctx", "wsh", None),
            P("ctx", "wsh", None),
            P("ctx", None, "wsh"),
        ),
        check_vma=False,
    )
```

```python
import functools

import jax
import jax.numpy as jnp
from jax import lax
from jax.experimental import pallas as pl
from jax.experimental.pallas import tpu as pltpu
from jax.sharding import PartitionSpec as P

QUERY_HEADS = 24
KEY_VALUE_HEADS = 8
HEAD_SIZE = 64
GROUP = QUERY_HEADS // KEY_VALUE_HEADS
TOP = 2
BLOCK = 64
WIDTH = GROUP * HEAD_SIZE
HEAD_COLUMNS = WIDTH + 2 * HEAD_SIZE
CHUNK = 512
LANES = 3
TURN = 256

EPSILON = 1e-05
NEG_BIG = -1e30
BF = jnp.bfloat16
F32 = jnp.float32

def turned(index):
    return index % 4 * 8 + index // 4 % 2 * 4 + index // 8


ROW = [[turned(y * 8 + r) for r in range(8)] for y in range(4)]
OWNERS = [[(2 * e + k) * 4 + w for k in range(2) for w in range(4)] for e in range(16)]
OTHER_HALF = [(c, c ^ 1) for c in range(32)]
OTHER_SIDE = [(w, w ^ 2) for w in range(4)]
OTHER_CORE = [(w, w ^ 1) for w in range(4)]
NEXT_Z = [(c * 4 + w, (c ^ 4) * 4 + (w ^ 2)) for c in range(32) for w in range(4)]

def dot(a, b, dims=((1,), (0,))):
    return lax.dot_general(a, b, (dims, ((), ())), preferred_element_type=F32)


NT = ((1,), (1,))
TN = ((0,), (0,))


def block_range(meta, b):
    base = meta[BLOCK + b] * BLOCK
    lane = lax.broadcasted_iota(jnp.int32, (1, WIDTH), 1)
    query = base + (lane & (BLOCK - 1))
    start = jnp.zeros((1, WIDTH), jnp.int32)
    first = jnp.int32(0)
    for i in range(3):
        bound = meta[80 + i]
        start = jnp.where(query >= bound, bound, start)
        first = jnp.where(base >= bound, bound, first)
    first = (first // 128) * 128
    count = (base + BLOCK - first + CHUNK - 1) // CHUNK
    return query, start, first, count


def list_work(meta, blocks, block_s, key_s):
    def one(b, n):
        _, _, first, count = block_range(meta, b)

        def put(i, n):
            block_s[n] = b
            key_s[n] = first + i * CHUNK
            return n + 1

        return lax.fori_loop(0, count, put, n)

    total = lax.fori_loop(0, blocks, one, jnp.int32(0))
    for i in range(LANES):
        block_s[total + i] = blocks
        key_s[total + i] = 0
    return (total + LANES - 1) // LANES


def allowed_of(key_start, query, start):
    key = key_start + lax.broadcasted_iota(jnp.int32, (CHUNK, WIDTH), 0)
    return (key <= query) & (key >= start)


def stack_heads(rows):
    return jnp.concatenate([rows[:, g * HEAD_SIZE : (g + 1) * HEAD_SIZE] for g in range(GROUP)], axis=0)


def sort_blocks(meta, kv_ref, sorted_ref):
    total = kv_ref.shape[0]

    def one(p, carry):
        source = pl.multiple_of(meta[p] * BLOCK, BLOCK)
        target = pl.multiple_of(p * BLOCK, BLOCK)
        sorted_ref[pl.ds(target, BLOCK), :] = kv_ref[pl.ds(source, BLOCK), :]
        return carry

    lax.fori_loop(0, total // BLOCK, one, 0, unroll=8)
    sorted_ref[total:, :] = jnp.zeros((CHUNK, sorted_ref.shape[1]), sorted_ref.dtype)


def transpose_all(sorted_ref, turned_ref):
    steps = sorted_ref.shape[0] // TURN

    def one(i, carry):
        at = pl.multiple_of(i * TURN, TURN)
        turned_ref[:, pl.ds(at, TURN)] = sorted_ref[pl.ds(at, TURN), :].T
        return carry

    lax.fori_loop(0, steps, one, 0)


def attention_forward(
    meta, q_ref, kv_ref, o_ref, lse_ref,
    sorted_ref, turned_ref, pad_ref, query_ref, start_ref, top_ref, total_ref, acc_ref, block_s, key_s,
):
    blocks = q_ref.shape[0] // BLOCK
    sort_blocks(meta, kv_ref, sorted_ref)
    transpose_all(sorted_ref, turned_ref)
    share = list_work(meta, blocks, block_s, key_s)
    zeros = jnp.zeros((WIDTH, HEAD_SIZE), BF)
    top_ref[...] = jnp.full(top_ref.shape, NEG_BIG, F32)
    total_ref[...] = jnp.zeros_like(total_ref)
    acc_ref[...] = jnp.zeros_like(acc_ref)
    query_ref[blocks] = jnp.full((1, WIDTH), -1, jnp.int32)
    start_ref[blocks] = jnp.zeros((1, WIDTH), jnp.int32)
    pad_ref[blocks] = jnp.zeros((WIDTH, 2 * HEAD_SIZE), BF)

    def prepare_block(b, carry):
        query_ref[b], start_ref[b], _, _ = block_range(meta, b)
        at = pl.multiple_of(b * BLOCK, BLOCK)
        rows = stack_heads(q_ref[pl.ds(at, BLOCK), :]) * jnp.asarray(HEAD_SIZE**-0.5, BF)
        pad_ref[b] = jnp.concatenate([rows, zeros], axis=1)
        return carry

    lax.fori_loop(0, blocks, prepare_block, 0, unroll=4)

    def work(i, carry):
        blocks_now = [block_s[lane * share + i] for lane in range(LANES)]
        starts_now = [pl.multiple_of(key_s[lane * share + i], 128) for lane in range(LANES)]
        results = []
        for b, key_start in zip(blocks_now, starts_now):
            scores = dot(sorted_ref[pl.ds(key_start, CHUNK), :], pad_ref[b], NT)
            scores = jnp.where(allowed_of(key_start, query_ref[b], start_ref[b]), scores, NEG_BIG)
            top = top_ref[b]
            top_new = jnp.maximum(top, jnp.max(scores, axis=0, keepdims=True))
            weights = jnp.exp(scores - top_new)
            fade = jnp.exp(top - top_new)
            total = total_ref[b] * fade + jnp.sum(weights, axis=0, keepdims=True)
            values = turned_ref[HEAD_SIZE:, pl.ds(key_start, CHUNK)]
            results.append((top_new, total, acc_ref[b] * fade + dot(values, weights.astype(BF))))
        for b, (top, total, acc) in zip(blocks_now, results):
            top_ref[b] = top
            total_ref[b] = total
            acc_ref[b] = acc
        return carry

    lax.fori_loop(0, share, work, 0)

    def finish_block(b, carry):
        at = pl.multiple_of(b * BLOCK, BLOCK)
        total = total_ref[b]
        lse_ref[b] = top_ref[b] + jnp.log(total)
        result = (acc_ref[b] / total).T.astype(BF)
        o_ref[pl.ds(at, BLOCK), :] = jnp.concatenate(
            [result[g * BLOCK : (g + 1) * BLOCK] for g in range(GROUP)], axis=1
        )
        return carry

    lax.fori_loop(0, blocks, finish_block, 0, unroll=4)


def attention_backward(
    meta, q_ref, kv_ref, o_ref, lse_ref, do_ref, dq_ref, dkv_ref,
    sorted_ref, turned_ref, total_ref, both_ref, query_ref, start_ref, delta_ref, acc_ref, block_s, key_s,
):
    blocks = q_ref.shape[0] // BLOCK
    sort_blocks(meta, kv_ref, sorted_ref)
    transpose_all(sorted_ref, turned_ref)
    share = list_work(meta, blocks, block_s, key_s)
    total_ref[...] = jnp.zeros_like(total_ref)
    acc_ref[...] = jnp.zeros_like(acc_ref)
    query_ref[blocks] = jnp.full((1, WIDTH), -1, jnp.int32)
    start_ref[blocks] = jnp.zeros((1, WIDTH), jnp.int32)
    delta_ref[blocks] = jnp.zeros((1, WIDTH), F32)
    both_ref[blocks] = jnp.zeros((2 * WIDTH, 2 * HEAD_SIZE), BF)
    zeros = jnp.zeros((WIDTH, HEAD_SIZE), BF)
    scaling = HEAD_SIZE**-0.5

    def prepare_block(b, carry):
        query_ref[b], start_ref[b], _, _ = block_range(meta, b)
        at = pl.multiple_of(b * BLOCK, BLOCK)
        rows = stack_heads(q_ref[pl.ds(at, BLOCK), :]) * jnp.asarray(scaling, BF)
        grad = stack_heads(do_ref[pl.ds(at, BLOCK), :])
        value = stack_heads(o_ref[pl.ds(at, BLOCK), :])
        delta_ref[b] = jnp.sum((grad.astype(F32) * value.astype(F32)).T, axis=0, keepdims=True)
        both_ref[b, :WIDTH] = jnp.concatenate([rows, zeros], axis=1)
        both_ref[b, WIDTH:] = jnp.concatenate([zeros, grad], axis=1)
        return carry

    lax.fori_loop(0, blocks, prepare_block, 0, unroll=4)

    def work(i, carry):
        blocks_now = [block_s[lane * share + i] for lane in range(LANES)]
        starts_now = [pl.multiple_of(key_s[lane * share + i], 128) for lane in range(LANES)]
        results = []
        for b, key_start in zip(blocks_now, starts_now):
            keys = sorted_ref[pl.ds(key_start, CHUNK), :]
            scores = dot(keys, both_ref[b, :WIDTH], NT)
            d_probs = dot(keys, both_ref[b, WIDTH:], NT)
            allowed = allowed_of(key_start, query_ref[b], start_ref[b])
            probs = jnp.where(allowed, jnp.exp(scores - lse_ref[b]), 0.0)
            d_scores = (probs * (d_probs - delta_ref[b])).astype(BF)
            joined = jnp.concatenate([d_scores, probs.astype(BF)], axis=1)
            turned = turned_ref[:HEAD_SIZE, pl.ds(key_start, CHUNK)]
            results.append((acc_ref[b] + dot(turned, d_scores), dot(joined, both_ref[b])))
        for b, key_start, (acc, d_keys) in zip(blocks_now, starts_now, results):
            acc_ref[b] = acc
            total_ref[pl.ds(key_start, CHUNK), :] += d_keys
        return carry

    lax.fori_loop(0, share, work, 0)

    def finish_block(b, carry):
        at = pl.multiple_of(b * BLOCK, BLOCK)
        result = (acc_ref[b] * scaling).T.astype(BF)
        dq_ref[pl.ds(at, BLOCK), :] = jnp.concatenate(
            [result[g * BLOCK : (g + 1) * BLOCK] for g in range(GROUP)], axis=1
        )
        return carry

    lax.fori_loop(0, blocks, finish_block, 0, unroll=4)

    def back(p, carry):
        target = pl.multiple_of(meta[p] * BLOCK, BLOCK)
        source = pl.multiple_of(p * BLOCK, BLOCK)
        dkv_ref[pl.ds(target, BLOCK), :] = total_ref[pl.ds(source, BLOCK), :].astype(BF)
        return carry

    lax.fori_loop(0, kv_ref.shape[0] // BLOCK, back, 0, unroll=8)


def local_call(kernel, outs, n_vmem, scratch, name):
    return pl.pallas_call(
        kernel,
        out_shape=outs,
        in_specs=[pl.BlockSpec(memory_space=pltpu.SMEM)] + [pl.BlockSpec(memory_space=pltpu.VMEM)] * n_vmem,
        out_specs=tuple(pl.BlockSpec(memory_space=pltpu.VMEM) for _ in outs),
        scratch_shapes=scratch,
        compiler_params=pltpu.CompilerParams(vmem_limit_bytes=40 * 2**20),
        cost_estimate=pl.CostEstimate(flops=4 * 10**9, bytes_accessed=10**7, transcendentals=4 * 10**6),
        name=name,
    )


def work_scratch(rows, keys):
    blocks = rows // BLOCK
    most = blocks * (keys // CHUNK + 1) + LANES
    return [pltpu.SMEM((most,), jnp.int32), pltpu.SMEM((most,), jnp.int32)]


def run_forward(meta, q, kv):
    rows, keys = q.shape[0], kv.shape[0]
    blocks = rows // BLOCK
    line = (blocks + 1, 1, WIDTH)
    return local_call(
        attention_forward,
        (jax.ShapeDtypeStruct((rows, WIDTH), BF), jax.ShapeDtypeStruct(line, F32)),
        2,
        [
            pltpu.VMEM((keys + CHUNK, 2 * HEAD_SIZE), BF),
            pltpu.VMEM((2 * HEAD_SIZE, keys + CHUNK), BF),
            pltpu.VMEM((blocks + 1, WIDTH, 2 * HEAD_SIZE), BF),
            pltpu.VMEM(line, jnp.int32),
            pltpu.VMEM(line, jnp.int32),
            pltpu.VMEM(line, F32),
            pltpu.VMEM(line, F32),
            pltpu.VMEM((blocks + 1, HEAD_SIZE, WIDTH), F32),
        ]
        + work_scratch(rows, keys),
        "attention_forward",
    )(meta, q, kv)


def run_backward(meta, q, kv, o, lse, d_o):
    rows, keys = q.shape[0], kv.shape[0]
    blocks = rows // BLOCK
    line = (blocks + 1, 1, WIDTH)
    return local_call(
        attention_backward,
        (jax.ShapeDtypeStruct((rows, WIDTH), BF), jax.ShapeDtypeStruct((keys, 2 * HEAD_SIZE), BF)),
        5,
        [
            pltpu.VMEM((keys + CHUNK, 2 * HEAD_SIZE), BF),
            pltpu.VMEM((2 * HEAD_SIZE, keys + CHUNK), BF),
            pltpu.VMEM((keys + CHUNK, 2 * HEAD_SIZE), F32),
            pltpu.VMEM((blocks + 1, 2 * WIDTH, 2 * HEAD_SIZE), BF),
            pltpu.VMEM(line, jnp.int32),
            pltpu.VMEM(line, jnp.int32),
            pltpu.VMEM(line, F32),
            pltpu.VMEM((blocks + 1, HEAD_SIZE, WIDTH), F32),
        ]
        + work_scratch(rows, keys),
        "attention_backward",
    )(meta, q, kv, o, lse, d_o)


def assemble_kernel(by_row_ref, by_head_ref, qkv_ref, out_ref, rest_ref):
    heads = [by_row_ref[0, h].astype(F32) for h in range(8)]
    ends = (0, WIDTH, WIDTH + HEAD_SIZE, HEAD_COLUMNS)
    qkv_ref[...] = jnp.concatenate([t[:, a:b] for a, b in zip(ends[:-1], ends[1:]) for t in heads], axis=1)
    tail = heads[0]
    for t in heads[1:]:
        tail = tail + t
    rest_ref[...] = tail[:, HEAD_COLUMNS:384]
    for parity in range(2):
        parts = [by_head_ref[y, 0, 1 - parity, :, 384:].astype(F32).T for y in range(4)]
        out_ref[parity * WIDTH : (parity + 1) * WIDTH, :] = jnp.concatenate(parts, axis=1)


def assemble(gathered):
    _, _, piece, columns = gathered.shape
    shard = 4 * piece
    return pl.pallas_call(
        assemble_kernel,
        out_shape=(
            jax.ShapeDtypeStruct((shard, 8 * HEAD_COLUMNS), F32),
            jax.ShapeDtypeStruct((2 * WIDTH, 4 * shard), F32),
            jax.ShapeDtypeStruct((shard, 64), F32),
        ),
        grid=(4,),
        in_specs=[
            pl.BlockSpec((1, 8, piece, columns), lambda i: (i, 0, 0, 0)),
            pl.BlockSpec((4, 1, 2, piece, columns), lambda i: (0, i, 0, 0, 0)),
        ],
        out_specs=(
            pl.BlockSpec((piece, 8 * HEAD_COLUMNS), lambda i: (i, 0)),
            pl.BlockSpec((2 * WIDTH, shard), lambda i: (0, i)),
            pl.BlockSpec((piece, 64), lambda i: (i, 0)),
        ),
        compiler_params=pltpu.CompilerParams(vmem_limit_bytes=40 * 2**20),
        name="assemble",
    )(gathered, gathered.reshape(4, 4, 2, piece, columns))


MESH = pl.DeviceIdType.MESH
ANY = pl.BlockSpec(memory_space=pl.ANY)


class Copies:
    def __init__(self, send, recv, local):
        self.send, self.recv, self.local = send, recv, local
        self.remote_count = self.local_count = 0
        self.started, self.kept = [], []

    def to(self, source, target, device):
        k = self.remote_count
        self.remote_count += 1
        copy = pltpu.make_async_remote_copy(
            source, target, self.send.at[k], self.recv.at[k], device_id=device, device_id_type=MESH
        )
        copy.start()
        self.started.append(copy)
        return copy

    def keep(self, source, middle, target):
        k = self.local_count
        self.local_count += 2
        first = pltpu.make_async_copy(source, middle, self.local.at[k])
        first.start()
        self.kept.append((first, pltpu.make_async_copy(middle, target, self.local.at[k + 1])))

    def move_kept(self):
        for first, second in self.kept:
            first.wait()
            second.start()

    def finish(self, arrived):
        for copy in self.started:
            copy.wait_send()
            if not any(copy is other for other in arrived):
                copy.wait_recv()
        for _, second in self.kept:
            second.wait()


def meet(devices):
    barrier = pltpu.get_barrier_semaphore()
    for device in devices:
        pl.semaphore_signal(barrier, inc=1, device_id=device, device_id_type=MESH)
    pl.semaphore_wait(barrier, len(devices))


def gather_rows_kernel(
    tok_ref, wp_ref, gain_ref, wo_ref, tok_out, wp_out, gain_out, wo_out, v_tok, v_wp, v_gain, v_wo, send, recv, local
):
    place, stream = turned(lax.axis_index("ctx")), lax.axis_index("wsh")
    x, z = place % 4, (place // 4) % 2
    right, left = {"ctx": turned(place - x + (x + 1) % 4)}, {"ctx": turned(place - x + (x + 3) % 4)}
    across = place + 4 - 8 * z
    other = {"wsh": stream + 1 - 2 * (stream % 2)}
    far = {"ctx": turned(across), "wsh": (stream + 2) % 4}
    meet([right, left, {"ctx": turned(across)}, other, far])
    copies = Copies(send, recv, local)
    half = tok_ref.shape[0] // 2
    own, own_z = z * 4 + x, (1 - z) * 4 + x
    left_id, right_id = z * 4 + (x + 3) % 4, z * 4 + (x + 1) % 4
    left_z, right_z = (1 - z) * 4 + (x + 3) % 4, (1 - z) * 4 + (x + 1) % 4

    def rows(ref, h):
        return ref.at[pl.ds(h * half, half)]

    def spot(block, h):
        return tok_out.at[block, pl.ds(h * half, half)]

    head = place % 8
    far_wp = copies.to(wp_ref.at[across % 8], wp_out.at[stream], far)
    far_gain = copies.to(gain_ref, gain_out.at[stream], far)
    cross = [copies.to(rows(tok_ref, h), spot(own, h), {"ctx": turned(across)}) for h in range(2)]
    to_right = [copies.to(rows(tok_ref, h), spot(own, h), right) for h in (0, 1)]
    to_left = [copies.to(rows(tok_ref, h), spot(own, h), left) for h in (1, 0)]
    copies.to(wp_ref.at[head], wp_out.at[stream], other)
    copies.to(gain_ref, gain_out.at[stream], other)
    third = wo_ref.shape[0] // 3
    parts = [pl.ds(i * third, third) for i in range(3)]
    far_wo = [copies.to(wo_ref.at[p], wo_out.at[stream, p], far) for p in parts]
    copies.to(wo_ref, wo_out.at[stream], other)
    copies.keep(tok_ref, v_tok, tok_out.at[own])
    copies.keep(wp_ref.at[head], v_wp, wp_out.at[stream])
    copies.keep(gain_ref, v_gain, gain_out.at[stream])
    copies.keep(wo_ref, v_wo, wo_out.at[stream])
    copies.move_kept()

    arrived = []

    def arrive(copy):
        copy.wait_recv()
        arrived.append(copy)

    far_stream = (stream + 2) % 4
    arrive(far_wp)
    copies.to(wp_out.at[far_stream], wp_out.at[far_stream], other)
    arrive(far_gain)
    copies.to(gain_out.at[far_stream], gain_out.at[far_stream], other)
    arrive(to_right[0])
    copies.to(spot(left_id, 0), spot(left_id, 0), right)
    arrive(to_left[0])
    copies.to(spot(right_id, 1), spot(right_id, 1), left)
    arrive(cross[0])
    arrive(cross[1])
    z_right = [copies.to(spot(own_z, h), spot(own_z, h), right) for h in (0, 1)]
    z_left = [copies.to(spot(own_z, h), spot(own_z, h), left) for h in (1, 0)]
    arrive(z_right[0])
    copies.to(spot(left_z, 0), spot(left_z, 0), right)
    arrive(z_left[0])
    copies.to(spot(right_z, 1), spot(right_z, 1), left)
    for p, copy in zip(parts, far_wo):
        arrive(copy)
        copies.to(wo_out.at[far_stream, p], wo_out.at[far_stream, p], other)
    copies.finish(arrived)


def gather_rows(tok, wp, gain, wo):
    return pl.pallas_call(
        gather_rows_kernel,
        out_shape=(
            jax.ShapeDtypeStruct((8,) + tok.shape, BF),
            jax.ShapeDtypeStruct((4,) + wp.shape[1:], BF),
            jax.ShapeDtypeStruct((4,) + gain.shape, BF),
            jax.ShapeDtypeStruct((4,) + wo.shape, BF),
        ),
        in_specs=[ANY] * 4,
        out_specs=(ANY,) * 4,
        scratch_shapes=[
            pltpu.VMEM(tok.shape, BF),
            pltpu.VMEM(wp.shape[1:], BF),
            pltpu.VMEM(gain.shape, BF),
            pltpu.VMEM(wo.shape, BF),
            pltpu.SemaphoreType.DMA((27,)),
            pltpu.SemaphoreType.DMA((27,)),
            pltpu.SemaphoreType.DMA((8,)),
        ],
        compiler_params=pltpu.CompilerParams(collective_id=1, has_side_effects=True, vmem_limit_bytes=40 * 2**20),
        name="gather_rows",
    )(tok, wp, gain, wo)


def gather_keys_kernel(kv_ref, kv_out, v_kv, send, recv, local):
    place = turned(lax.axis_index("ctx"))
    y = place // 8
    up, down = {"ctx": turned((place + 8) % 32)}, {"ctx": turned((place + 24) % 32)}
    meet([up, down])
    copies = Copies(send, recv, local)
    half = kv_ref.shape[0] // 2

    def rows(h):
        return kv_ref.at[pl.ds(h * half, half)]

    def spot(block, h):
        return kv_out.at[block, pl.ds(h * half, half)]

    to_up = [copies.to(rows(h), spot(y, h), up) for h in (0, 1)]
    to_down = [copies.to(rows(h), spot(y, h), down) for h in (1, 0)]
    copies.keep(kv_ref, v_kv, kv_out.at[y])
    copies.move_kept()
    to_up[0].wait_recv()
    copies.to(spot((y + 3) % 4, 0), spot((y + 3) % 4, 0), up)
    to_down[0].wait_recv()
    copies.to(spot((y + 1) % 4, 1), spot((y + 1) % 4, 1), down)
    copies.finish([to_up[0], to_down[0]])


def gather_keys(kv):
    return pl.pallas_call(
        gather_keys_kernel,
        out_shape=jax.ShapeDtypeStruct((4,) + kv.shape, BF),
        in_specs=[ANY],
        out_specs=ANY,
        scratch_shapes=[
            pltpu.VMEM(kv.shape, BF),
            pltpu.SemaphoreType.DMA((6,)),
            pltpu.SemaphoreType.DMA((6,)),
            pltpu.SemaphoreType.DMA((2,)),
        ],
        compiler_params=pltpu.CompilerParams(collective_id=2, has_side_effects=True, vmem_limit_bytes=40 * 2**20),
        name="gather_keys",
    )(kv)


FF_STEP = 256


def experts_kernel(
    rows_ref, grads_ref, w_ref, back_out, returned_out, half_send, half_keep, side_send, side_keep,
    w_v, x_v, g_v, turned_x, turned_g, out_v, d_in_v, acc_v, gate_v, up_v, hidden_v, d_gate_v, d_up_v, sent_v, got_v,
    send, recv, local,
):
    index, stream = lax.axis_index("ctx"), lax.axis_index("wsh")
    x, mine = index % 4, index // 2
    inner = (x + 1) // 2 % 2

    def device(p):
        return {"ctx": p // 2 * 4 + (1 - inner) * (3 * (p % 2)) + inner * (1 + p % 2)}

    peers = [(mine + k) % 16 for k in range(1, 16)]
    core = stream % 2
    other = {"wsh": stream + 1 - 2 * core}
    meet([device(p) for p in peers] + [other])
    copies = Copies(send, recv, local)
    width, rows = turned_x.shape
    quarter = width // 4
    own = []

    def here(source, target):
        copy = pltpu.make_async_copy(source, target, local.at[len(own)])
        copy.start()
        own.append(copy)
        return copy

    came = [copies.to(rows_ref.at[p], x_v.at[mine], device(p)) for p in peers]
    own_x = here(rows_ref.at[mine], x_v.at[mine])
    weights = [
        here(w_ref.at[4 * k + q, m], w_v.at[k, m, pl.ds(q * quarter, quarter)])
        for k in range(2)
        for q in range(4)
        for m in range(3)
    ]
    came_g = [copies.to(grads_ref.at[p], g_v.at[mine], device(p)) for p in peers]
    own_g = here(grads_ref.at[mine], g_v.at[mine])
    arrived = []

    def arrive(several):
        for copy in several:
            copy.wait_recv()
            arrived.append(copy)

    for copy in weights:
        copy.wait()
    arrive(came)
    own_x.wait()
    steps = w_v.shape[3] // FF_STEP
    acc_v[...] = jnp.zeros_like(acc_v)

    def forward(i, carry):
        k, at = i // steps, pl.ds(pl.multiple_of(i % steps * FF_STEP, FF_STEP), FF_STEP)
        inputs = x_v[...].reshape(rows, width)
        gate = dot(inputs, w_v[k, 0, :, at])
        up = dot(inputs, w_v[k, 1, :, at])
        hidden = (gate * jax.nn.sigmoid(gate) * up).astype(BF)
        gate_v[i] = gate
        up_v[i] = up
        hidden_v[k, :, at] = hidden
        acc_v[...] += dot(hidden, w_v[k, 2, :, at], NT)
        return carry

    lax.fori_loop(0, 2 * steps, forward, 0)
    out_v[...] = acc_v[...].astype(BF).reshape(out_v.shape)
    for p in peers:
        copies.to(out_v.at[p], back_out.at[mine], device(p))
    own_back = here(out_v.at[mine], back_out.at[mine])
    for q in range(4):
        at = slice(q * quarter, (q + 1) * quarter)
        turned_x[at, :] = x_v[:, :, at].reshape(rows, quarter).T
    acc_v[...] = jnp.zeros_like(acc_v)
    arrive(came_g)
    own_g.wait()

    def backward(i, carry):
        k, at = i // steps, pl.ds(pl.multiple_of(i % steps * FF_STEP, FF_STEP), FF_STEP)
        d_hidden = dot(g_v[...].reshape(rows, width), w_v[k, 2, :, at])
        gate, up = gate_v[i], up_v[i]
        sigmoid = jax.nn.sigmoid(gate)
        d_gate = (d_hidden * up * sigmoid * (1.0 + gate * (1.0 - sigmoid))).astype(BF)
        d_up = (d_hidden * (gate * sigmoid)).astype(BF)
        d_gate_v[k, :, at] = d_gate
        d_up_v[k, :, at] = d_up
        acc_v[...] += dot(d_gate, w_v[k, 0, :, at], NT) + dot(d_up, w_v[k, 1, :, at], NT)
        return carry

    lax.fori_loop(0, 2 * steps, backward, 0)
    d_in_v[...] = acc_v[...].astype(BF).reshape(d_in_v.shape)
    for p in peers:
        copies.to(d_in_v.at[p], returned_out.at[mine], device(p))
    own_returned = here(d_in_v.at[mine], returned_out.at[mine])
    for q in range(4):
        at = slice(q * quarter, (q + 1) * quarter)
        turned_g[at, :] = g_v[:, :, at].reshape(rows, quarter).T

    def terms(k, z, c):
        at = pl.ds(pl.multiple_of((2 * z + c) * quarter, quarter), quarter)
        part = turned_x[at, :]
        return (
            dot(part, d_gate_v[k]),
            dot(part, d_up_v[k]),
            dot(turned_g[at, :], hidden_v[k]),
        )

    half, side = index % 2, stream // 2
    crossing = []
    for dz in (1, 0):
        z = side + dz - 2 * side * dz

        def other_term(k, carry, z=z, dz=dz):
            for m, term in enumerate(terms(k, z, 1 - core)):
                sent_v[dz, k, m] = term.astype(BF)
            return carry

        lax.fori_loop(0, 2, other_term, 0)
        crossing.append(copies.to(sent_v.at[dz], got_v.at[dz], other))
    halfway = quarter // 2
    for dz, copy in zip((1, 0), crossing):
        z = side + dz - 2 * side * dz
        arrive([copy])
        for dk in (1, 0):
            k = half + dk - 2 * half * dk
            for m, term in enumerate(terms(k, z, core)):
                total = (term + got_v[dz, k, m].astype(F32)).astype(BF)
                (half_send if dk else half_keep)[z, m] = total[:halfway]
                (side_send if dz else side_keep)[k, m] = total[halfway:]
    copies.finish(arrived)
    own_back.wait()
    own_returned.wait()


def experts(send_rows, send_grads, weights):
    groups, capacity, width = send_rows.shape
    rows = groups * capacity
    half = weights.shape[3]
    vmem = pltpu.VMEM
    steps = 2 * half // FF_STEP
    slots = vmem(send_rows.shape, BF)
    terms = (2, 2, 3, width // 4, half)
    return pl.pallas_call(
        experts_kernel,
        out_shape=(
            jax.ShapeDtypeStruct(send_rows.shape, BF),
            jax.ShapeDtypeStruct(send_rows.shape, BF),
        )
        + (jax.ShapeDtypeStruct((2, 3, width // 8, half), BF),) * 4,
        in_specs=[ANY, ANY, ANY],
        out_specs=(ANY, ANY) + (pl.BlockSpec(memory_space=pltpu.VMEM),) * 4,
        scratch_shapes=[
            vmem((2, 3, width, half), BF),
            slots,
            slots,
            vmem((width, rows), BF),
            vmem((width, rows), BF),
            slots,
            slots,
            vmem((rows, width), F32),
            vmem((steps, rows, FF_STEP), F32),
            vmem((steps, rows, FF_STEP), F32),
            vmem((2, rows, half), BF),
            vmem((2, rows, half), BF),
            vmem((2, rows, half), BF),
            vmem(terms, BF),
            vmem(terms, BF),
            pltpu.SemaphoreType.DMA((62,)),
            pltpu.SemaphoreType.DMA((62,)),
            pltpu.SemaphoreType.DMA((28,)),
        ],
        compiler_params=pltpu.CompilerParams(collective_id=6, has_side_effects=True, vmem_limit_bytes=56 * 2**20),
        cost_estimate=pl.CostEstimate(flops=15 * 10**9, bytes_accessed=10**8, transcendentals=10**6),
        name="experts",
    )(send_rows, send_grads, weights)


def prepare_kernel(qkv_ref, router_ref, wo_ref, wp_out, wo_out):
    rows = qkv_ref.shape[0]
    experts = router_ref.shape[1]
    wo_out[...] = wo_ref[...].astype(BF)
    router = router_ref[...].astype(BF)
    tail = jnp.zeros((rows, wp_out.shape[2] - HEAD_COLUMNS - experts), BF)
    k_at, v_at = QUERY_HEADS * HEAD_SIZE, (QUERY_HEADS + KEY_VALUE_HEADS) * HEAD_SIZE
    for h in range(KEY_VALUE_HEADS):
        wp_out[h] = jnp.concatenate(
            [
                qkv_ref[:, h * WIDTH : (h + 1) * WIDTH].astype(BF),
                qkv_ref[:, k_at + h * HEAD_SIZE : k_at + (h + 1) * HEAD_SIZE].astype(BF),
                qkv_ref[:, v_at + h * HEAD_SIZE : v_at + (h + 1) * HEAD_SIZE].astype(BF),
                router,
                tail,
            ],
            axis=1,
        )


def prepare(w_qkv, w_router, w_out):
    shard = w_qkv.shape[0]
    step = shard // 3

    def block(n):
        return pl.BlockSpec((step, n), lambda i: (i, 0))

    return pl.pallas_call(
        prepare_kernel,
        out_shape=(
            jax.ShapeDtypeStruct((KEY_VALUE_HEADS, shard, 384), BF),
            jax.ShapeDtypeStruct(w_out.shape, BF),
        ),
        grid=(3,),
        in_specs=[block(w_qkv.shape[1]), block(w_router.shape[1]), block(w_out.shape[1])],
        out_specs=(
            pl.BlockSpec((KEY_VALUE_HEADS, step, 384), lambda i: (0, i, 0)),
            block(w_out.shape[1]),
        ),
        compiler_params=pltpu.CompilerParams(vmem_limit_bytes=40 * 2**20),
        name="prepare",
    )(w_qkv, w_router, w_out)


def finish_kernel(
    dq_ref, kv_ref, act_ref, small_ref, out_ref, p0, p1, p2, p3, x_ref, d_mid_ref, gain_ref, d_tokens_ref, all_out,
    kv_v, out_v, grad_v, grad_to, term_v, term_to, act_t, own_v, w_v, acc_v,
    send, recv, out_send, out_recv, local,
):
    place, stream = turned(lax.axis_index("ctx")), lax.axis_index("wsh")
    y, r = place // 8, place % 8
    x, z = r % 4, r // 4

    def at_place(p):
        return {"ctx": turned(p)}

    right, left = at_place(place - x + (x + 1) % 4), at_place(place - x + (x + 3) % 4)
    across = at_place(place + 4 - 8 * z)
    up, down, beyond = (at_place((place + 8 * k) % 32) for k in (1, 3, 2))
    others = [((y + k // 4) % 4, (stream + k % 4) % 4) for k in range(1, 16)]
    in_row = [(r + k) % 8 for k in range(1, 8)]
    served = 2 * stream + 1 - r % 2

    def out_target(p):
        return {"ctx": turned(p // 4 * 8 + 2 * (p % 4) + 1 - r % 2), "wsh": r // 2}

    barrier = pltpu.get_barrier_semaphore()
    partners = [{"ctx": turned(r + 8 * py), "wsh": pw} for py, pw in others]
    partners += [at_place(8 * y + pr) for pr in in_row]
    sources = [{"ctx": turned(i // 4 * 8 + served), "wsh": i % 4} for i in range(16)]
    for device in partners + sources:
        pl.semaphore_signal(barrier, inc=1, device_id=device, device_id_type=MESH)
    pl.semaphore_wait(barrier, len(partners) + 16)

    copies = Copies(send, recv, local)
    rows, width = act_ref.shape
    shard, piece = width // 4, own_v.shape[0]
    arrived = []

    def arrive(*which):
        for copy in which:
            copy.wait_recv()
            arrived.append(copy)

    own = []

    def here(source, target):
        copy = pltpu.make_async_copy(source, target, local.at[len(own)])
        copy.start()
        own.append(copy)
        return copy

    kv_came = [
        copies.to(kv_ref.at[(y + k) % 4], kv_v.at[y], at_place((place + 8 * k) % 32)) for k in (2, 1, 3)
    ]
    own_kv = here(kv_ref.at[y], kv_v.at[y])
    out_copies = []
    for p in range(16):
        copy = pltpu.make_async_remote_copy(
            out_ref.at[pl.ds(p % 4 * shard + p // 4 * piece, piece)],
            out_v.at[y * 4 + stream],
            out_send.at[p],
            out_recv.at[y * 4 + stream],
            device_id=out_target(p),
            device_id_type=MESH,
        )
        copy.start()
        out_copies.append(copy)
    weights = [here(p, w_v.at[j]) for j, p in enumerate((p0, p1, p2, p3))]
    dq = dq_ref[...]
    for q in range(4):
        act_t[q * shard : (q + 1) * shard, :] = act_ref[:, q * shard : (q + 1) * shard].T
    for q in range(4):
        term = dot(act_t[q * shard : (q + 1) * shard, :], dq).astype(BF)
        for i in range(4):
            term_v[i, q, :, :WIDTH] = term[i * piece : (i + 1) * piece]
            at = q * shard + i * piece
            term_v[i, q, :, HEAD_COLUMNS:] = small_ref[at : at + piece, :]
    own_kv.wait()
    arrive(*kv_came)
    total = kv_v[0].astype(F32)
    for i in range(1, 4):
        total = total + kv_v[i].astype(F32)
    kv = total.astype(BF)
    grad_v[...] = jnp.concatenate([dq, kv, jnp.zeros((rows, 64), BF)], axis=1).reshape(grad_v.shape)
    grads = [copies.to(grad_v.at[pr], grad_to.at[r], at_place(8 * y + pr)) for pr in in_row]
    own_grad = here(grad_v.at[r], grad_to.at[r])
    terms = []
    for dw in (2, 3, 1, 0):
        pw = (stream + dw) % 4
        part = act_t[pl.ds(pl.multiple_of(pw * shard, shard), shard), :]
        term = dot(part, kv).astype(BF)
        for i in range(4):
            term_v[i, pw, :, WIDTH:HEAD_COLUMNS] = term[i * piece : (i + 1) * piece]
        for dy in (2, 1, 3, 0):
            py = (y + dy) % 4
            if dw or dy:
                device = {"ctx": turned(r + 8 * py), "wsh": pw}
                terms.append(copies.to(term_v.at[py, pw], term_to.at[y, stream], device))
    own_term = here(term_v.at[y, stream], term_to.at[y, stream])
    for i, copy in enumerate(out_copies):
        pltpu.make_async_remote_copy(
            out_v.at[i], out_v.at[i], out_send.at[i], out_recv.at[i], device_id=across, device_id_type=MESH
        ).wait_recv()
        copy.wait_send()
    total = out_v[0].astype(F32)
    for i in range(1, 16):
        total = total + out_v[i].astype(F32)
    own_v[:, 384:] = total.astype(BF)
    own_term.wait()
    arrive(*terms)
    total = term_to[0, 0].astype(F32)
    for i in range(1, 16):
        total = total + term_to[i // 4, i % 4].astype(F32)
    own_v[:, :384] = total.astype(BF)

    half = piece // 2
    first, last = pl.ds(0, half), pl.ds(half, half)
    r_z = (1 - z) * 4 + x
    r_left, r_right = z * 4 + (x + 3) % 4, z * 4 + (x + 1) % 4
    z_left, z_right = (1 - z) * 4 + (x + 3) % 4, (1 - z) * 4 + (x + 1) % 4

    def on(device, *at):
        return copies.to(all_out.at[at], all_out.at[at], device)

    a_cross = copies.to(own_v.at[first], all_out.at[y, r, first], across)
    a_right = copies.to(own_v.at[first], all_out.at[y, r, first], right)
    a_left = copies.to(own_v.at[first], all_out.at[y, r, first], left)
    b_up = copies.to(own_v.at[last], all_out.at[y, r, last], up)
    b_down = copies.to(own_v.at[last], all_out.at[y, r, last], down)
    b_beyond = copies.to(own_v.at[last], all_out.at[y, r, last], beyond)
    keep = here(own_v, all_out.at[y, r])

    for copy in weights:
        copy.wait()
    own_grad.wait()
    arrive(*grads)
    acc_v[...] = jnp.zeros_like(acc_v)
    shards = (stream, stream + 1 - 2 * (stream % 2), (stream + 2) % 4, 3 - stream)

    def heads(start, count):
        def one(h, carry):
            grad = grad_to[h][:, :HEAD_COLUMNS]
            for j in range(4):
                acc_v[shards[j]] += dot(grad, w_v[j, h][:, :HEAD_COLUMNS], NT)
            return carry

        lax.fori_loop(start, start + count, one, 0)

    heads(0, 2)
    keep.wait()
    arrive(a_cross)
    a_z_right = on(right, y, r_z, first)
    a_z_left = on(left, y, r_z, first)
    arrive(a_right)
    a_on = on(right, y, r_left, first)
    arrive(b_up, b_down, b_beyond)
    lower, upper, every = pl.ds(0, 2), pl.ds(2, 2), pl.ds(0, 4)
    b_right = on(right, every, r, last)
    b_left = on(left, every, r, last)
    b_cross = on(across, every, r, last)
    heads(2, 2)
    arrive(a_z_left, a_left)
    a_z_on = on(left, y, z_right, first)
    arrive(a_z_right, a_on, a_z_on)
    low_r, high_r = pl.ds(0, 4), pl.ds(4, 4)
    c_up = [on(up, y, low_r, first), on(up, y, high_r, first)]
    c_down = [on(down, y, high_r, first), on(down, y, low_r, first)]
    heads(4, 2)
    arrive(b_right)
    on(right, lower, r_left, last)
    arrive(b_left)
    on(left, upper, r_right, last)
    arrive(b_cross)
    b_z_right = on(right, every, r_z, last)
    b_z_left = on(left, every, r_z, last)
    arrive(c_up[0])
    on(up, (y + 3) % 4, low_r, first)
    arrive(c_down[0])
    on(down, (y + 1) % 4, high_r, first)
    heads(6, 2)
    arrive(b_z_right)
    on(right, lower, z_left, last)
    arrive(b_z_left)
    on(left, upper, z_right, last)
    values = x_ref[...].astype(F32)
    scale = rms_scale(values)
    inner = 0.0
    for q in range(4):
        at = slice(q * shard, (q + 1) * shard)
        inner += jnp.sum(acc_v[q] * gain_ref[:, at] * values[:, at], axis=-1, keepdims=True)
    inner = inner * (1.0 / width)
    for q in range(4):
        at = slice(q * shard, (q + 1) * shard)
        d_tokens_ref[:, at] = (
            d_mid_ref[:, at] + scale * (acc_v[q] * gain_ref[:, at]) - values[:, at] * scale**3 * inner
        ).astype(BF)
    copies.finish(arrived)


def finish(dq, kv, act, small, out_term, pieces, x, d_middle, gain):
    rows, width = act.shape
    piece = width // 16
    vmem = pl.BlockSpec(memory_space=pltpu.VMEM)
    scratch = pltpu.VMEM
    return pl.pallas_call(
        finish_kernel,
        out_shape=(
            jax.ShapeDtypeStruct(x.shape, BF),
            jax.ShapeDtypeStruct((4, 8, piece, 384 + WIDTH), BF),
        ),
        in_specs=[vmem, ANY, vmem, vmem, ANY] + [ANY] * 4 + [vmem] * 3,
        out_specs=(vmem, ANY),
        scratch_shapes=[
            scratch(kv.shape, BF),
            scratch((16, piece, WIDTH), BF),
            scratch((8, rows // 8, 384), BF),
            scratch((8, rows // 8, 384), BF),
            scratch((4, 4, piece, 384), BF),
            scratch((4, 4, piece, 384), BF),
            scratch((width, rows), BF),
            scratch((piece, 384 + WIDTH), BF),
            scratch((4,) + pieces[0].shape, BF),
            scratch((4, rows // 8, width // 4), F32),
            pltpu.SemaphoreType.DMA((50,)),
            pltpu.SemaphoreType.DMA((50,)),
            pltpu.SemaphoreType.DMA((16,)),
            pltpu.SemaphoreType.DMA((16,)),
            pltpu.SemaphoreType.DMA((8,)),
        ],
        compiler_params=pltpu.CompilerParams(collective_id=3, has_side_effects=True, vmem_limit_bytes=52 * 2**20),
        cost_estimate=pl.CostEstimate(flops=3 * 10**9, bytes_accessed=10**8, transcendentals=0),
        name="finish",
    )(dq, kv, act, small, out_term, *pieces, x, d_middle, gain.reshape(1, width))


def swap(x, groups, axis="ctx"):
    return lax.all_to_all(x, axis, 0, 0, axis_index_groups=groups, tiled=True)


def rms_scale(values):
    return lax.rsqrt(jnp.mean(values * values, axis=-1, keepdims=True) + EPSILON)


def body(
    tokens,
    lengths,
    deal,
    expert_ids,
    gain_attn,
    w_qkv,
    w_out,
    gain_moe,
    w_router,
    w_gate,
    w_up,
    w_down,
    cotangent,
):
    stream = lax.axis_index("wsh")
    index = lax.axis_index("ctx")
    place = turned(index)
    rows, width = tokens.shape[1], tokens.shape[2]
    shard = w_qkv.shape[0]
    experts_count = w_router.shape[1]
    capacity = 2 * rows * TOP // experts_count
    head = place % 8
    head_row = place // 8
    lengths_row = lax.dynamic_index_in_dim(lengths, stream, 0, keepdims=False)
    deal_row = lax.dynamic_index_in_dim(deal, stream, 0, keepdims=False)
    blocks = deal_row.shape[0]
    deal_row = deal_row.reshape(4, 2, 4, 2).transpose(2, 1, 0, 3).reshape(blocks)
    block_ids = jnp.arange(blocks, dtype=jnp.int32)
    inverse = jnp.sum(jnp.where(deal_row[None, :] == block_ids[:, None], block_ids[None, :], 0), axis=1)
    own_blocks = lax.dynamic_slice_in_dim(deal_row, head_row * 16, 16)
    meta = jnp.concatenate([inverse, own_blocks, jnp.cumsum(lengths_row)]).astype(jnp.int32)

    q_columns = QUERY_HEADS * HEAD_SIZE
    by_head, own_out = prepare(w_qkv, w_router, w_out)
    own_gains = jnp.concatenate(
        [gain_attn.astype(BF)[None], gain_moe.astype(BF)[None], jnp.zeros((14, shard), BF)], axis=0
    )
    group_tokens, head_full, gains, full_out = gather_rows(tokens[0], by_head, own_gains, own_out)
    head_full = head_full.reshape(width, -1)
    head_weight = head_full[:, :HEAD_COLUMNS]
    full_router = head_full[:, HEAD_COLUMNS : HEAD_COLUMNS + experts_count]
    gain_first = gains[:, 0].reshape(width).astype(F32)
    gain_second = gains[:, 1].reshape(width).astype(F32)
    full_out = full_out.reshape(q_columns, width)

    w_gate, w_up, w_down, _ = lax.optimization_barrier((w_gate, w_up, w_down, gains))
    expert_shard = jnp.stack([w_gate[0].astype(BF), w_up[0].astype(BF), w_down[0].T.astype(BF)])
    expert_all = lax.all_gather(expert_shard, ("ctx", "wsh"), axis_index_groups=OWNERS)
    far_qkv = lax.ppermute(by_head, ("ctx", "wsh"), NEXT_Z)
    qkv_pieces = [
        by_head,
        lax.ppermute(by_head, "wsh", OTHER_CORE),
        far_qkv,
        lax.ppermute(far_qkv, "wsh", OTHER_CORE),
    ]

    group_x = group_tokens.reshape(8 * rows, width).astype(F32)
    group_act = (group_x * rms_scale(group_x) * gain_first).astype(BF)
    head_qkv = dot(group_act, head_weight).astype(BF)
    kv_all = gather_keys(head_qkv[:, WIDTH:]).reshape(32 * rows, 2 * HEAD_SIZE)
    head_q = head_qkv[:, :WIDTH]
    head_attn, lse = run_forward(meta, head_q, kv_all)
    attn_low = swap(head_attn.reshape(8, rows, WIDTH), ROW).transpose(1, 0, 2).reshape(rows, q_columns)

    x_first = tokens[0].astype(F32)
    middle = x_first + dot(attn_low, full_out)
    scale_second = rms_scale(middle)
    act_moe = (middle * scale_second * gain_second).astype(BF)
    logits = dot(act_moe, full_router)
    choice = expert_ids[0]
    expert_range = jnp.arange(experts_count, dtype=jnp.int32)
    picked_hot = choice[:, :, None] == expert_range[None, None, :]
    picked = jnp.sum(jnp.where(picked_hot, logits[:, None, :], 0.0), axis=-1)
    picked_exp = jnp.exp(picked - jnp.max(picked, axis=-1, keepdims=True))
    gates = picked_exp / jnp.sum(picked_exp, axis=-1, keepdims=True)
    flat_ids = choice.reshape(-1)
    assign_hot = (flat_ids[:, None] == expert_range[None, :]).astype(jnp.int32)
    ranks = jnp.sum((jnp.cumsum(assign_hot, axis=0) - 1) * assign_hot, axis=1)
    slots = (flat_ids * capacity + ranks).reshape(rows, TOP)
    slot_range = jnp.arange(experts_count * capacity, dtype=jnp.int32)
    hot = [slots[:, j][:, None] == slot_range[None, :] for j in range(TOP)]
    hot_low = [h.astype(BF) for h in hot]
    hot_any = hot_low[0] + hot_low[1]
    slot_gate = sum(jnp.sum(jnp.where(hot[j], gates[:, j][:, None], 0.0), axis=0) for j in range(TOP))

    send_rows = dot(hot_any, act_moe, TN).astype(BF).reshape(experts_count, capacity, width)
    send_grads = (slot_gate[:, None] * dot(hot_any, cotangent[0], TN)).astype(BF)
    back_rows, returned, *expert_terms = experts(send_rows, send_grads.reshape(experts_count, capacity, width), expert_all)
    back_rows, returned = (r.reshape(-1, width) for r in (back_rows, returned))

    both = [dot(hot_low[j], back_rows) for j in range(TOP)]
    output_rows = (middle + gates[:, :1] * both[0] + gates[:, 1:] * both[1]).astype(BF)
    d_out = cotangent[0].astype(F32)
    d_gates = jnp.stack([jnp.sum(d_out * both[j], axis=-1) for j in range(TOP)], axis=1)
    d_picked = gates * (d_gates - jnp.sum(gates * d_gates, axis=-1, keepdims=True))
    d_logits = jnp.sum(jnp.where(picked_hot, d_picked[:, :, None], 0.0), axis=1).astype(BF)
    d_act_moe = dot(hot_any, returned) + dot(d_logits, full_router, NT)
    d_router_local = dot(act_moe, d_logits, TN)
    d_gain_second = jnp.sum(d_act_moe * middle * scale_second, axis=0)
    scaled = d_act_moe * gain_second
    d_middle = (
        d_out
        + scale_second * scaled
        - middle * scale_second**3 * jnp.mean(scaled * middle, axis=-1, keepdims=True)
    )
    d_branch = d_middle.astype(BF)

    d_attn = dot(d_branch, full_out, NT).astype(BF)
    head_d_attn = swap(d_attn.reshape(rows, 8, WIDTH).transpose(1, 0, 2), ROW).reshape(8 * rows, WIDTH)
    group_branch = lax.all_gather(d_branch, "ctx", axis_index_groups=ROW).reshape(8 * rows, width)
    head_d_attn, expert_terms, qkv_pieces = lax.optimization_barrier((head_d_attn, expert_terms, qkv_pieces))
    half_send, half_keep, side_send, side_keep = expert_terms
    by_half = (half_keep, lax.ppermute(half_send, "ctx", OTHER_HALF))
    by_side = (side_keep, lax.ppermute(side_send, "wsh", OTHER_SIDE))
    d_q, d_kv = run_backward(meta, head_q, kv_all, head_attn, lse, head_d_attn)
    small_term = jnp.concatenate(
        [d_router_local.astype(BF), d_gain_second.astype(BF)[:, None], jnp.zeros((width, 47), BF)], axis=1
    )
    out_term = dot(group_branch, head_attn, TN).astype(BF)
    by_half, by_side, d_q = lax.optimization_barrier((by_half, by_side, d_q))

    def part_sum(terms, which):
        return sum(lax.dynamic_index_in_dim(t, which, 0, keepdims=False).astype(F32) for t in terms)

    half, side = index % 2, stream // 2
    half_got = lax.ppermute(part_sum(by_half, 1 - side).astype(BF), "wsh", OTHER_SIDE)
    side_got = lax.ppermute(part_sum(by_side, 1 - half).astype(BF), "ctx", OTHER_HALF)
    d_tokens, gathered = finish(
        d_q,
        d_kv.reshape(4, 8 * rows, 2 * HEAD_SIZE),
        group_act,
        small_term,
        out_term,
        qkv_pieces,
        tokens[0],
        d_middle,
        gain_first,
    )
    gathered, half_got, side_got = lax.optimization_barrier((gathered, half_got, side_got))
    expert_own = jnp.concatenate(
        [part_sum(by_half, side) + half_got.astype(F32), part_sum(by_side, half) + side_got.astype(F32)], axis=1
    )
    d_w_qkv, d_w_out, rest = assemble(gathered)
    d_gain_first = jnp.sum(d_w_qkv * w_qkv.astype(BF).astype(F32), axis=1) / gain_attn.astype(BF).astype(F32)
    return (
        output_rows[None],
        d_tokens[None],
        d_gain_first,
        d_w_qkv,
        d_w_out,
        rest[:, experts_count],
        rest[:, :experts_count],
        expert_own[0][None],
        expert_own[1][None],
        expert_own[2].T[None],
    )


def solution(mesh):
    placed = (
        P("wsh", "ctx", None),
        P(),
        P(),
        P("wsh", "ctx", None),
        P("wsh"),
        P("wsh", None),
        P("wsh", None),
        P("wsh"),
        P("wsh", None),
        P("ctx", "wsh", None),
        P("ctx", "wsh", None),
        P("ctx", None, "wsh"),
        P("wsh", "ctx", None),
    )
    return jax.shard_map(
        body,
        mesh=mesh,
        in_specs=placed,
        out_specs=(
            P("wsh", "ctx", None),
            P("wsh", "ctx", None),
            P("wsh"),
            P("wsh", None),
            P("wsh", None),
            P("wsh"),
            P("wsh", None),
            P("ctx", "wsh", None),
            P("ctx", "wsh", None),
            P("ctx", None, "wsh"),
        ),
        check_vma=False,
    )
```

```python
import functools

import jax
import jax.numpy as jnp
from jax import lax
from jax.experimental import pallas as pl
from jax.experimental.pallas import tpu as pltpu
from jax.sharding import PartitionSpec as P

QUERY_HEADS = 24
KEY_VALUE_HEADS = 8
HEAD_SIZE = 64
GROUP = QUERY_HEADS // KEY_VALUE_HEADS
TOP = 2
BLOCK = 64
WIDTH = GROUP * HEAD_SIZE
HEAD_COLUMNS = WIDTH + 2 * HEAD_SIZE
CHUNK = 512
LANES = 3
TURN = 256

EPSILON = 1e-05
NEG_BIG = -1e30
BF = jnp.bfloat16
F32 = jnp.float32

def turned(index):
    return index % 4 * 8 + index // 4 % 2 * 4 + index // 8


ROW = [[turned(y * 8 + r) for r in range(8)] for y in range(4)]
OWNERS = [[(2 * e + k) * 4 + w for k in range(2) for w in range(4)] for e in range(16)]
OTHER_HALF = [(c, c ^ 1) for c in range(32)]
OTHER_SIDE = [(w, w ^ 2) for w in range(4)]
OTHER_CORE = [(w, w ^ 1) for w in range(4)]
NEXT_Z = [(c * 4 + w, (c ^ 4) * 4 + (w ^ 2)) for c in range(32) for w in range(4)]

def dot(a, b, dims=((1,), (0,))):
    return lax.dot_general(a, b, (dims, ((), ())), preferred_element_type=F32)


NT = ((1,), (1,))
TN = ((0,), (0,))


def block_range(meta, b):
    base = meta[BLOCK + b] * BLOCK
    lane = lax.broadcasted_iota(jnp.int32, (1, WIDTH), 1)
    query = base + (lane & (BLOCK - 1))
    start = jnp.zeros((1, WIDTH), jnp.int32)
    first = jnp.int32(0)
    for i in range(3):
        bound = meta[80 + i]
        start = jnp.where(query >= bound, bound, start)
        first = jnp.where(base >= bound, bound, first)
    first = (first // 128) * 128
    count = (base + BLOCK - first + CHUNK - 1) // CHUNK
    return query, start, first, count


def list_work(meta, blocks, block_s, key_s):
    def one(b, n):
        _, _, first, count = block_range(meta, b)

        def put(i, n):
            block_s[n] = b
            key_s[n] = first + i * CHUNK
            return n + 1

        return lax.fori_loop(0, count, put, n)

    total = lax.fori_loop(0, blocks, one, jnp.int32(0))
    for i in range(LANES):
        block_s[total + i] = blocks
        key_s[total + i] = 0
    return (total + LANES - 1) // LANES


def allowed_of(key_start, query, start):
    key = key_start + lax.broadcasted_iota(jnp.int32, (CHUNK, WIDTH), 0)
    return (key <= query) & (key >= start)


def stack_heads(rows):
    return jnp.concatenate([rows[:, g * HEAD_SIZE : (g + 1) * HEAD_SIZE] for g in range(GROUP)], axis=0)


def sort_blocks(meta, kv_ref, sorted_ref):
    total = kv_ref.shape[0]

    def one(p, carry):
        source = pl.multiple_of(meta[p] * BLOCK, BLOCK)
        target = pl.multiple_of(p * BLOCK, BLOCK)
        sorted_ref[pl.ds(target, BLOCK), :] = kv_ref[pl.ds(source, BLOCK), :]
        return carry

    lax.fori_loop(0, total // BLOCK, one, 0, unroll=8)
    sorted_ref[total:, :] = jnp.zeros((CHUNK, sorted_ref.shape[1]), sorted_ref.dtype)


def transpose_all(sorted_ref, turned_ref):
    steps = sorted_ref.shape[0] // TURN

    def one(i, carry):
        at = pl.multiple_of(i * TURN, TURN)
        turned_ref[:, pl.ds(at, TURN)] = sorted_ref[pl.ds(at, TURN), :].T
        return carry

    lax.fori_loop(0, steps, one, 0)


def attention_forward(
    meta, q_ref, kv_ref, o_ref, lse_ref,
    sorted_ref, turned_ref, pad_ref, query_ref, start_ref, top_ref, total_ref, acc_ref, block_s, key_s,
):
    blocks = q_ref.shape[0] // BLOCK
    sort_blocks(meta, kv_ref, sorted_ref)
    transpose_all(sorted_ref, turned_ref)
    share = list_work(meta, blocks, block_s, key_s)
    zeros = jnp.zeros((WIDTH, HEAD_SIZE), BF)
    top_ref[...] = jnp.full(top_ref.shape, NEG_BIG, F32)
    total_ref[...] = jnp.zeros_like(total_ref)
    acc_ref[...] = jnp.zeros_like(acc_ref)
    query_ref[blocks] = jnp.full((1, WIDTH), -1, jnp.int32)
    start_ref[blocks] = jnp.zeros((1, WIDTH), jnp.int32)
    pad_ref[blocks] = jnp.zeros((WIDTH, 2 * HEAD_SIZE), BF)

    def prepare_block(b, carry):
        query_ref[b], start_ref[b], _, _ = block_range(meta, b)
        at = pl.multiple_of(b * BLOCK, BLOCK)
        rows = stack_heads(q_ref[pl.ds(at, BLOCK), :]) * jnp.asarray(HEAD_SIZE**-0.5, BF)
        pad_ref[b] = jnp.concatenate([rows, zeros], axis=1)
        return carry

    lax.fori_loop(0, blocks, prepare_block, 0, unroll=4)

    def work(i, carry):
        blocks_now = [block_s[lane * share + i] for lane in range(LANES)]
        starts_now = [pl.multiple_of(key_s[lane * share + i], 128) for lane in range(LANES)]
        results = []
        for b, key_start in zip(blocks_now, starts_now):
            scores = dot(sorted_ref[pl.ds(key_start, CHUNK), :], pad_ref[b], NT)
            scores = jnp.where(allowed_of(key_start, query_ref[b], start_ref[b]), scores, NEG_BIG)
            top = top_ref[b]
            top_new = jnp.maximum(top, jnp.max(scores, axis=0, keepdims=True))
            weights = jnp.exp(scores - top_new)
            fade = jnp.exp(top - top_new)
            total = total_ref[b] * fade + jnp.sum(weights, axis=0, keepdims=True)
            values = turned_ref[HEAD_SIZE:, pl.ds(key_start, CHUNK)]
            results.append((top_new, total, acc_ref[b] * fade + dot(values, weights.astype(BF))))
        for b, (top, total, acc) in zip(blocks_now, results):
            top_ref[b] = top
            total_ref[b] = total
            acc_ref[b] = acc
        return carry

    lax.fori_loop(0, share, work, 0)

    def finish_block(b, carry):
        at = pl.multiple_of(b * BLOCK, BLOCK)
        total = total_ref[b]
        lse_ref[b] = top_ref[b] + jnp.log(total)
        result = (acc_ref[b] / total).T.astype(BF)
        o_ref[pl.ds(at, BLOCK), :] = jnp.concatenate(
            [result[g * BLOCK : (g + 1) * BLOCK] for g in range(GROUP)], axis=1
        )
        return carry

    lax.fori_loop(0, blocks, finish_block, 0, unroll=4)


def attention_backward(
    meta, q_ref, kv_ref, o_ref, lse_ref, do_ref, dq_ref, dkv_ref,
    sorted_ref, turned_ref, total_ref, both_ref, query_ref, start_ref, delta_ref, acc_ref, block_s, key_s,
):
    blocks = q_ref.shape[0] // BLOCK
    sort_blocks(meta, kv_ref, sorted_ref)
    transpose_all(sorted_ref, turned_ref)
    share = list_work(meta, blocks, block_s, key_s)
    total_ref[...] = jnp.zeros_like(total_ref)
    acc_ref[...] = jnp.zeros_like(acc_ref)
    query_ref[blocks] = jnp.full((1, WIDTH), -1, jnp.int32)
    start_ref[blocks] = jnp.zeros((1, WIDTH), jnp.int32)
    delta_ref[blocks] = jnp.zeros((1, WIDTH), F32)
    both_ref[blocks] = jnp.zeros((2 * WIDTH, 2 * HEAD_SIZE), BF)
    zeros = jnp.zeros((WIDTH, HEAD_SIZE), BF)
    scaling = HEAD_SIZE**-0.5

    def prepare_block(b, carry):
        query_ref[b], start_ref[b], _, _ = block_range(meta, b)
        at = pl.multiple_of(b * BLOCK, BLOCK)
        rows = stack_heads(q_ref[pl.ds(at, BLOCK), :]) * jnp.asarray(scaling, BF)
        grad = stack_heads(do_ref[pl.ds(at, BLOCK), :])
        value = stack_heads(o_ref[pl.ds(at, BLOCK), :])
        delta_ref[b] = jnp.sum((grad.astype(F32) * value.astype(F32)).T, axis=0, keepdims=True)
        both_ref[b, :WIDTH] = jnp.concatenate([rows, zeros], axis=1)
        both_ref[b, WIDTH:] = jnp.concatenate([zeros, grad], axis=1)
        return carry

    lax.fori_loop(0, blocks, prepare_block, 0, unroll=4)

    def work(i, carry):
        blocks_now = [block_s[lane * share + i] for lane in range(LANES)]
        starts_now = [pl.multiple_of(key_s[lane * share + i], 128) for lane in range(LANES)]
        results = []
        for b, key_start in zip(blocks_now, starts_now):
            keys = sorted_ref[pl.ds(key_start, CHUNK), :]
            scores = dot(keys, both_ref[b, :WIDTH], NT)
            d_probs = dot(keys, both_ref[b, WIDTH:], NT)
            allowed = allowed_of(key_start, query_ref[b], start_ref[b])
            probs = jnp.where(allowed, jnp.exp(scores - lse_ref[b]), 0.0)
            d_scores = (probs * (d_probs - delta_ref[b])).astype(BF)
            joined = jnp.concatenate([d_scores, probs.astype(BF)], axis=1)
            turned = turned_ref[:HEAD_SIZE, pl.ds(key_start, CHUNK)]
            results.append((acc_ref[b] + dot(turned, d_scores), dot(joined, both_ref[b])))
        for b, key_start, (acc, d_keys) in zip(blocks_now, starts_now, results):
            acc_ref[b] = acc
            total_ref[pl.ds(key_start, CHUNK), :] += d_keys
        return carry

    lax.fori_loop(0, share, work, 0)

    def finish_block(b, carry):
        at = pl.multiple_of(b * BLOCK, BLOCK)
        result = (acc_ref[b] * scaling).T.astype(BF)
        dq_ref[pl.ds(at, BLOCK), :] = jnp.concatenate(
            [result[g * BLOCK : (g + 1) * BLOCK] for g in range(GROUP)], axis=1
        )
        return carry

    lax.fori_loop(0, blocks, finish_block, 0, unroll=4)

    def back(p, carry):
        target = pl.multiple_of(meta[p] * BLOCK, BLOCK)
        source = pl.multiple_of(p * BLOCK, BLOCK)
        dkv_ref[pl.ds(target, BLOCK), :] = total_ref[pl.ds(source, BLOCK), :].astype(BF)
        return carry

    lax.fori_loop(0, kv_ref.shape[0] // BLOCK, back, 0, unroll=8)


def local_call(kernel, outs, n_vmem, scratch, name):
    return pl.pallas_call(
        kernel,
        out_shape=outs,
        in_specs=[pl.BlockSpec(memory_space=pltpu.SMEM)] + [pl.BlockSpec(memory_space=pltpu.VMEM)] * n_vmem,
        out_specs=tuple(pl.BlockSpec(memory_space=pltpu.VMEM) for _ in outs),
        scratch_shapes=scratch,
        compiler_params=pltpu.CompilerParams(vmem_limit_bytes=40 * 2**20),
        cost_estimate=pl.CostEstimate(flops=4 * 10**9, bytes_accessed=10**7, transcendentals=4 * 10**6),
        name=name,
    )


def work_scratch(rows, keys):
    blocks = rows // BLOCK
    most = blocks * (keys // CHUNK + 1) + LANES
    return [pltpu.SMEM((most,), jnp.int32), pltpu.SMEM((most,), jnp.int32)]


def run_forward(meta, q, kv):
    rows, keys = q.shape[0], kv.shape[0]
    blocks = rows // BLOCK
    line = (blocks + 1, 1, WIDTH)
    return local_call(
        attention_forward,
        (jax.ShapeDtypeStruct((rows, WIDTH), BF), jax.ShapeDtypeStruct(line, F32)),
        2,
        [
            pltpu.VMEM((keys + CHUNK, 2 * HEAD_SIZE), BF),
            pltpu.VMEM((2 * HEAD_SIZE, keys + CHUNK), BF),
            pltpu.VMEM((blocks + 1, WIDTH, 2 * HEAD_SIZE), BF),
            pltpu.VMEM(line, jnp.int32),
            pltpu.VMEM(line, jnp.int32),
            pltpu.VMEM(line, F32),
            pltpu.VMEM(line, F32),
            pltpu.VMEM((blocks + 1, HEAD_SIZE, WIDTH), F32),
        ]
        + work_scratch(rows, keys),
        "attention_forward",
    )(meta, q, kv)


def run_backward(meta, q, kv, o, lse, d_o):
    rows, keys = q.shape[0], kv.shape[0]
    blocks = rows // BLOCK
    line = (blocks + 1, 1, WIDTH)
    return local_call(
        attention_backward,
        (jax.ShapeDtypeStruct((rows, WIDTH), BF), jax.ShapeDtypeStruct((keys, 2 * HEAD_SIZE), BF)),
        5,
        [
            pltpu.VMEM((keys + CHUNK, 2 * HEAD_SIZE), BF),
            pltpu.VMEM((2 * HEAD_SIZE, keys + CHUNK), BF),
            pltpu.VMEM((keys + CHUNK, 2 * HEAD_SIZE), F32),
            pltpu.VMEM((blocks + 1, 2 * WIDTH, 2 * HEAD_SIZE), BF),
            pltpu.VMEM(line, jnp.int32),
            pltpu.VMEM(line, jnp.int32),
            pltpu.VMEM(line, F32),
            pltpu.VMEM((blocks + 1, HEAD_SIZE, WIDTH), F32),
        ]
        + work_scratch(rows, keys),
        "attention_backward",
    )(meta, q, kv, o, lse, d_o)


def assemble_kernel(pieces_ref, qkv_ref, out_ref, rest_ref):
    parts = [pieces_ref[0, i].astype(F32) for i in range(8)]
    ends = (0, WIDTH, WIDTH + HEAD_SIZE, HEAD_COLUMNS)
    qkv_ref[...] = jnp.concatenate([t[:, a:b] for a, b in zip(ends[:-1], ends[1:]) for t in parts], axis=1)
    out_ref[...] = jnp.concatenate([t[:, 384:] for t in parts], axis=1)
    tail = parts[0]
    for t in parts[1:]:
        tail = tail + t
    rest_ref[...] = tail[:, HEAD_COLUMNS:384]


def assemble(gathered):
    _, _, piece, columns = gathered.shape

    def by_rows(n):
        return pl.BlockSpec((piece, n), lambda i: (i, 0))

    return pl.pallas_call(
        assemble_kernel,
        out_shape=(
            jax.ShapeDtypeStruct((4 * piece, 8 * HEAD_COLUMNS), F32),
            jax.ShapeDtypeStruct((4 * piece, 8 * WIDTH), F32),
            jax.ShapeDtypeStruct((4 * piece, 64), F32),
        ),
        grid=(4,),
        in_specs=[pl.BlockSpec((1, 8, piece, columns), lambda i: (i, 0, 0, 0))],
        out_specs=(by_rows(8 * HEAD_COLUMNS), by_rows(8 * WIDTH), by_rows(64)),
        compiler_params=pltpu.CompilerParams(vmem_limit_bytes=40 * 2**20),
        name="assemble",
    )(gathered)


MESH = pl.DeviceIdType.MESH
ANY = pl.BlockSpec(memory_space=pl.ANY)


class Copies:
    def __init__(self, send, recv, local):
        self.send, self.recv, self.local = send, recv, local
        self.remote_count = self.local_count = 0
        self.started, self.kept, self.left = [], [], []

    def to(self, source, target, device):
        k = self.remote_count
        self.remote_count += 1
        copy = pltpu.make_async_remote_copy(
            source, target, self.send.at[k], self.recv.at[k], device_id=device, device_id_type=MESH
        )
        copy.start()
        self.started.append(copy)
        return copy

    def keep(self, source, middle, target):
        k = self.local_count
        self.local_count += 2
        first = pltpu.make_async_copy(source, middle, self.local.at[k])
        first.start()
        self.kept.append((first, pltpu.make_async_copy(middle, target, self.local.at[k + 1])))

    def move_kept(self):
        for first, second in self.kept:
            first.wait()
            second.start()

    def sent(self, several):
        for copy in several:
            copy.wait_send()
            self.left.append(copy)

    def finish(self, arrived):
        for copy in self.started:
            if not any(copy is other for other in self.left):
                copy.wait_send()
            if not any(copy is other for other in arrived):
                copy.wait_recv()
        for _, second in self.kept:
            second.wait()


def meet(devices):
    barrier = pltpu.get_barrier_semaphore()
    for device in devices:
        pl.semaphore_signal(barrier, inc=1, device_id=device, device_id_type=MESH)
    pl.semaphore_wait(barrier, len(devices))


def gather_rows_kernel(
    tok_ref, wp_ref, gain_ref, wo_ref, tok_out, wp_out, gain_out, wo_out, v_tok, v_wp, v_gain, v_wo, send, recv, local
):
    place, stream = turned(lax.axis_index("ctx")), lax.axis_index("wsh")
    x, z = place % 4, (place // 4) % 2
    right, left = {"ctx": turned(place - x + (x + 1) % 4)}, {"ctx": turned(place - x + (x + 3) % 4)}
    across = place + 4 - 8 * z
    other = {"wsh": stream + 1 - 2 * (stream % 2)}
    far = {"ctx": turned(across), "wsh": (stream + 2) % 4}
    meet([right, left, {"ctx": turned(across)}, other, far])
    copies = Copies(send, recv, local)
    half = tok_ref.shape[0] // 2
    own, own_z = z * 4 + x, (1 - z) * 4 + x
    left_id, right_id = z * 4 + (x + 3) % 4, z * 4 + (x + 1) % 4
    left_z, right_z = (1 - z) * 4 + (x + 3) % 4, (1 - z) * 4 + (x + 1) % 4

    def rows(ref, h):
        return ref.at[pl.ds(h * half, half)]

    def spot(block, h):
        return tok_out.at[block, pl.ds(h * half, half)]

    head = place % 8
    far_wp = copies.to(wp_ref.at[across % 8], wp_out.at[stream], far)
    far_gain = copies.to(gain_ref, gain_out.at[stream], far)
    cross = [copies.to(rows(tok_ref, h), spot(own, h), {"ctx": turned(across)}) for h in range(2)]
    to_right = [copies.to(rows(tok_ref, h), spot(own, h), right) for h in (0, 1)]
    to_left = [copies.to(rows(tok_ref, h), spot(own, h), left) for h in (1, 0)]
    copies.to(wp_ref.at[head], wp_out.at[stream], other)
    copies.to(gain_ref, gain_out.at[stream], other)
    third = wo_ref.shape[0] // 3
    parts = [pl.ds(i * third, third) for i in range(3)]
    far_wo = [copies.to(wo_ref.at[p], wo_out.at[stream, p], far) for p in parts]
    copies.to(wo_ref, wo_out.at[stream], other)
    copies.keep(tok_ref, v_tok, tok_out.at[own])
    copies.keep(wp_ref.at[head], v_wp, wp_out.at[stream])
    copies.keep(gain_ref, v_gain, gain_out.at[stream])
    copies.keep(wo_ref, v_wo, wo_out.at[stream])
    copies.move_kept()

    arrived = []

    def arrive(copy):
        copy.wait_recv()
        arrived.append(copy)

    far_stream = (stream + 2) % 4
    arrive(far_wp)
    copies.to(wp_out.at[far_stream], wp_out.at[far_stream], other)
    arrive(far_gain)
    copies.to(gain_out.at[far_stream], gain_out.at[far_stream], other)
    arrive(to_right[0])
    copies.to(spot(left_id, 0), spot(left_id, 0), right)
    arrive(to_left[0])
    copies.to(spot(right_id, 1), spot(right_id, 1), left)
    arrive(cross[0])
    arrive(cross[1])
    z_right = [copies.to(spot(own_z, h), spot(own_z, h), right) for h in (0, 1)]
    z_left = [copies.to(spot(own_z, h), spot(own_z, h), left) for h in (1, 0)]
    arrive(z_right[0])
    copies.to(spot(left_z, 0), spot(left_z, 0), right)
    arrive(z_left[0])
    copies.to(spot(right_z, 1), spot(right_z, 1), left)
    for p, copy in zip(parts, far_wo):
        arrive(copy)
        copies.to(wo_out.at[far_stream, p], wo_out.at[far_stream, p], other)
    copies.finish(arrived)


def gather_rows(tok, wp, gain, wo):
    return pl.pallas_call(
        gather_rows_kernel,
        out_shape=(
            jax.ShapeDtypeStruct((8,) + tok.shape, BF),
            jax.ShapeDtypeStruct((4,) + wp.shape[1:], BF),
            jax.ShapeDtypeStruct((4,) + gain.shape, BF),
            jax.ShapeDtypeStruct((4,) + wo.shape, BF),
        ),
        in_specs=[ANY] * 4,
        out_specs=(ANY,) * 4,
        scratch_shapes=[
            pltpu.VMEM(tok.shape, BF),
            pltpu.VMEM(wp.shape[1:], BF),
            pltpu.VMEM(gain.shape, BF),
            pltpu.VMEM(wo.shape, BF),
            pltpu.SemaphoreType.DMA((27,)),
            pltpu.SemaphoreType.DMA((27,)),
            pltpu.SemaphoreType.DMA((8,)),
        ],
        compiler_params=pltpu.CompilerParams(collective_id=1, has_side_effects=True, vmem_limit_bytes=40 * 2**20),
        name="gather_rows",
    )(tok, wp, gain, wo)


def gather_keys_kernel(kv_ref, kv_out, v_kv, send, recv, local):
    place = turned(lax.axis_index("ctx"))
    y = place // 8
    up, down = {"ctx": turned((place + 8) % 32)}, {"ctx": turned((place + 24) % 32)}
    meet([up, down])
    copies = Copies(send, recv, local)
    half = kv_ref.shape[0] // 2

    def rows(h):
        return kv_ref.at[pl.ds(h * half, half)]

    def spot(block, h):
        return kv_out.at[block, pl.ds(h * half, half)]

    to_up = [copies.to(rows(h), spot(y, h), up) for h in (0, 1)]
    to_down = [copies.to(rows(h), spot(y, h), down) for h in (1, 0)]
    copies.keep(kv_ref, v_kv, kv_out.at[y])
    copies.move_kept()
    to_up[0].wait_recv()
    copies.to(spot((y + 3) % 4, 0), spot((y + 3) % 4, 0), up)
    to_down[0].wait_recv()
    copies.to(spot((y + 1) % 4, 1), spot((y + 1) % 4, 1), down)
    copies.finish([to_up[0], to_down[0]])


def gather_keys(kv):
    return pl.pallas_call(
        gather_keys_kernel,
        out_shape=jax.ShapeDtypeStruct((4,) + kv.shape, BF),
        in_specs=[ANY],
        out_specs=ANY,
        scratch_shapes=[
            pltpu.VMEM(kv.shape, BF),
            pltpu.SemaphoreType.DMA((6,)),
            pltpu.SemaphoreType.DMA((6,)),
            pltpu.SemaphoreType.DMA((2,)),
        ],
        compiler_params=pltpu.CompilerParams(collective_id=2, has_side_effects=True, vmem_limit_bytes=40 * 2**20),
        name="gather_keys",
    )(kv)


FF_STEP = 256


def middle_kernel(
    attn_ref, x_ref, cot_ref, wo_ref, head_ref, gain_ref, choice_ref, slot_ref, slot_t_ref, w_ref,
    out_ref, d_mid_ref, small_ref, d_attn_to, branch_to, half_out, side_out,
    attn_v, wo_v, w_v, x_v, g_v, turned_x, turned_g, out_v, d_in_v, back_v, returned_v, acc_v, gate_v, up_v,
    hidden_v, d_gate_v, d_up_v, got_v, half_got, side_got, mid_v, act_v, d_attn_v, branch_v, send, recv, local,
):
    index, stream = lax.axis_index("ctx"), lax.axis_index("wsh")
    place, mine = turned(index), index // 2
    y, r = place // 8, place % 8
    inner = (index % 4 + 1) // 2 % 2

    def device(p):
        return {"ctx": p // 2 * 4 + (1 - inner) * (3 * (p % 2)) + inner * (1 + p % 2)}

    peers = [(mine + k) % 16 for k in range(1, 16)]
    in_row = [(r + k) % 8 for k in range(1, 8)]
    core, half, side = stream % 2, index % 2, stream // 2
    other = {"wsh": stream + 1 - 2 * core}
    other_half, other_side = {"ctx": index + 1 - 2 * half}, {"wsh": (stream + 2) % 4}
    meet([device(p) for p in peers] + [other, other_half, other_side])
    copies = Copies(send, recv, local)
    width, rows = turned_x.shape
    tokens = x_ref.shape[0]
    quarter = width // 4
    own, arrived = [], []

    def here(source, target):
        copy = pltpu.make_async_copy(source, target, local.at[len(own)])
        copy.start()
        own.append(copy)
        return copy

    def arrive(several):
        for copy in several:
            copy.wait_recv()
            arrived.append(copy)

    attn_came = [copies.to(attn_ref.at[pr], attn_v.at[r], {"ctx": turned(8 * y + pr)}) for pr in in_row]
    own_attn = here(attn_ref.at[r], attn_v.at[r])
    own_wo = here(wo_ref, wo_v)
    weights = [
        here(w_ref.at[4 * k + q, m], w_v.at[k, m, pl.ds(q * quarter, quarter)])
        for k in range(2)
        for q in range(4)
        for m in range(3)
    ]
    lanes = lax.broadcasted_iota(jnp.int32, (tokens, 64), 1)
    chosen = [choice_ref[:, j : j + 1] == lanes for j in range(TOP)]
    slot_rows = lax.broadcasted_iota(jnp.int32, (rows, tokens), 0)
    to_slot = [jnp.where(slot_t_ref[j : j + 1, :] == slot_rows, 1.0, 0.0).astype(BF) for j in range(TOP)]
    own_attn.wait()
    own_wo.wait()
    arrive(attn_came)
    middle = x_ref[...].astype(F32)
    for i in range(4):
        pair = jnp.concatenate([attn_v[2 * i], attn_v[2 * i + 1]], axis=1)
        middle += dot(pair, wo_v[i * quarter : (i + 1) * quarter, :])
    mid_v[...] = middle
    scale = rms_scale(middle)
    act = (middle * scale * gain_ref[...]).astype(BF)
    act_v[...] = act
    out_v[...] = dot(to_slot[0] + to_slot[1], act).astype(BF).reshape(out_v.shape)
    came = [copies.to(out_v.at[p], x_v.at[mine], device(p)) for p in peers]
    own_x = here(out_v.at[mine], x_v.at[mine])
    logits = dot(act, head_ref[:, HEAD_COLUMNS:])
    picked = [jnp.sum(jnp.where(c, logits, 0.0), axis=-1, keepdims=True) for c in chosen]
    top = jnp.maximum(picked[0], picked[1])
    powers = [jnp.exp(p - top) for p in picked]
    gates = [p / (powers[0] + powers[1]) for p in powers]
    gated = jnp.concatenate([(g * cot_ref[...].astype(F32)).astype(BF) for g in gates], axis=0)
    d_in_v[...] = dot(jnp.concatenate(to_slot, axis=1), gated).astype(BF).reshape(d_in_v.shape)
    came_g = [copies.to(d_in_v.at[p], g_v.at[mine], device(p)) for p in peers]
    own_g = here(d_in_v.at[mine], g_v.at[mine])

    for copy in weights:
        copy.wait()
    arrive(came)
    own_x.wait()
    steps = w_v.shape[3] // FF_STEP
    acc_v[...] = jnp.zeros_like(acc_v)

    def forward(i, carry):
        k, at = i // steps, pl.ds(pl.multiple_of(i % steps * FF_STEP, FF_STEP), FF_STEP)
        inputs = x_v[...].reshape(rows, width)
        gate = dot(inputs, w_v[k, 0, :, at])
        up = dot(inputs, w_v[k, 1, :, at])
        hidden = (gate * jax.nn.sigmoid(gate) * up).astype(BF)
        gate_v[i] = gate
        up_v[i] = up
        hidden_v[k, :, at] = hidden
        acc_v[...] += dot(hidden, w_v[k, 2, :, at], NT)
        return carry

    lax.fori_loop(0, 2 * steps, forward, 0)
    copies.sent(came)
    out_v[...] = acc_v[...].astype(BF).reshape(out_v.shape)
    outs = [copies.to(out_v.at[p], back_v.at[mine], device(p)) for p in peers]
    own_back = here(out_v.at[mine], back_v.at[mine])
    for q in range(4):
        at = slice(q * quarter, (q + 1) * quarter)
        turned_x[at, :] = x_v[:, :, at].reshape(rows, quarter).T
    acc_v[...] = jnp.zeros_like(acc_v)
    arrive(came_g)
    own_g.wait()

    def backward(i, carry):
        k, at = i // steps, pl.ds(pl.multiple_of(i % steps * FF_STEP, FF_STEP), FF_STEP)
        d_hidden = dot(g_v[...].reshape(rows, width), w_v[k, 2, :, at])
        gate, up = gate_v[i], up_v[i]
        sigmoid = jax.nn.sigmoid(gate)
        d_gate = (d_hidden * up * sigmoid * (1.0 + gate * (1.0 - sigmoid))).astype(BF)
        d_up = (d_hidden * (gate * sigmoid)).astype(BF)
        d_gate_v[k, :, at] = d_gate
        d_up_v[k, :, at] = d_up
        acc_v[...] += dot(d_gate, w_v[k, 0, :, at], NT) + dot(d_up, w_v[k, 1, :, at], NT)
        return carry

    lax.fori_loop(0, 2 * steps, backward, 0)
    copies.sent(came_g)
    d_in_v[...] = acc_v[...].astype(BF).reshape(d_in_v.shape)
    returns = [copies.to(d_in_v.at[p], returned_v.at[mine], device(p)) for p in peers]
    own_returned = here(d_in_v.at[mine], returned_v.at[mine])
    for q in range(4):
        at = slice(q * quarter, (q + 1) * quarter)
        turned_g[at, :] = g_v[:, :, at].reshape(rows, quarter).T

    def terms(k, z, c):
        at = pl.ds(pl.multiple_of((2 * z + c) * quarter, quarter), quarter)
        part = turned_x[at, :]
        return (
            dot(part, d_gate_v[k]),
            dot(part, d_up_v[k]),
            dot(turned_g[at, :], hidden_v[k]),
        )

    crossing = []
    for dz in (1, 0):
        z = side + dz - 2 * side * dz

        def other_term(k, carry, z=z, dz=dz):
            at = pl.ds(pl.multiple_of((2 * dz + k) * quarter, quarter), quarter)
            for m, term in enumerate(terms(k, z, 1 - core)):
                w_v[0, m, at] = term.astype(BF)
            return carry

        lax.fori_loop(0, 2, other_term, 0)
        at = pl.ds(2 * dz * quarter, 2 * quarter)
        crossing.append(copies.to(w_v.at[0, :, at], got_v.at[:, at], other))
    halfway = quarter // 2
    for dz, copy in zip((1, 0), crossing):
        z = side + dz - 2 * side * dz
        arrive([copy])
        for dk in (1, 0):
            k = half + dk - 2 * half * dk
            got_at = pl.ds(pl.multiple_of((2 * dz + k) * quarter, quarter), quarter)
            z_at = pl.ds(pl.multiple_of(z * halfway, halfway), halfway)
            k_at = pl.ds(pl.multiple_of(quarter + k * halfway, halfway), halfway)
            for m, term in enumerate(terms(k, z, core)):
                total = (term + got_v[m, got_at].astype(F32)).astype(BF)
                if dk:
                    w_v[1, m, z_at] = total[:halfway]
                else:
                    half_out[m, z] = total[:halfway]
                if dz:
                    w_v[1, m, k_at] = total[halfway:]
                else:
                    side_out[m, k] = total[halfway:]
    first = copies.to(w_v.at[1, :, pl.ds(0, quarter)], half_got, other_half)
    second = copies.to(w_v.at[1, :, pl.ds(quarter, quarter)], side_got, other_side)

    slot_lanes = lax.broadcasted_iota(jnp.int32, (tokens, rows), 1)
    of_slot = [jnp.where(slot_ref[:, j : j + 1] == slot_lanes, 1.0, 0.0).astype(BF) for j in range(TOP)]
    own_back.wait()
    arrive(outs)
    back = back_v[...].reshape(rows, width)
    d_out = cot_ref[...].astype(F32)
    total = mid_v[...]
    d_gates = []
    for j in range(TOP):
        both = dot(of_slot[j], back)
        total += gates[j] * both
        d_gates.append(jnp.sum(d_out * both, axis=-1, keepdims=True))
    out_ref[...] = total.astype(BF)
    inner_sum = gates[0] * d_gates[0] + gates[1] * d_gates[1]
    d_logits = 0.0
    for j in range(TOP):
        d_logits += jnp.where(chosen[j], gates[j] * (d_gates[j] - inner_sum), 0.0)
    d_logits = d_logits.astype(BF)
    own_returned.wait()
    arrive(returns)
    d_act = dot(of_slot[0] + of_slot[1], returned_v[...].reshape(rows, width))
    d_act += dot(d_logits, head_ref[:, HEAD_COLUMNS:], NT)
    middle = mid_v[...]
    normed = middle * scale
    spot = jnp.where(lanes == 16, 1.0, 0.0).astype(BF)
    small_ref[...] = (dot(act_v[...].T, d_logits) + dot((d_act * normed).astype(BF).T, spot)).astype(BF)
    scaled = d_act * gain_ref[...]
    d_mid = d_out + scale * (scaled - normed * scale * jnp.mean(scaled * middle, axis=-1, keepdims=True))
    d_mid_ref[...] = d_mid
    d_branch = d_mid.astype(BF)
    for i in range(8):
        branch_v[i] = d_branch[:, i * WIDTH : (i + 1) * WIDTH]
    to_row = [copies.to(branch_v.at[pr], branch_to.at[r], {"ctx": turned(8 * y + pr)}) for pr in in_row]
    for i in range(4):
        pair = dot(d_branch, wo_v[i * quarter : (i + 1) * quarter, :], NT).astype(BF)
        d_attn_v[2 * i] = pair[:, :WIDTH]
        d_attn_v[2 * i + 1] = pair[:, WIDTH:]
    to_row += [copies.to(d_attn_v.at[pr], d_attn_to.at[r], {"ctx": turned(8 * y + pr)}) for pr in in_row]
    own_row = [here(branch_v.at[r], branch_to.at[r]), here(d_attn_v.at[r], d_attn_to.at[r])]
    arrive([first, second])
    for m in range(3):
        for i in range(2):
            at = slice(i * halfway, (i + 1) * halfway)
            half_out[m, i] = (half_out[m, i].astype(F32) + half_got[m, at].astype(F32)).astype(BF)
            side_out[m, i] = (side_out[m, i].astype(F32) + side_got[m, at].astype(F32)).astype(BF)
    copies.finish(arrived)
    own_back = own_row
    for copy in own_back:
        copy.wait()


def run_middle(attn, x, cotangent, w_out, head_full, gain, choice, slots, weights):
    _, tokens, _ = attn.shape
    width = x.shape[1]
    groups, capacity = 16, 2 * TOP * tokens // 16
    rows, half, quarter = groups * capacity, weights.shape[3], width // 4
    steps = 2 * half // FF_STEP
    vmem = pltpu.VMEM
    whole = pl.BlockSpec(memory_space=pltpu.VMEM)
    slot_rows = vmem((groups, capacity, width), BF)
    wide, low = vmem((steps, rows, FF_STEP), F32), vmem((2, rows, half), BF)
    part = jax.ShapeDtypeStruct((3, 2, quarter // 2, half), BF)
    return pl.pallas_call(
        middle_kernel,
        out_shape=(
            jax.ShapeDtypeStruct(x.shape, BF),
            jax.ShapeDtypeStruct(x.shape, F32),
            jax.ShapeDtypeStruct((width, 64), BF),
            jax.ShapeDtypeStruct(attn.shape, BF),
            jax.ShapeDtypeStruct(attn.shape, BF),
            part,
            part,
        ),
        in_specs=[ANY, whole, whole, ANY, whole, whole, whole, whole, whole, ANY],
        out_specs=(whole, whole, whole, ANY, ANY, whole, whole),
        scratch_shapes=[
            vmem(attn.shape, BF),
            vmem(w_out.shape, BF),
            vmem((2, 3, width, half), BF),
            slot_rows,
            slot_rows,
            vmem((width, rows), BF),
            vmem((width, rows), BF),
            slot_rows,
            slot_rows,
            slot_rows,
            slot_rows,
            vmem((rows, width), F32),
            wide,
            wide,
            low,
            low,
            low,
            vmem((3, width, half), BF),
            vmem((3, quarter, half), BF),
            vmem((3, quarter, half), BF),
            vmem(x.shape, F32),
            vmem(x.shape, BF),
            vmem(attn.shape, BF),
            vmem(attn.shape, BF),
            pltpu.SemaphoreType.DMA((85,)),
            pltpu.SemaphoreType.DMA((85,)),
            pltpu.SemaphoreType.DMA((32,)),
        ],
        compiler_params=pltpu.CompilerParams(collective_id=6, has_side_effects=True, vmem_limit_bytes=60 * 2**20),
        cost_estimate=pl.CostEstimate(flops=15 * 10**9, bytes_accessed=10**8, transcendentals=10**6),
        name="middle",
    )(attn, x, cotangent, w_out, head_full, gain.reshape(1, width), choice, slots, slots.T, weights)


def prepare_kernel(qkv_ref, router_ref, wo_ref, wp_out, wo_out):
    rows = qkv_ref.shape[0]
    experts = router_ref.shape[1]
    wo_out[...] = wo_ref[...].astype(BF)
    router = router_ref[...].astype(BF)
    tail = jnp.zeros((rows, wp_out.shape[2] - HEAD_COLUMNS - experts), BF)
    k_at, v_at = QUERY_HEADS * HEAD_SIZE, (QUERY_HEADS + KEY_VALUE_HEADS) * HEAD_SIZE
    for h in range(KEY_VALUE_HEADS):
        wp_out[h] = jnp.concatenate(
            [
                qkv_ref[:, h * WIDTH : (h + 1) * WIDTH].astype(BF),
                qkv_ref[:, k_at + h * HEAD_SIZE : k_at + (h + 1) * HEAD_SIZE].astype(BF),
                qkv_ref[:, v_at + h * HEAD_SIZE : v_at + (h + 1) * HEAD_SIZE].astype(BF),
                router,
                tail,
            ],
            axis=1,
        )


def prepare(w_qkv, w_router, w_out):
    shard = w_qkv.shape[0]
    step = shard // 3

    def block(n):
        return pl.BlockSpec((step, n), lambda i: (i, 0))

    return pl.pallas_call(
        prepare_kernel,
        out_shape=(
            jax.ShapeDtypeStruct((KEY_VALUE_HEADS, shard, 384), BF),
            jax.ShapeDtypeStruct(w_out.shape, BF),
        ),
        grid=(3,),
        in_specs=[block(w_qkv.shape[1]), block(w_router.shape[1]), block(w_out.shape[1])],
        out_specs=(
            pl.BlockSpec((KEY_VALUE_HEADS, step, 384), lambda i: (0, i, 0)),
            block(w_out.shape[1]),
        ),
        compiler_params=pltpu.CompilerParams(vmem_limit_bytes=40 * 2**20),
        name="prepare",
    )(w_qkv, w_router, w_out)


def finish_kernel(
    dq_ref, kv_ref, act_ref, small_ref, attn_ref, branch_ref, p0, p1, p2, p3, x_ref, d_mid_ref, gain_ref,
    d_tokens_ref, all_out, kv_v, grad_v, grad_to, term_v, term_to, out_v, out_to, attn_v, act_t, own_v, w_v, acc_v,
    send, recv, local,
):
    place, stream = turned(lax.axis_index("ctx")), lax.axis_index("wsh")
    y, r = place // 8, place % 8
    x, z = r % 4, r // 4

    def at_place(p):
        return {"ctx": turned(p)}

    right, left = at_place(place - x + (x + 1) % 4), at_place(place - x + (x + 3) % 4)
    across = at_place(place + 4 - 8 * z)
    up, down, beyond = (at_place((place + 8 * k) % 32) for k in (1, 3, 2))
    others = [((y + k // 4) % 4, (stream + k % 4) % 4) for k in range(1, 16)]
    in_row = [(r + k) % 8 for k in range(1, 8)]
    meet([{"ctx": turned(r + 8 * py), "wsh": pw} for py, pw in others] + [at_place(8 * y + pr) for pr in in_row])
    copies = Copies(send, recv, local)
    rows, width = act_ref.shape
    shard, piece = width // 4, own_v.shape[0]
    arrived = []

    def arrive(*which):
        for copy in which:
            copy.wait_recv()
            arrived.append(copy)

    own = []

    def here(source, target):
        copy = pltpu.make_async_copy(source, target, local.at[len(own)])
        copy.start()
        own.append(copy)
        return copy

    kv_came = [
        copies.to(kv_ref.at[(y + k) % 4], kv_v.at[y], at_place((place + 8 * k) % 32)) for k in (2, 1, 3)
    ]
    own_kv = here(kv_ref.at[y], kv_v.at[y])
    r_z = (1 - z) * 4 + x
    r_left, r_right = z * 4 + (x + 3) % 4, z * 4 + (x + 1) % 4
    z_left, z_right = (1 - z) * 4 + (x + 3) % 4, (1 - z) * 4 + (x + 1) % 4
    front, rear = pl.ds(0, 4), pl.ds(4, 4)

    def pass_on(device, *at):
        return copies.to(attn_v.at[at], attn_v.at[at], device)

    attn_cross = copies.to(attn_ref, attn_v.at[r], across)
    attn_right = copies.to(attn_ref, attn_v.at[r], right)
    attn_left = copies.to(attn_ref, attn_v.at[r], left)
    own_attn = here(attn_ref, attn_v.at[r])
    weights = [here(p, w_v.at[j]) for j, p in enumerate((p0, p1, p2, p3))]
    dq = dq_ref[...]
    for q in range(4):
        act_t[q * shard : (q + 1) * shard, :] = act_ref[:, q * shard : (q + 1) * shard].T
    for q in range(4):
        term = dot(act_t[q * shard : (q + 1) * shard, :], dq).astype(BF)
        for i in range(4):
            term_v[i, q, :, :WIDTH] = term[i * piece : (i + 1) * piece]
            at = q * shard + i * piece
            term_v[i, q, :, HEAD_COLUMNS:] = small_ref[at : at + piece, :]
    arrive(attn_cross)
    attn_far = [pass_on(right, r_z), pass_on(left, r_z)]
    arrive(attn_right)
    attn_on = [pass_on(right, r_left, front)]
    arrive(attn_left)
    attn_on.append(pass_on(left, r_right, rear))
    own_kv.wait()
    arrive(*kv_came)
    total = kv_v[0].astype(F32)
    for i in range(1, 4):
        total = total + kv_v[i].astype(F32)
    kv = total.astype(BF)
    grad_v[...] = jnp.concatenate([dq, kv, jnp.zeros((rows, 64), BF)], axis=1).reshape(grad_v.shape)
    grads = [copies.to(grad_v.at[pr], grad_to.at[r], at_place(8 * y + pr)) for pr in in_row]
    own_grad = here(grad_v.at[r], grad_to.at[r])
    terms = []
    for dw in (2, 3, 1, 0):
        pw = (stream + dw) % 4
        part = act_t[pl.ds(pl.multiple_of(pw * shard, shard), shard), :]
        term = dot(part, kv).astype(BF)
        for i in range(4):
            term_v[i, pw, :, WIDTH:HEAD_COLUMNS] = term[i * piece : (i + 1) * piece]
        for dy in (2, 1, 3, 0):
            py = (y + dy) % 4
            if dw or dy:
                device = {"ctx": turned(r + 8 * py), "wsh": pw}
                terms.append(copies.to(term_v.at[py, pw], term_to.at[y, stream], device))
    own_term = here(term_v.at[y, stream], term_to.at[y, stream])
    arrive(attn_far[0])
    attn_on.append(pass_on(right, z_left, front))
    arrive(attn_far[1])
    attn_on.append(pass_on(left, z_right, rear))
    own_attn.wait()
    arrive(*attn_on)
    branch = branch_ref[...]
    for h in range(8):
        term = dot(attn_v[h].reshape(rows, WIDTH).T, branch).astype(BF)
        for i in range(2):
            n = 2 * h + i
            out_v[n % 4, n // 4] = term[i * piece : (i + 1) * piece]
    outs = []
    for k in (8, 4, 12, 10, 6, 14, 2, 9, 5, 13, 1, 11, 7, 15, 3):
        py, pw = others[k - 1]
        outs.append(copies.to(out_v.at[py, pw], out_to.at[y, stream], {"ctx": turned(r + 8 * py), "wsh": pw}))
    own_out = here(out_v.at[y, stream], out_to.at[y, stream])
    own_term.wait()
    arrive(*terms)
    total = term_to[0, 0].astype(F32)
    for i in range(1, 16):
        total = total + term_to[i // 4, i % 4].astype(F32)
    own_v[:, :384] = total.astype(BF)
    own_out.wait()
    arrive(*outs)
    total = out_to[0, 0].astype(F32)
    for i in range(1, 16):
        total = total + out_to[i // 4, i % 4].astype(F32)
    own_v[:, 384:] = total.astype(BF)

    half = piece // 2
    first, last = pl.ds(0, half), pl.ds(half, half)

    def on(device, *at):
        return copies.to(all_out.at[at], all_out.at[at], device)

    a_cross = copies.to(own_v.at[first], all_out.at[y, r, first], across)
    a_right = copies.to(own_v.at[first], all_out.at[y, r, first], right)
    a_left = copies.to(own_v.at[first], all_out.at[y, r, first], left)
    b_up = copies.to(own_v.at[last], all_out.at[y, r, last], up)
    b_down = copies.to(own_v.at[last], all_out.at[y, r, last], down)
    b_beyond = copies.to(own_v.at[last], all_out.at[y, r, last], beyond)
    keep = here(own_v, all_out.at[y, r])

    for copy in weights:
        copy.wait()
    own_grad.wait()
    arrive(*grads)
    acc_v[...] = jnp.zeros_like(acc_v)
    shards = (stream, stream + 1 - 2 * (stream % 2), (stream + 2) % 4, 3 - stream)

    def heads(start, count):
        def one(h, carry):
            grad = grad_to[h][:, :HEAD_COLUMNS]
            for j in range(4):
                acc_v[shards[j]] += dot(grad, w_v[j, h][:, :HEAD_COLUMNS], NT)
            return carry

        lax.fori_loop(start, start + count, one, 0)

    heads(0, 2)
    keep.wait()
    arrive(a_cross)
    a_z_right = on(right, y, r_z, first)
    a_z_left = on(left, y, r_z, first)
    arrive(a_right)
    a_on = on(right, y, r_left, first)
    arrive(b_up, b_down, b_beyond)
    lower, upper, every = pl.ds(0, 2), pl.ds(2, 2), pl.ds(0, 4)
    b_right = on(right, every, r, last)
    b_left = on(left, every, r, last)
    b_cross = on(across, every, r, last)
    heads(2, 2)
    arrive(a_z_left, a_left)
    a_z_on = on(left, y, z_right, first)
    arrive(a_z_right, a_on, a_z_on)
    low_r, high_r = pl.ds(0, 4), pl.ds(4, 4)
    c_up = [on(up, y, low_r, first), on(up, y, high_r, first)]
    c_down = [on(down, y, high_r, first), on(down, y, low_r, first)]
    heads(4, 2)
    arrive(b_right)
    on(right, lower, r_left, last)
    arrive(b_left)
    on(left, upper, r_right, last)
    arrive(b_cross)
    b_z_right = on(right, every, r_z, last)
    b_z_left = on(left, every, r_z, last)
    arrive(c_up[0])
    on(up, (y + 3) % 4, low_r, first)
    arrive(c_down[0])
    on(down, (y + 1) % 4, high_r, first)
    heads(6, 2)
    arrive(b_z_right)
    on(right, lower, z_left, last)
    arrive(b_z_left)
    on(left, upper, z_right, last)
    values = x_ref[...].astype(F32)
    scale = rms_scale(values)
    inner = 0.0
    for q in range(4):
        at = slice(q * shard, (q + 1) * shard)
        inner += jnp.sum(acc_v[q] * gain_ref[:, at] * values[:, at], axis=-1, keepdims=True)
    inner = inner * (1.0 / width)
    for q in range(4):
        at = slice(q * shard, (q + 1) * shard)
        d_tokens_ref[:, at] = (
            d_mid_ref[:, at] + scale * (acc_v[q] * gain_ref[:, at]) - values[:, at] * scale**3 * inner
        ).astype(BF)
    copies.finish(arrived)


def finish(dq, kv, act, small, attn, branch, pieces, x, d_middle, gain):
    rows, width = act.shape
    piece = width // 16
    vmem = pl.BlockSpec(memory_space=pltpu.VMEM)
    scratch = pltpu.VMEM
    return pl.pallas_call(
        finish_kernel,
        out_shape=(
            jax.ShapeDtypeStruct(x.shape, BF),
            jax.ShapeDtypeStruct((4, 8, piece, 384 + WIDTH), BF),
        ),
        in_specs=[vmem, ANY, vmem, vmem, ANY, vmem] + [ANY] * 4 + [vmem] * 3,
        out_specs=(vmem, ANY),
        scratch_shapes=[
            scratch(kv.shape, BF),
            scratch((8, rows // 8, 384), BF),
            scratch((8, rows // 8, 384), BF),
            scratch((4, 4, piece, 384), BF),
            scratch((4, 4, piece, 384), BF),
            scratch((4, 4, piece, WIDTH), BF),
            scratch((4, 4, piece, WIDTH), BF),
            scratch((8,) + attn.shape, BF),
            scratch((width, rows), BF),
            scratch((piece, 384 + WIDTH), BF),
            scratch((4,) + pieces[0].shape, BF),
            scratch((4, rows // 8, width // 4), F32),
            pltpu.SemaphoreType.DMA((74,)),
            pltpu.SemaphoreType.DMA((74,)),
            pltpu.SemaphoreType.DMA((10,)),
        ],
        compiler_params=pltpu.CompilerParams(collective_id=3, has_side_effects=True, vmem_limit_bytes=52 * 2**20),
        cost_estimate=pl.CostEstimate(flops=3 * 10**9, bytes_accessed=10**8, transcendentals=0),
        name="finish",
    )(dq, kv, act, small, attn, branch, *pieces, x, d_middle, gain.reshape(1, width))


def swap(x, groups, axis="ctx"):
    return lax.all_to_all(x, axis, 0, 0, axis_index_groups=groups, tiled=True)


def rms_scale(values):
    return lax.rsqrt(jnp.mean(values * values, axis=-1, keepdims=True) + EPSILON)


def body(
    tokens,
    lengths,
    deal,
    expert_ids,
    gain_attn,
    w_qkv,
    w_out,
    gain_moe,
    w_router,
    w_gate,
    w_up,
    w_down,
    cotangent,
):
    stream = lax.axis_index("wsh")
    index = lax.axis_index("ctx")
    place = turned(index)
    rows, width = tokens.shape[1], tokens.shape[2]
    shard = w_qkv.shape[0]
    experts_count = w_router.shape[1]
    capacity = 2 * rows * TOP // experts_count
    head = place % 8
    head_row = place // 8
    lengths_row = lax.dynamic_index_in_dim(lengths, stream, 0, keepdims=False)
    deal_row = lax.dynamic_index_in_dim(deal, stream, 0, keepdims=False)
    blocks = deal_row.shape[0]
    deal_row = deal_row.reshape(4, 2, 4, 2).transpose(2, 1, 0, 3).reshape(blocks)
    block_ids = jnp.arange(blocks, dtype=jnp.int32)
    inverse = jnp.sum(jnp.where(deal_row[None, :] == block_ids[:, None], block_ids[None, :], 0), axis=1)
    own_blocks = lax.dynamic_slice_in_dim(deal_row, head_row * 16, 16)
    meta = jnp.concatenate([inverse, own_blocks, jnp.cumsum(lengths_row)]).astype(jnp.int32)

    q_columns = QUERY_HEADS * HEAD_SIZE
    by_head, own_out = prepare(w_qkv, w_router, w_out)
    own_gains = jnp.concatenate(
        [gain_attn.astype(BF)[None], gain_moe.astype(BF)[None], jnp.zeros((14, shard), BF)], axis=0
    )
    group_tokens, head_full, gains, full_out = gather_rows(tokens[0], by_head, own_gains, own_out)
    head_full = head_full.reshape(width, -1)
    head_weight = head_full[:, :HEAD_COLUMNS]
    full_router = head_full[:, HEAD_COLUMNS : HEAD_COLUMNS + experts_count]
    gain_first = gains[:, 0].reshape(width).astype(F32)
    gain_second = gains[:, 1].reshape(width).astype(F32)
    full_out = full_out.reshape(q_columns, width)

    w_gate, w_up, w_down, _ = lax.optimization_barrier((w_gate, w_up, w_down, gains))
    expert_shard = jnp.stack([w_gate[0].astype(BF), w_up[0].astype(BF), w_down[0].T.astype(BF)])
    expert_all = lax.all_gather(expert_shard, ("ctx", "wsh"), axis_index_groups=OWNERS)

    group_x = group_tokens.reshape(8 * rows, width).astype(F32)
    group_act = (group_x * rms_scale(group_x) * gain_first).astype(BF)
    head_qkv = dot(group_act, head_weight).astype(BF)
    kv_all = gather_keys(head_qkv[:, WIDTH:]).reshape(32 * rows, 2 * HEAD_SIZE)
    head_q = head_qkv[:, :WIDTH]
    head_attn, lse = run_forward(meta, head_q, kv_all)
    by_head, head_attn = lax.optimization_barrier((by_head, head_attn))
    far_qkv = lax.ppermute(by_head, ("ctx", "wsh"), NEXT_Z)
    near_qkv = lax.ppermute(by_head, "wsh", OTHER_CORE)
    head_blocks = head_attn.reshape(8, rows, WIDTH)
    flat_ids = expert_ids[0].reshape(-1)
    expert_range = jnp.arange(experts_count, dtype=jnp.int32)
    assign_hot = (flat_ids[:, None] == expert_range[None, :]).astype(jnp.int32)
    ranks = jnp.sum((jnp.cumsum(assign_hot, axis=0) - 1) * assign_hot, axis=1)
    slots = (flat_ids * capacity + ranks).reshape(rows, TOP)
    output_rows, d_middle, small_term, head_d_attn, branch_part, half_sum, side_sum = run_middle(
        head_blocks, tokens[0], cotangent[0], full_out, head_full, gain_second, expert_ids[0], slots, expert_all
    )
    head_d_attn = head_d_attn.reshape(8 * rows, WIDTH)
    head_d_attn, far_qkv, near_qkv = lax.optimization_barrier((head_d_attn, far_qkv, near_qkv))
    qkv_pieces = [by_head, near_qkv, far_qkv, lax.ppermute(far_qkv, "wsh", OTHER_CORE)]

    half, side = index % 2, stream // 2

    def part_of(terms, which):
        return lax.dynamic_index_in_dim(terms, which, 1, keepdims=False)

    half_got = lax.ppermute(part_of(half_sum, 1 - side), "wsh", OTHER_SIDE)
    side_got = lax.ppermute(part_of(side_sum, 1 - half), "ctx", OTHER_HALF)
    d_q, d_kv = run_backward(meta, head_q, kv_all, head_attn, lse, head_d_attn)
    d_tokens, gathered = finish(
        d_q,
        d_kv.reshape(4, 8 * rows, 2 * HEAD_SIZE),
        group_act,
        small_term,
        head_blocks,
        branch_part.reshape(8 * rows, WIDTH),
        qkv_pieces,
        tokens[0],
        d_middle,
        gain_first,
    )
    gathered, half_got, side_got = lax.optimization_barrier((gathered, half_got, side_got))
    expert_own = jnp.concatenate(
        [
            part_of(half_sum, side).astype(F32) + half_got.astype(F32),
            part_of(side_sum, half).astype(F32) + side_got.astype(F32),
        ],
        axis=1,
    )
    d_w_qkv, d_w_out, rest = assemble(gathered)
    d_gain_first = jnp.sum(d_w_qkv * w_qkv.astype(BF).astype(F32), axis=1) / gain_attn.astype(BF).astype(F32)
    return (
        output_rows[None],
        d_tokens[None],
        d_gain_first,
        d_w_qkv,
        d_w_out,
        rest[:, experts_count],
        rest[:, :experts_count],
        expert_own[0][None],
        expert_own[1][None],
        expert_own[2].T[None],
    )


def solution(mesh):
    placed = (
        P("wsh", "ctx", None),
        P(),
        P(),
        P("wsh", "ctx", None),
        P("wsh"),
        P("wsh", None),
        P("wsh", None),
        P("wsh"),
        P("wsh", None),
        P("ctx", "wsh", None),
        P("ctx", "wsh", None),
        P("ctx", None, "wsh"),
        P("wsh", "ctx", None),
    )
    return jax.shard_map(
        body,
        mesh=mesh,
        in_specs=placed,
        out_specs=(
            P("wsh", "ctx", None),
            P("wsh", "ctx", None),
            P("wsh"),
            P("wsh", None),
            P("wsh", None),
            P("wsh"),
            P("wsh", None),
            P("ctx", "wsh", None),
            P("ctx", "wsh", None),
            P("ctx", None, "wsh"),
        ),
        check_vma=False,
    )
```

```python
import functools

import jax
import jax.numpy as jnp
from jax import lax
from jax.experimental import pallas as pl
from jax.experimental.pallas import tpu as pltpu
from jax.sharding import PartitionSpec as P

QUERY_HEADS = 24
KEY_VALUE_HEADS = 8
HEAD_SIZE = 64
GROUP = QUERY_HEADS // KEY_VALUE_HEADS
TOP = 2
BLOCK = 64
WIDTH = GROUP * HEAD_SIZE
HEAD_COLUMNS = WIDTH + 2 * HEAD_SIZE
CHUNK = 512
LANES = 3
TURN = 256

EPSILON = 1e-05
NEG_BIG = -1e30
BF = jnp.bfloat16
F32 = jnp.float32

def turned(index):
    return index % 4 * 8 + index // 4 % 2 * 4 + index // 8


ROW = [[turned(y * 8 + r) for r in range(8)] for y in range(4)]
OWNERS = [[(2 * e + k) * 4 + w for k in range(2) for w in range(4)] for e in range(16)]
OTHER_HALF = [(c, c ^ 1) for c in range(32)]
OTHER_SIDE = [(w, w ^ 2) for w in range(4)]
OTHER_CORE = [(w, w ^ 1) for w in range(4)]
NEXT_Z = [(c * 4 + w, (c ^ 4) * 4 + (w ^ 2)) for c in range(32) for w in range(4)]

def dot(a, b, dims=((1,), (0,))):
    return lax.dot_general(a, b, (dims, ((), ())), preferred_element_type=F32)


NT = ((1,), (1,))
TN = ((0,), (0,))


def block_range(meta, b):
    base = meta[BLOCK + b] * BLOCK
    lane = lax.broadcasted_iota(jnp.int32, (1, WIDTH), 1)
    query = base + (lane & (BLOCK - 1))
    start = jnp.zeros((1, WIDTH), jnp.int32)
    first = jnp.int32(0)
    for i in range(3):
        bound = meta[80 + i]
        start = jnp.where(query >= bound, bound, start)
        first = jnp.where(base >= bound, bound, first)
    first = (first // 128) * 128
    count = (base + BLOCK - first + CHUNK - 1) // CHUNK
    return query, start, first, count


def list_work(meta, blocks, block_s, key_s):
    def one(b, n):
        _, _, first, count = block_range(meta, b)

        def put(i, n):
            block_s[n] = b
            key_s[n] = first + i * CHUNK
            return n + 1

        return lax.fori_loop(0, count, put, n)

    total = lax.fori_loop(0, blocks, one, jnp.int32(0))
    for i in range(LANES):
        block_s[total + i] = blocks
        key_s[total + i] = 0
    return (total + LANES - 1) // LANES


def allowed_of(key_start, query, start):
    key = key_start + lax.broadcasted_iota(jnp.int32, (CHUNK, WIDTH), 0)
    return (key <= query) & (key >= start)


def stack_heads(rows):
    return jnp.concatenate([rows[:, g * HEAD_SIZE : (g + 1) * HEAD_SIZE] for g in range(GROUP)], axis=0)


def sort_blocks(meta, kv_ref, sorted_ref):
    total = kv_ref.shape[0]

    def one(p, carry):
        source = pl.multiple_of(meta[p] * BLOCK, BLOCK)
        target = pl.multiple_of(p * BLOCK, BLOCK)
        sorted_ref[pl.ds(target, BLOCK), :] = kv_ref[pl.ds(source, BLOCK), :]
        return carry

    lax.fori_loop(0, total // BLOCK, one, 0, unroll=8)
    sorted_ref[total:, :] = jnp.zeros((CHUNK, sorted_ref.shape[1]), sorted_ref.dtype)


def transpose_all(sorted_ref, turned_ref):
    steps = sorted_ref.shape[0] // TURN

    def one(i, carry):
        at = pl.multiple_of(i * TURN, TURN)
        turned_ref[:, pl.ds(at, TURN)] = sorted_ref[pl.ds(at, TURN), :].T
        return carry

    lax.fori_loop(0, steps, one, 0)


def attention_forward(
    meta, q_ref, kv_ref, o_ref, lse_ref,
    sorted_ref, turned_ref, pad_ref, query_ref, start_ref, top_ref, total_ref, acc_ref, block_s, key_s,
):
    blocks = q_ref.shape[0] // BLOCK
    sort_blocks(meta, kv_ref, sorted_ref)
    transpose_all(sorted_ref, turned_ref)
    share = list_work(meta, blocks, block_s, key_s)
    zeros = jnp.zeros((WIDTH, HEAD_SIZE), BF)
    top_ref[...] = jnp.full(top_ref.shape, NEG_BIG, F32)
    total_ref[...] = jnp.zeros_like(total_ref)
    acc_ref[...] = jnp.zeros_like(acc_ref)
    query_ref[blocks] = jnp.full((1, WIDTH), -1, jnp.int32)
    start_ref[blocks] = jnp.zeros((1, WIDTH), jnp.int32)
    pad_ref[blocks] = jnp.zeros((WIDTH, 2 * HEAD_SIZE), BF)

    def prepare_block(b, carry):
        query_ref[b], start_ref[b], _, _ = block_range(meta, b)
        at = pl.multiple_of(b * BLOCK, BLOCK)
        rows = stack_heads(q_ref[pl.ds(at, BLOCK), :]) * jnp.asarray(HEAD_SIZE**-0.5, BF)
        pad_ref[b] = jnp.concatenate([rows, zeros], axis=1)
        return carry

    lax.fori_loop(0, blocks, prepare_block, 0, unroll=4)

    def work(i, carry):
        blocks_now = [block_s[lane * share + i] for lane in range(LANES)]
        starts_now = [pl.multiple_of(key_s[lane * share + i], 128) for lane in range(LANES)]
        results = []
        for b, key_start in zip(blocks_now, starts_now):
            scores = dot(sorted_ref[pl.ds(key_start, CHUNK), :], pad_ref[b], NT)
            scores = jnp.where(allowed_of(key_start, query_ref[b], start_ref[b]), scores, NEG_BIG)
            top = top_ref[b]
            top_new = jnp.maximum(top, jnp.max(scores, axis=0, keepdims=True))
            weights = jnp.exp(scores - top_new)
            fade = jnp.exp(top - top_new)
            total = total_ref[b] * fade + jnp.sum(weights, axis=0, keepdims=True)
            values = turned_ref[HEAD_SIZE:, pl.ds(key_start, CHUNK)]
            results.append((top_new, total, acc_ref[b] * fade + dot(values, weights.astype(BF))))
        for b, (top, total, acc) in zip(blocks_now, results):
            top_ref[b] = top
            total_ref[b] = total
            acc_ref[b] = acc
        return carry

    lax.fori_loop(0, share, work, 0)

    def finish_block(b, carry):
        at = pl.multiple_of(b * BLOCK, BLOCK)
        total = total_ref[b]
        lse_ref[b] = top_ref[b] + jnp.log(total)
        result = (acc_ref[b] / total).T.astype(BF)
        o_ref[pl.ds(at, BLOCK), :] = jnp.concatenate(
            [result[g * BLOCK : (g + 1) * BLOCK] for g in range(GROUP)], axis=1
        )
        return carry

    lax.fori_loop(0, blocks, finish_block, 0, unroll=4)


def attention_backward(
    meta, q_ref, kv_ref, o_ref, lse_ref, do_ref, dq_ref, dkv_ref,
    sorted_ref, turned_ref, total_ref, both_ref, query_ref, start_ref, delta_ref, acc_ref, block_s, key_s,
):
    blocks = q_ref.shape[0] // BLOCK
    sort_blocks(meta, kv_ref, sorted_ref)
    transpose_all(sorted_ref, turned_ref)
    share = list_work(meta, blocks, block_s, key_s)
    total_ref[...] = jnp.zeros_like(total_ref)
    acc_ref[...] = jnp.zeros_like(acc_ref)
    query_ref[blocks] = jnp.full((1, WIDTH), -1, jnp.int32)
    start_ref[blocks] = jnp.zeros((1, WIDTH), jnp.int32)
    delta_ref[blocks] = jnp.zeros((1, WIDTH), F32)
    both_ref[blocks] = jnp.zeros((2 * WIDTH, 2 * HEAD_SIZE), BF)
    zeros = jnp.zeros((WIDTH, HEAD_SIZE), BF)
    scaling = HEAD_SIZE**-0.5

    def prepare_block(b, carry):
        query_ref[b], start_ref[b], _, _ = block_range(meta, b)
        at = pl.multiple_of(b * BLOCK, BLOCK)
        rows = stack_heads(q_ref[pl.ds(at, BLOCK), :]) * jnp.asarray(scaling, BF)
        grad = stack_heads(do_ref[pl.ds(at, BLOCK), :])
        value = stack_heads(o_ref[pl.ds(at, BLOCK), :])
        delta_ref[b] = jnp.sum((grad.astype(F32) * value.astype(F32)).T, axis=0, keepdims=True)
        both_ref[b, :WIDTH] = jnp.concatenate([rows, zeros], axis=1)
        both_ref[b, WIDTH:] = jnp.concatenate([zeros, grad], axis=1)
        return carry

    lax.fori_loop(0, blocks, prepare_block, 0, unroll=4)

    def work(i, carry):
        blocks_now = [block_s[lane * share + i] for lane in range(LANES)]
        starts_now = [pl.multiple_of(key_s[lane * share + i], 128) for lane in range(LANES)]
        results = []
        for b, key_start in zip(blocks_now, starts_now):
            keys = sorted_ref[pl.ds(key_start, CHUNK), :]
            scores = dot(keys, both_ref[b, :WIDTH], NT)
            d_probs = dot(keys, both_ref[b, WIDTH:], NT)
            allowed = allowed_of(key_start, query_ref[b], start_ref[b])
            probs = jnp.where(allowed, jnp.exp(scores - lse_ref[b]), 0.0)
            d_scores = (probs * (d_probs - delta_ref[b])).astype(BF)
            joined = jnp.concatenate([d_scores, probs.astype(BF)], axis=1)
            turned = turned_ref[:HEAD_SIZE, pl.ds(key_start, CHUNK)]
            results.append((acc_ref[b] + dot(turned, d_scores), dot(joined, both_ref[b])))
        for b, key_start, (acc, d_keys) in zip(blocks_now, starts_now, results):
            acc_ref[b] = acc
            total_ref[pl.ds(key_start, CHUNK), :] += d_keys
        return carry

    lax.fori_loop(0, share, work, 0)

    def finish_block(b, carry):
        at = pl.multiple_of(b * BLOCK, BLOCK)
        result = (acc_ref[b] * scaling).T.astype(BF)
        dq_ref[pl.ds(at, BLOCK), :] = jnp.concatenate(
            [result[g * BLOCK : (g + 1) * BLOCK] for g in range(GROUP)], axis=1
        )
        return carry

    lax.fori_loop(0, blocks, finish_block, 0, unroll=4)

    def back(p, carry):
        target = pl.multiple_of(meta[p] * BLOCK, BLOCK)
        source = pl.multiple_of(p * BLOCK, BLOCK)
        dkv_ref[pl.ds(target, BLOCK), :] = total_ref[pl.ds(source, BLOCK), :].astype(BF)
        return carry

    lax.fori_loop(0, kv_ref.shape[0] // BLOCK, back, 0, unroll=8)


def local_call(kernel, outs, n_vmem, scratch, name):
    return pl.pallas_call(
        kernel,
        out_shape=outs,
        in_specs=[pl.BlockSpec(memory_space=pltpu.SMEM)] + [pl.BlockSpec(memory_space=pltpu.VMEM)] * n_vmem,
        out_specs=tuple(pl.BlockSpec(memory_space=pltpu.VMEM) for _ in outs),
        scratch_shapes=scratch,
        compiler_params=pltpu.CompilerParams(vmem_limit_bytes=40 * 2**20),
        cost_estimate=pl.CostEstimate(flops=4 * 10**9, bytes_accessed=10**7, transcendentals=4 * 10**6),
        name=name,
    )


def work_scratch(rows, keys):
    blocks = rows // BLOCK
    most = blocks * (keys // CHUNK + 1) + LANES
    return [pltpu.SMEM((most,), jnp.int32), pltpu.SMEM((most,), jnp.int32)]


def run_forward(meta, q, kv):
    rows, keys = q.shape[0], kv.shape[0]
    blocks = rows // BLOCK
    line = (blocks + 1, 1, WIDTH)
    return local_call(
        attention_forward,
        (jax.ShapeDtypeStruct((rows, WIDTH), BF), jax.ShapeDtypeStruct(line, F32)),
        2,
        [
            pltpu.VMEM((keys + CHUNK, 2 * HEAD_SIZE), BF),
            pltpu.VMEM((2 * HEAD_SIZE, keys + CHUNK), BF),
            pltpu.VMEM((blocks + 1, WIDTH, 2 * HEAD_SIZE), BF),
            pltpu.VMEM(line, jnp.int32),
            pltpu.VMEM(line, jnp.int32),
            pltpu.VMEM(line, F32),
            pltpu.VMEM(line, F32),
            pltpu.VMEM((blocks + 1, HEAD_SIZE, WIDTH), F32),
        ]
        + work_scratch(rows, keys),
        "attention_forward",
    )(meta, q, kv)


def run_backward(meta, q, kv, o, lse, d_o):
    rows, keys = q.shape[0], kv.shape[0]
    blocks = rows // BLOCK
    line = (blocks + 1, 1, WIDTH)
    return local_call(
        attention_backward,
        (jax.ShapeDtypeStruct((rows, WIDTH), BF), jax.ShapeDtypeStruct((keys, 2 * HEAD_SIZE), BF)),
        5,
        [
            pltpu.VMEM((keys + CHUNK, 2 * HEAD_SIZE), BF),
            pltpu.VMEM((2 * HEAD_SIZE, keys + CHUNK), BF),
            pltpu.VMEM((keys + CHUNK, 2 * HEAD_SIZE), F32),
            pltpu.VMEM((blocks + 1, 2 * WIDTH, 2 * HEAD_SIZE), BF),
            pltpu.VMEM(line, jnp.int32),
            pltpu.VMEM(line, jnp.int32),
            pltpu.VMEM(line, F32),
            pltpu.VMEM((blocks + 1, HEAD_SIZE, WIDTH), F32),
        ]
        + work_scratch(rows, keys),
        "attention_backward",
    )(meta, q, kv, o, lse, d_o)


def assemble_kernel(pieces_ref, weight_ref, qkv_ref, out_ref, rest_ref):
    parts = [pieces_ref[0, i].astype(F32) for i in range(8)]
    ends = (0, WIDTH, WIDTH + HEAD_SIZE, HEAD_COLUMNS)
    d_qkv = jnp.concatenate([t[:, a:b] for a, b in zip(ends[:-1], ends[1:]) for t in parts], axis=1)
    qkv_ref[...] = d_qkv
    gain_part = jnp.sum(d_qkv * weight_ref[...].astype(BF).astype(F32), axis=1, keepdims=True)
    out_ref[...] = jnp.concatenate([t[:, 384:] for t in parts], axis=1)
    tail = parts[0]
    for t in parts[1:]:
        tail = tail + t
    lane = lax.broadcasted_iota(jnp.int32, rest_ref.shape, 1)
    rest_ref[...] = jnp.where(lane == 17, gain_part, tail[:, HEAD_COLUMNS:384])


def assemble(gathered, weight):
    _, _, piece, columns = gathered.shape

    def by_rows(n):
        return pl.BlockSpec((piece, n), lambda i: (i, 0))

    return pl.pallas_call(
        assemble_kernel,
        out_shape=(
            jax.ShapeDtypeStruct((4 * piece, 8 * HEAD_COLUMNS), F32),
            jax.ShapeDtypeStruct((4 * piece, 8 * WIDTH), F32),
            jax.ShapeDtypeStruct((4 * piece, 64), F32),
        ),
        grid=(4,),
        in_specs=[pl.BlockSpec((1, 8, piece, columns), lambda i: (i, 0, 0, 0)), by_rows(weight.shape[1])],
        out_specs=(by_rows(8 * HEAD_COLUMNS), by_rows(8 * WIDTH), by_rows(64)),
        compiler_params=pltpu.CompilerParams(vmem_limit_bytes=40 * 2**20),
        name="assemble",
    )(gathered, weight)


MESH = pl.DeviceIdType.MESH
ANY = pl.BlockSpec(memory_space=pl.ANY)


class Copies:
    def __init__(self, send, recv, local):
        self.send, self.recv, self.local = send, recv, local
        self.remote_count = self.local_count = 0
        self.started, self.kept, self.left = [], [], []

    def to(self, source, target, device):
        k = self.remote_count
        self.remote_count += 1
        copy = pltpu.make_async_remote_copy(
            source, target, self.send.at[k], self.recv.at[k], device_id=device, device_id_type=MESH
        )
        copy.start()
        self.started.append(copy)
        return copy

    def keep(self, source, middle, target):
        k = self.local_count
        self.local_count += 2
        first = pltpu.make_async_copy(source, middle, self.local.at[k])
        first.start()
        self.kept.append((first, pltpu.make_async_copy(middle, target, self.local.at[k + 1])))

    def move_kept(self):
        for first, second in self.kept:
            first.wait()
            second.start()

    def sent(self, several):
        for copy in several:
            copy.wait_send()
            self.left.append(copy)

    def finish(self, arrived):
        for copy in self.started:
            if not any(copy is other for other in self.left):
                copy.wait_send()
            if not any(copy is other for other in arrived):
                copy.wait_recv()
        for _, second in self.kept:
            second.wait()


def meet(devices):
    barrier = pltpu.get_barrier_semaphore()
    for device in devices:
        pl.semaphore_signal(barrier, inc=1, device_id=device, device_id_type=MESH)
    pl.semaphore_wait(barrier, len(devices))


def gather_rows_kernel(
    tok_ref, wp_ref, gain_ref, wo_ref, tok_out, wp_out, gain_out, wo_out, v_tok, v_wp, v_gain, v_wo, send, recv, local
):
    place, stream = turned(lax.axis_index("ctx")), lax.axis_index("wsh")
    x, z = place % 4, (place // 4) % 2
    right, left = {"ctx": turned(place - x + (x + 1) % 4)}, {"ctx": turned(place - x + (x + 3) % 4)}
    across = place + 4 - 8 * z
    other = {"wsh": stream + 1 - 2 * (stream % 2)}
    far = {"ctx": turned(across), "wsh": (stream + 2) % 4}
    meet([right, left, {"ctx": turned(across)}, other, far])
    copies = Copies(send, recv, local)
    half = tok_ref.shape[0] // 2
    own, own_z = z * 4 + x, (1 - z) * 4 + x
    left_id, right_id = z * 4 + (x + 3) % 4, z * 4 + (x + 1) % 4
    left_z, right_z = (1 - z) * 4 + (x + 3) % 4, (1 - z) * 4 + (x + 1) % 4

    def rows(ref, h):
        return ref.at[pl.ds(h * half, half)]

    def spot(block, h):
        return tok_out.at[block, pl.ds(h * half, half)]

    head = place % 8
    far_wp = copies.to(wp_ref.at[across % 8], wp_out.at[stream], far)
    far_gain = copies.to(gain_ref, gain_out.at[stream], far)
    cross = [copies.to(rows(tok_ref, h), spot(own, h), {"ctx": turned(across)}) for h in range(2)]
    to_right = [copies.to(rows(tok_ref, h), spot(own, h), right) for h in (0, 1)]
    to_left = [copies.to(rows(tok_ref, h), spot(own, h), left) for h in (1, 0)]
    copies.to(wp_ref.at[head], wp_out.at[stream], other)
    copies.to(gain_ref, gain_out.at[stream], other)
    third = wo_ref.shape[0] // 3
    parts = [pl.ds(i * third, third) for i in range(3)]
    far_wo = [copies.to(wo_ref.at[p], wo_out.at[stream, p], far) for p in parts]
    copies.to(wo_ref, wo_out.at[stream], other)
    copies.keep(tok_ref, v_tok, tok_out.at[own])
    copies.keep(wp_ref.at[head], v_wp, wp_out.at[stream])
    copies.keep(gain_ref, v_gain, gain_out.at[stream])
    copies.keep(wo_ref, v_wo, wo_out.at[stream])
    copies.move_kept()

    arrived = []

    def arrive(copy):
        copy.wait_recv()
        arrived.append(copy)

    far_stream = (stream + 2) % 4
    arrive(far_wp)
    copies.to(wp_out.at[far_stream], wp_out.at[far_stream], other)
    arrive(far_gain)
    copies.to(gain_out.at[far_stream], gain_out.at[far_stream], other)
    arrive(to_right[0])
    copies.to(spot(left_id, 0), spot(left_id, 0), right)
    arrive(to_left[0])
    copies.to(spot(right_id, 1), spot(right_id, 1), left)
    arrive(cross[0])
    arrive(cross[1])
    z_right = [copies.to(spot(own_z, h), spot(own_z, h), right) for h in (0, 1)]
    z_left = [copies.to(spot(own_z, h), spot(own_z, h), left) for h in (1, 0)]
    arrive(z_right[0])
    copies.to(spot(left_z, 0), spot(left_z, 0), right)
    arrive(z_left[0])
    copies.to(spot(right_z, 1), spot(right_z, 1), left)
    for p, copy in zip(parts, far_wo):
        arrive(copy)
        copies.to(wo_out.at[far_stream, p], wo_out.at[far_stream, p], other)
    copies.finish(arrived)


def gather_rows(tok, wp, gain, wo):
    return pl.pallas_call(
        gather_rows_kernel,
        out_shape=(
            jax.ShapeDtypeStruct((8,) + tok.shape, BF),
            jax.ShapeDtypeStruct((4,) + wp.shape[1:], BF),
            jax.ShapeDtypeStruct((4,) + gain.shape, BF),
            jax.ShapeDtypeStruct((4,) + wo.shape, BF),
        ),
        in_specs=[ANY] * 4,
        out_specs=(ANY,) * 4,
        scratch_shapes=[
            pltpu.VMEM(tok.shape, BF),
            pltpu.VMEM(wp.shape[1:], BF),
            pltpu.VMEM(gain.shape, BF),
            pltpu.VMEM(wo.shape, BF),
            pltpu.SemaphoreType.DMA((27,)),
            pltpu.SemaphoreType.DMA((27,)),
            pltpu.SemaphoreType.DMA((8,)),
        ],
        compiler_params=pltpu.CompilerParams(collective_id=1, has_side_effects=True, vmem_limit_bytes=40 * 2**20),
        name="gather_rows",
    )(tok, wp, gain, wo)


def gather_keys_kernel(kv_ref, kv_out, v_kv, send, recv, local):
    place = turned(lax.axis_index("ctx"))
    y = place // 8
    up, down = {"ctx": turned((place + 8) % 32)}, {"ctx": turned((place + 24) % 32)}
    meet([up, down])
    copies = Copies(send, recv, local)
    half = kv_ref.shape[0] // 2

    def rows(h):
        return kv_ref.at[pl.ds(h * half, half)]

    def spot(block, h):
        return kv_out.at[block, pl.ds(h * half, half)]

    to_up = [copies.to(rows(h), spot(y, h), up) for h in (0, 1)]
    to_down = [copies.to(rows(h), spot(y, h), down) for h in (1, 0)]
    copies.keep(kv_ref, v_kv, kv_out.at[y])
    copies.move_kept()
    to_up[0].wait_recv()
    copies.to(spot((y + 3) % 4, 0), spot((y + 3) % 4, 0), up)
    to_down[0].wait_recv()
    copies.to(spot((y + 1) % 4, 1), spot((y + 1) % 4, 1), down)
    copies.finish([to_up[0], to_down[0]])


def gather_keys(kv):
    return pl.pallas_call(
        gather_keys_kernel,
        out_shape=jax.ShapeDtypeStruct((4,) + kv.shape, BF),
        in_specs=[ANY],
        out_specs=ANY,
        scratch_shapes=[
            pltpu.VMEM(kv.shape, BF),
            pltpu.SemaphoreType.DMA((6,)),
            pltpu.SemaphoreType.DMA((6,)),
            pltpu.SemaphoreType.DMA((2,)),
        ],
        compiler_params=pltpu.CompilerParams(collective_id=2, has_side_effects=True, vmem_limit_bytes=40 * 2**20),
        name="gather_keys",
    )(kv)


FF_STEP = 256


def middle_kernel(
    attn_ref, x_ref, cot_ref, wo_ref, head_ref, gain_ref, choice_ref, slot_ref, slot_t_ref, w_ref,
    out_ref, d_mid_ref, small_ref, d_attn_to, branch_to, half_out, side_out,
    attn_v, wo_v, w_v, x_v, g_v, turned_x, turned_g, out_v, d_in_v, back_v, returned_v, acc_v, gate_v, up_v,
    hidden_v, d_gate_v, d_up_v, got_v, half_got, side_got, mid_v, act_v, d_attn_v, branch_v, send, recv, local,
):
    index, stream = lax.axis_index("ctx"), lax.axis_index("wsh")
    place, mine = turned(index), index // 2
    y, r = place // 8, place % 8
    inner = (index % 4 + 1) // 2 % 2

    def device(p):
        return {"ctx": p // 2 * 4 + (1 - inner) * (3 * (p % 2)) + inner * (1 + p % 2)}

    peers = [(mine + k) % 16 for k in range(1, 16)]
    in_row = [(r + k) % 8 for k in range(1, 8)]
    core, half, side = stream % 2, index % 2, stream // 2
    other = {"wsh": stream + 1 - 2 * core}
    other_half, other_side = {"ctx": index + 1 - 2 * half}, {"wsh": (stream + 2) % 4}
    meet([device(p) for p in peers] + [other, other_half, other_side])
    copies = Copies(send, recv, local)
    width, rows = turned_x.shape
    tokens = x_ref.shape[0]
    quarter = width // 4
    own, arrived = [], []

    def here(source, target):
        copy = pltpu.make_async_copy(source, target, local.at[len(own)])
        copy.start()
        own.append(copy)
        return copy

    def arrive(several):
        for copy in several:
            copy.wait_recv()
            arrived.append(copy)

    attn_came = [copies.to(attn_ref.at[pr], attn_v.at[r], {"ctx": turned(8 * y + pr)}) for pr in in_row]
    own_attn = here(attn_ref.at[r], attn_v.at[r])
    own_wo = here(wo_ref, wo_v)
    weights = [
        here(w_ref.at[4 * k + q, m], w_v.at[k, m, pl.ds(q * quarter, quarter)])
        for k in range(2)
        for q in range(4)
        for m in range(3)
    ]
    lanes = lax.broadcasted_iota(jnp.int32, (tokens, 64), 1)
    chosen = [choice_ref[:, j : j + 1] == lanes for j in range(TOP)]
    slot_rows = lax.broadcasted_iota(jnp.int32, (rows, tokens), 0)
    to_slot = [jnp.where(slot_t_ref[j : j + 1, :] == slot_rows, 1.0, 0.0).astype(BF) for j in range(TOP)]
    own_attn.wait()
    own_wo.wait()
    arrive(attn_came)
    middle = x_ref[...].astype(F32)
    for i in range(4):
        pair = jnp.concatenate([attn_v[2 * i], attn_v[2 * i + 1]], axis=1)
        middle += dot(pair, wo_v[i * quarter : (i + 1) * quarter, :])
    mid_v[...] = middle
    scale = rms_scale(middle)
    act = (middle * scale * gain_ref[...]).astype(BF)
    act_v[...] = act
    out_v[...] = dot(to_slot[0] + to_slot[1], act).astype(BF).reshape(out_v.shape)
    came = [copies.to(out_v.at[p], x_v.at[mine], device(p)) for p in peers]
    own_x = here(out_v.at[mine], x_v.at[mine])
    logits = dot(act, head_ref[:, HEAD_COLUMNS:])
    picked = [jnp.sum(jnp.where(c, logits, 0.0), axis=-1, keepdims=True) for c in chosen]
    top = jnp.maximum(picked[0], picked[1])
    powers = [jnp.exp(p - top) for p in picked]
    gates = [p / (powers[0] + powers[1]) for p in powers]
    gated = jnp.concatenate([(g * cot_ref[...].astype(F32)).astype(BF) for g in gates], axis=0)
    d_in_v[...] = dot(jnp.concatenate(to_slot, axis=1), gated).astype(BF).reshape(d_in_v.shape)
    came_g = [copies.to(d_in_v.at[p], g_v.at[mine], device(p)) for p in peers]
    own_g = here(d_in_v.at[mine], g_v.at[mine])

    for copy in weights:
        copy.wait()
    arrive(came)
    own_x.wait()
    steps = w_v.shape[3] // FF_STEP
    acc_v[...] = jnp.zeros_like(acc_v)

    def forward(i, carry):
        k, at = i // steps, pl.ds(pl.multiple_of(i % steps * FF_STEP, FF_STEP), FF_STEP)
        inputs = x_v[...].reshape(rows, width)
        gate = dot(inputs, w_v[k, 0, :, at])
        up = dot(inputs, w_v[k, 1, :, at])
        hidden = (gate * jax.nn.sigmoid(gate) * up).astype(BF)
        gate_v[i] = gate
        up_v[i] = up
        hidden_v[k, :, at] = hidden
        acc_v[...] += dot(hidden, w_v[k, 2, :, at], NT)
        return carry

    lax.fori_loop(0, 2 * steps, forward, 0)
    copies.sent(came)
    out_v[...] = acc_v[...].astype(BF).reshape(out_v.shape)
    outs = [copies.to(out_v.at[p], back_v.at[mine], device(p)) for p in peers]
    own_back = here(out_v.at[mine], back_v.at[mine])
    for q in range(4):
        at = slice(q * quarter, (q + 1) * quarter)
        turned_x[at, :] = x_v[:, :, at].reshape(rows, quarter).T
    acc_v[...] = jnp.zeros_like(acc_v)
    arrive(came_g)
    own_g.wait()

    def backward(i, carry):
        k, at = i // steps, pl.ds(pl.multiple_of(i % steps * FF_STEP, FF_STEP), FF_STEP)
        d_hidden = dot(g_v[...].reshape(rows, width), w_v[k, 2, :, at])
        gate, up = gate_v[i], up_v[i]
        sigmoid = jax.nn.sigmoid(gate)
        d_gate = (d_hidden * up * sigmoid * (1.0 + gate * (1.0 - sigmoid))).astype(BF)
        d_up = (d_hidden * (gate * sigmoid)).astype(BF)
        d_gate_v[k, :, at] = d_gate
        d_up_v[k, :, at] = d_up
        acc_v[...] += dot(d_gate, w_v[k, 0, :, at], NT) + dot(d_up, w_v[k, 1, :, at], NT)
        return carry

    lax.fori_loop(0, 2 * steps, backward, 0)
    copies.sent(came_g)
    d_in_v[...] = acc_v[...].astype(BF).reshape(d_in_v.shape)
    returns = [copies.to(d_in_v.at[p], returned_v.at[mine], device(p)) for p in peers]
    own_returned = here(d_in_v.at[mine], returned_v.at[mine])
    for q in range(4):
        at = slice(q * quarter, (q + 1) * quarter)
        turned_g[at, :] = g_v[:, :, at].reshape(rows, quarter).T

    def terms(k, z, c):
        at = pl.ds(pl.multiple_of((2 * z + c) * quarter, quarter), quarter)
        part = turned_x[at, :]
        return (
            dot(part, d_gate_v[k]),
            dot(part, d_up_v[k]),
            dot(turned_g[at, :], hidden_v[k]),
        )

    crossing = []
    for dz in (1, 0):
        z = side + dz - 2 * side * dz

        def other_term(k, carry, z=z, dz=dz):
            at = pl.ds(pl.multiple_of((2 * dz + k) * quarter, quarter), quarter)
            for m, term in enumerate(terms(k, z, 1 - core)):
                w_v[0, m, at] = term.astype(BF)
            return carry

        lax.fori_loop(0, 2, other_term, 0)
        at = pl.ds(2 * dz * quarter, 2 * quarter)
        crossing.append(copies.to(w_v.at[0, :, at], got_v.at[:, at], other))
    halfway = quarter // 2
    for dz, copy in zip((1, 0), crossing):
        z = side + dz - 2 * side * dz
        arrive([copy])
        for dk in (1, 0):
            k = half + dk - 2 * half * dk
            got_at = pl.ds(pl.multiple_of((2 * dz + k) * quarter, quarter), quarter)
            z_at = pl.ds(pl.multiple_of(z * halfway, halfway), halfway)
            k_at = pl.ds(pl.multiple_of(quarter + k * halfway, halfway), halfway)
            for m, term in enumerate(terms(k, z, core)):
                total = (term + got_v[m, got_at].astype(F32)).astype(BF)
                if dk:
                    w_v[1, m, z_at] = total[:halfway]
                else:
                    half_out[m, z] = total[:halfway]
                if dz:
                    w_v[1, m, k_at] = total[halfway:]
                else:
                    side_out[m, k] = total[halfway:]
    first = copies.to(w_v.at[1, :, pl.ds(0, quarter)], half_got, other_half)
    second = copies.to(w_v.at[1, :, pl.ds(quarter, quarter)], side_got, other_side)

    slot_lanes = lax.broadcasted_iota(jnp.int32, (tokens, rows), 1)
    of_slot = [jnp.where(slot_ref[:, j : j + 1] == slot_lanes, 1.0, 0.0).astype(BF) for j in range(TOP)]
    own_back.wait()
    arrive(outs)
    back = back_v[...].reshape(rows, width)
    d_out = cot_ref[...].astype(F32)
    total = mid_v[...]
    d_gates = []
    for j in range(TOP):
        both = dot(of_slot[j], back)
        total += gates[j] * both
        d_gates.append(jnp.sum(d_out * both, axis=-1, keepdims=True))
    out_ref[...] = total.astype(BF)
    inner_sum = gates[0] * d_gates[0] + gates[1] * d_gates[1]
    d_logits = 0.0
    for j in range(TOP):
        d_logits += jnp.where(chosen[j], gates[j] * (d_gates[j] - inner_sum), 0.0)
    d_logits = d_logits.astype(BF)
    own_returned.wait()
    arrive(returns)
    d_act = dot(of_slot[0] + of_slot[1], returned_v[...].reshape(rows, width))
    d_act += dot(d_logits, head_ref[:, HEAD_COLUMNS:], NT)
    middle = mid_v[...]
    normed = middle * scale
    spot = jnp.where(lanes == 16, 1.0, 0.0).astype(BF)
    small_ref[...] = (dot(act_v[...].T, d_logits) + dot((d_act * normed).astype(BF).T, spot)).astype(BF)
    scaled = d_act * gain_ref[...]
    d_mid = d_out + scale * (scaled - normed * scale * jnp.mean(scaled * middle, axis=-1, keepdims=True))
    d_mid_ref[...] = d_mid
    d_branch = d_mid.astype(BF)
    for i in range(8):
        branch_v[i] = d_branch[:, i * WIDTH : (i + 1) * WIDTH]
    to_row = [copies.to(branch_v.at[pr], branch_to.at[r], {"ctx": turned(8 * y + pr)}) for pr in in_row]
    for i in range(4):
        pair = dot(d_branch, wo_v[i * quarter : (i + 1) * quarter, :], NT).astype(BF)
        d_attn_v[2 * i] = pair[:, :WIDTH]
        d_attn_v[2 * i + 1] = pair[:, WIDTH:]
    to_row += [copies.to(d_attn_v.at[pr], d_attn_to.at[r], {"ctx": turned(8 * y + pr)}) for pr in in_row]
    own_row = [here(branch_v.at[r], branch_to.at[r]), here(d_attn_v.at[r], d_attn_to.at[r])]
    arrive([first, second])
    for m in range(3):
        for i in range(2):
            at = slice(i * halfway, (i + 1) * halfway)
            half_out[m, i] = (half_out[m, i].astype(F32) + half_got[m, at].astype(F32)).astype(BF)
            side_out[m, i] = (side_out[m, i].astype(F32) + side_got[m, at].astype(F32)).astype(BF)
    copies.finish(arrived)
    own_back = own_row
    for copy in own_back:
        copy.wait()


def run_middle(attn, x, cotangent, w_out, head_full, gain, choice, slots, weights):
    _, tokens, _ = attn.shape
    width = x.shape[1]
    groups, capacity = 16, 2 * TOP * tokens // 16
    rows, half, quarter = groups * capacity, weights.shape[3], width // 4
    steps = 2 * half // FF_STEP
    vmem = pltpu.VMEM
    whole = pl.BlockSpec(memory_space=pltpu.VMEM)
    slot_rows = vmem((groups, capacity, width), BF)
    wide, low = vmem((steps, rows, FF_STEP), F32), vmem((2, rows, half), BF)
    part = jax.ShapeDtypeStruct((3, 2, quarter // 2, half), BF)
    return pl.pallas_call(
        middle_kernel,
        out_shape=(
            jax.ShapeDtypeStruct(x.shape, BF),
            jax.ShapeDtypeStruct(x.shape, F32),
            jax.ShapeDtypeStruct((width, 64), BF),
            jax.ShapeDtypeStruct(attn.shape, BF),
            jax.ShapeDtypeStruct(attn.shape, BF),
            part,
            part,
        ),
        in_specs=[ANY, whole, whole, ANY, whole, whole, whole, whole, whole, ANY],
        out_specs=(whole, whole, whole, ANY, ANY, whole, whole),
        scratch_shapes=[
            vmem(attn.shape, BF),
            vmem(w_out.shape, BF),
            vmem((2, 3, width, half), BF),
            slot_rows,
            slot_rows,
            vmem((width, rows), BF),
            vmem((width, rows), BF),
            slot_rows,
            slot_rows,
            slot_rows,
            slot_rows,
            vmem((rows, width), F32),
            wide,
            wide,
            low,
            low,
            low,
            vmem((3, width, half), BF),
            vmem((3, quarter, half), BF),
            vmem((3, quarter, half), BF),
            vmem(x.shape, F32),
            vmem(x.shape, BF),
            vmem(attn.shape, BF),
            vmem(attn.shape, BF),
            pltpu.SemaphoreType.DMA((85,)),
            pltpu.SemaphoreType.DMA((85,)),
            pltpu.SemaphoreType.DMA((32,)),
        ],
        compiler_params=pltpu.CompilerParams(collective_id=6, has_side_effects=True, vmem_limit_bytes=60 * 2**20),
        cost_estimate=pl.CostEstimate(flops=15 * 10**9, bytes_accessed=10**8, transcendentals=10**6),
        name="middle",
    )(attn, x, cotangent, w_out, head_full, gain.reshape(1, width), choice, slots, slots.T, weights)


def prepare_kernel(qkv_ref, router_ref, wo_ref, gate_ref, up_ref, down_ref, wp_out, wo_out, expert_out):
    rows = qkv_ref.shape[0]
    experts = router_ref.shape[1]
    wo_out[...] = wo_ref[...].astype(BF)
    expert_out[0] = gate_ref[0].astype(BF)
    expert_out[1] = up_ref[0].astype(BF)
    expert_out[2] = down_ref[0].T.astype(BF)
    router = router_ref[...].astype(BF)
    tail = jnp.zeros((rows, wp_out.shape[2] - HEAD_COLUMNS - experts), BF)
    k_at, v_at = QUERY_HEADS * HEAD_SIZE, (QUERY_HEADS + KEY_VALUE_HEADS) * HEAD_SIZE
    for h in range(KEY_VALUE_HEADS):
        wp_out[h] = jnp.concatenate(
            [
                qkv_ref[:, h * WIDTH : (h + 1) * WIDTH].astype(BF),
                qkv_ref[:, k_at + h * HEAD_SIZE : k_at + (h + 1) * HEAD_SIZE].astype(BF),
                qkv_ref[:, v_at + h * HEAD_SIZE : v_at + (h + 1) * HEAD_SIZE].astype(BF),
                router,
                tail,
            ],
            axis=1,
        )


def prepare(w_qkv, w_router, w_out, w_gate, w_up, w_down):
    shard, half = w_gate.shape[1:]
    step = shard // 3

    def block(n):
        return pl.BlockSpec((step, n), lambda i: (i, 0))

    return pl.pallas_call(
        prepare_kernel,
        out_shape=(
            jax.ShapeDtypeStruct((KEY_VALUE_HEADS, shard, 384), BF),
            jax.ShapeDtypeStruct(w_out.shape, BF),
            jax.ShapeDtypeStruct((3, shard, half), BF),
        ),
        grid=(3,),
        in_specs=[
            block(w_qkv.shape[1]),
            block(w_router.shape[1]),
            block(w_out.shape[1]),
            pl.BlockSpec((1, step, half), lambda i: (0, i, 0)),
            pl.BlockSpec((1, step, half), lambda i: (0, i, 0)),
            pl.BlockSpec((1, half, step), lambda i: (0, 0, i)),
        ],
        out_specs=(
            pl.BlockSpec((KEY_VALUE_HEADS, step, 384), lambda i: (0, i, 0)),
            block(w_out.shape[1]),
            pl.BlockSpec((3, step, half), lambda i: (0, i, 0)),
        ),
        compiler_params=pltpu.CompilerParams(vmem_limit_bytes=40 * 2**20),
        name="prepare",
    )(w_qkv, w_router, w_out, w_gate, w_up, w_down)


def finish_kernel(
    dq_ref, kv_ref, act_ref, small_ref, attn_ref, branch_ref, p0, p1, p2, p3, x_ref, d_mid_ref, gain_ref,
    d_tokens_ref, all_out, kv_v, grad_v, grad_to, term_v, term_to, out_v, out_to, attn_v, act_t, own_v, w_v, acc_v,
    send, recv, local,
):
    place, stream = turned(lax.axis_index("ctx")), lax.axis_index("wsh")
    y, r = place // 8, place % 8
    x, z = r % 4, r // 4

    def at_place(p):
        return {"ctx": turned(p)}

    right, left = at_place(place - x + (x + 1) % 4), at_place(place - x + (x + 3) % 4)
    across = at_place(place + 4 - 8 * z)
    up, down, beyond = (at_place((place + 8 * k) % 32) for k in (1, 3, 2))
    others = [((y + k // 4) % 4, (stream + k % 4) % 4) for k in range(1, 16)]
    in_row = [(r + k) % 8 for k in range(1, 8)]
    meet([{"ctx": turned(r + 8 * py), "wsh": pw} for py, pw in others] + [at_place(8 * y + pr) for pr in in_row])
    copies = Copies(send, recv, local)
    rows, width = act_ref.shape
    shard, piece = width // 4, own_v.shape[0]
    arrived = []

    def arrive(*which):
        for copy in which:
            copy.wait_recv()
            arrived.append(copy)

    own = []

    def here(source, target):
        copy = pltpu.make_async_copy(source, target, local.at[len(own)])
        copy.start()
        own.append(copy)
        return copy

    kv_came = [
        copies.to(kv_ref.at[(y + k) % 4], kv_v.at[y], at_place((place + 8 * k) % 32)) for k in (2, 1, 3)
    ]
    own_kv = here(kv_ref.at[y], kv_v.at[y])
    r_z = (1 - z) * 4 + x
    r_left, r_right = z * 4 + (x + 3) % 4, z * 4 + (x + 1) % 4
    z_left, z_right = (1 - z) * 4 + (x + 3) % 4, (1 - z) * 4 + (x + 1) % 4
    front, rear = pl.ds(0, 4), pl.ds(4, 4)

    def pass_on(device, *at):
        return copies.to(attn_v.at[at], attn_v.at[at], device)

    attn_cross = copies.to(attn_ref, attn_v.at[r], across)
    attn_right = copies.to(attn_ref, attn_v.at[r], right)
    attn_left = copies.to(attn_ref, attn_v.at[r], left)
    own_attn = here(attn_ref, attn_v.at[r])
    weights = [here(p, w_v.at[j]) for j, p in enumerate((p0, p1, p2, p3))]
    dq = dq_ref[...]
    for q in range(4):
        act_t[q * shard : (q + 1) * shard, :] = act_ref[:, q * shard : (q + 1) * shard].T
    for q in range(4):
        term = dot(act_t[q * shard : (q + 1) * shard, :], dq).astype(BF)
        for i in range(4):
            term_v[i, q, :, :WIDTH] = term[i * piece : (i + 1) * piece]
            at = q * shard + i * piece
            term_v[i, q, :, HEAD_COLUMNS:] = small_ref[at : at + piece, :]
    arrive(attn_cross)
    attn_far = [pass_on(right, r_z), pass_on(left, r_z)]
    arrive(attn_right)
    attn_on = [pass_on(right, r_left, front)]
    arrive(attn_left)
    attn_on.append(pass_on(left, r_right, rear))
    own_kv.wait()
    arrive(*kv_came)
    total = kv_v[0].astype(F32)
    for i in range(1, 4):
        total = total + kv_v[i].astype(F32)
    kv = total.astype(BF)
    grad_v[...] = jnp.concatenate([dq, kv, jnp.zeros((rows, 64), BF)], axis=1).reshape(grad_v.shape)
    grads = [copies.to(grad_v.at[pr], grad_to.at[r], at_place(8 * y + pr)) for pr in in_row]
    own_grad = here(grad_v.at[r], grad_to.at[r])
    terms = []
    for dw in (2, 3, 1, 0):
        pw = (stream + dw) % 4
        part = act_t[pl.ds(pl.multiple_of(pw * shard, shard), shard), :]
        term = dot(part, kv).astype(BF)
        for i in range(4):
            term_v[i, pw, :, WIDTH:HEAD_COLUMNS] = term[i * piece : (i + 1) * piece]
        for dy in (2, 1, 3, 0):
            py = (y + dy) % 4
            if dw or dy:
                device = {"ctx": turned(r + 8 * py), "wsh": pw}
                terms.append(copies.to(term_v.at[py, pw], term_to.at[y, stream], device))
    own_term = here(term_v.at[y, stream], term_to.at[y, stream])
    arrive(attn_far[0])
    attn_on.append(pass_on(right, z_left, front))
    arrive(attn_far[1])
    attn_on.append(pass_on(left, z_right, rear))
    own_attn.wait()
    arrive(*attn_on)
    branch = branch_ref[...]
    for h in range(8):
        term = dot(attn_v[h].reshape(rows, WIDTH).T, branch).astype(BF)
        for i in range(2):
            n = 2 * h + i
            out_v[n % 4, n // 4] = term[i * piece : (i + 1) * piece]
    outs = []
    for k in (8, 4, 12, 10, 6, 14, 2, 9, 5, 13, 1, 11, 7, 15, 3):
        py, pw = others[k - 1]
        outs.append(copies.to(out_v.at[py, pw], out_to.at[y, stream], {"ctx": turned(r + 8 * py), "wsh": pw}))
    own_out = here(out_v.at[y, stream], out_to.at[y, stream])
    own_term.wait()
    arrive(*terms)
    total = term_to[0, 0].astype(F32)
    for i in range(1, 16):
        total = total + term_to[i // 4, i % 4].astype(F32)
    own_v[:, :384] = total.astype(BF)
    own_out.wait()
    arrive(*outs)
    total = out_to[0, 0].astype(F32)
    for i in range(1, 16):
        total = total + out_to[i // 4, i % 4].astype(F32)
    own_v[:, 384:] = total.astype(BF)

    half = piece // 2
    first, last = pl.ds(0, half), pl.ds(half, half)

    def on(device, *at):
        return copies.to(all_out.at[at], all_out.at[at], device)

    a_cross = copies.to(own_v.at[first], all_out.at[y, r, first], across)
    a_right = copies.to(own_v.at[first], all_out.at[y, r, first], right)
    a_left = copies.to(own_v.at[first], all_out.at[y, r, first], left)
    b_up = copies.to(own_v.at[last], all_out.at[y, r, last], up)
    b_down = copies.to(own_v.at[last], all_out.at[y, r, last], down)
    b_beyond = copies.to(own_v.at[last], all_out.at[y, r, last], beyond)
    keep = here(own_v, all_out.at[y, r])

    for copy in weights:
        copy.wait()
    own_grad.wait()
    arrive(*grads)
    acc_v[...] = jnp.zeros_like(acc_v)
    shards = (stream, stream + 1 - 2 * (stream % 2), (stream + 2) % 4, 3 - stream)

    def heads(start, count):
        def one(h, carry):
            grad = grad_to[h][:, :HEAD_COLUMNS]
            for j in range(4):
                acc_v[shards[j]] += dot(grad, w_v[j, h][:, :HEAD_COLUMNS], NT)
            return carry

        lax.fori_loop(start, start + count, one, 0)

    heads(0, 2)
    keep.wait()
    arrive(a_cross)
    a_z_right = on(right, y, r_z, first)
    a_z_left = on(left, y, r_z, first)
    arrive(a_right)
    a_on = on(right, y, r_left, first)
    arrive(b_up, b_down, b_beyond)
    lower, upper, every = pl.ds(0, 2), pl.ds(2, 2), pl.ds(0, 4)
    b_right = on(right, every, r, last)
    b_left = on(left, every, r, last)
    b_cross = on(across, every, r, last)
    heads(2, 2)
    arrive(a_z_left, a_left)
    a_z_on = on(left, y, z_right, first)
    arrive(a_z_right, a_on, a_z_on)
    low_r, high_r = pl.ds(0, 4), pl.ds(4, 4)
    c_up = [on(up, y, low_r, first), on(up, y, high_r, first)]
    c_down = [on(down, y, high_r, first), on(down, y, low_r, first)]
    heads(4, 2)
    arrive(b_right)
    on(right, lower, r_left, last)
    arrive(b_left)
    on(left, upper, r_right, last)
    arrive(b_cross)
    b_z_right = on(right, every, r_z, last)
    b_z_left = on(left, every, r_z, last)
    arrive(c_up[0])
    on(up, (y + 3) % 4, low_r, first)
    arrive(c_down[0])
    on(down, (y + 1) % 4, high_r, first)
    heads(6, 2)
    arrive(b_z_right)
    on(right, lower, z_left, last)
    arrive(b_z_left)
    on(left, upper, z_right, last)
    values = x_ref[...].astype(F32)
    scale = rms_scale(values)
    inner = 0.0
    for q in range(4):
        at = slice(q * shard, (q + 1) * shard)
        inner += jnp.sum(acc_v[q] * gain_ref[:, at] * values[:, at], axis=-1, keepdims=True)
    inner = inner * (1.0 / width)
    for q in range(4):
        at = slice(q * shard, (q + 1) * shard)
        d_tokens_ref[:, at] = (
            d_mid_ref[:, at] + scale * (acc_v[q] * gain_ref[:, at]) - values[:, at] * scale**3 * inner
        ).astype(BF)
    copies.finish(arrived)


def finish(dq, kv, act, small, attn, branch, pieces, x, d_middle, gain):
    rows, width = act.shape
    piece = width // 16
    vmem = pl.BlockSpec(memory_space=pltpu.VMEM)
    scratch = pltpu.VMEM
    return pl.pallas_call(
        finish_kernel,
        out_shape=(
            jax.ShapeDtypeStruct(x.shape, BF),
            jax.ShapeDtypeStruct((4, 8, piece, 384 + WIDTH), BF),
        ),
        in_specs=[vmem, ANY, vmem, vmem, ANY, vmem] + [ANY] * 4 + [vmem] * 3,
        out_specs=(vmem, ANY),
        scratch_shapes=[
            scratch(kv.shape, BF),
            scratch((8, rows // 8, 384), BF),
            scratch((8, rows // 8, 384), BF),
            scratch((4, 4, piece, 384), BF),
            scratch((4, 4, piece, 384), BF),
            scratch((4, 4, piece, WIDTH), BF),
            scratch((4, 4, piece, WIDTH), BF),
            scratch((8,) + attn.shape, BF),
            scratch((width, rows), BF),
            scratch((piece, 384 + WIDTH), BF),
            scratch((4,) + pieces[0].shape, BF),
            scratch((4, rows // 8, width // 4), F32),
            pltpu.SemaphoreType.DMA((74,)),
            pltpu.SemaphoreType.DMA((74,)),
            pltpu.SemaphoreType.DMA((10,)),
        ],
        compiler_params=pltpu.CompilerParams(collective_id=3, has_side_effects=True, vmem_limit_bytes=52 * 2**20),
        cost_estimate=pl.CostEstimate(flops=3 * 10**9, bytes_accessed=10**8, transcendentals=0),
        name="finish",
    )(dq, kv, act, small, attn, branch, *pieces, x, d_middle, gain.reshape(1, width))


def swap(x, groups, axis="ctx"):
    return lax.all_to_all(x, axis, 0, 0, axis_index_groups=groups, tiled=True)


def rms_scale(values):
    return lax.rsqrt(jnp.mean(values * values, axis=-1, keepdims=True) + EPSILON)


def body(
    tokens,
    lengths,
    deal,
    expert_ids,
    gain_attn,
    w_qkv,
    w_out,
    gain_moe,
    w_router,
    w_gate,
    w_up,
    w_down,
    cotangent,
):
    stream = lax.axis_index("wsh")
    index = lax.axis_index("ctx")
    place = turned(index)
    rows, width = tokens.shape[1], tokens.shape[2]
    shard = w_qkv.shape[0]
    experts_count = w_router.shape[1]
    capacity = 2 * rows * TOP // experts_count
    head = place % 8
    head_row = place // 8
    lengths_row = lax.dynamic_index_in_dim(lengths, stream, 0, keepdims=False)
    deal_row = lax.dynamic_index_in_dim(deal, stream, 0, keepdims=False)
    blocks = deal_row.shape[0]
    deal_row = deal_row.reshape(4, 2, 4, 2).transpose(2, 1, 0, 3).reshape(blocks)
    block_ids = jnp.arange(blocks, dtype=jnp.int32)
    inverse = jnp.sum(jnp.where(deal_row[None, :] == block_ids[:, None], block_ids[None, :], 0), axis=1)
    own_blocks = lax.dynamic_slice_in_dim(deal_row, head_row * 16, 16)
    meta = jnp.concatenate([inverse, own_blocks, jnp.cumsum(lengths_row)]).astype(jnp.int32)

    q_columns = QUERY_HEADS * HEAD_SIZE
    by_head, own_out, expert_shard = prepare(w_qkv, w_router, w_out, w_gate, w_up, w_down)
    own_gains = jnp.concatenate(
        [gain_attn.astype(BF)[None], gain_moe.astype(BF)[None], jnp.zeros((14, shard), BF)], axis=0
    )
    group_tokens, head_full, gains, full_out = gather_rows(tokens[0], by_head, own_gains, own_out)
    head_full = head_full.reshape(width, -1)
    head_weight = head_full[:, :HEAD_COLUMNS]
    full_router = head_full[:, HEAD_COLUMNS : HEAD_COLUMNS + experts_count]
    gain_first = gains[:, 0].reshape(width).astype(F32)
    gain_second = gains[:, 1].reshape(width).astype(F32)
    full_out = full_out.reshape(q_columns, width)

    expert_shard, gains = lax.optimization_barrier((expert_shard, gains))
    expert_all = lax.all_gather(expert_shard, ("ctx", "wsh"), axis_index_groups=OWNERS)

    group_x = group_tokens.reshape(8 * rows, width).astype(F32)
    group_act = (group_x * rms_scale(group_x) * gain_first).astype(BF)
    head_qkv = dot(group_act, head_weight).astype(BF)
    kv_all = gather_keys(head_qkv[:, WIDTH:]).reshape(32 * rows, 2 * HEAD_SIZE)
    head_q = head_qkv[:, :WIDTH]
    head_attn, lse = run_forward(meta, head_q, kv_all)
    by_head, head_attn = lax.optimization_barrier((by_head, head_attn))
    far_qkv = lax.ppermute(by_head, ("ctx", "wsh"), NEXT_Z)
    near_qkv = lax.ppermute(by_head, "wsh", OTHER_CORE)
    head_blocks = head_attn.reshape(8, rows, WIDTH)
    flat_ids = expert_ids[0].reshape(-1)
    expert_range = jnp.arange(experts_count, dtype=jnp.int32)
    assign_hot = (flat_ids[:, None] == expert_range[None, :]).astype(jnp.int32)
    ranks = jnp.sum((jnp.cumsum(assign_hot, axis=0) - 1) * assign_hot, axis=1)
    slots = (flat_ids * capacity + ranks).reshape(rows, TOP)
    output_rows, d_middle, small_term, head_d_attn, branch_part, half_sum, side_sum = run_middle(
        head_blocks, tokens[0], cotangent[0], full_out, head_full, gain_second, expert_ids[0], slots, expert_all
    )
    head_d_attn = head_d_attn.reshape(8 * rows, WIDTH)
    head_d_attn, far_qkv, near_qkv = lax.optimization_barrier((head_d_attn, far_qkv, near_qkv))
    qkv_pieces = [by_head, near_qkv, far_qkv, lax.ppermute(far_qkv, "wsh", OTHER_CORE)]

    half, side = index % 2, stream // 2

    def part_of(terms, which):
        return lax.dynamic_index_in_dim(terms, which, 1, keepdims=False)

    half_got = lax.ppermute(part_of(half_sum, 1 - side), "wsh", OTHER_SIDE)
    side_got = lax.ppermute(part_of(side_sum, 1 - half), "ctx", OTHER_HALF)
    d_q, d_kv = run_backward(meta, head_q, kv_all, head_attn, lse, head_d_attn)
    d_tokens, gathered = finish(
        d_q,
        d_kv.reshape(4, 8 * rows, 2 * HEAD_SIZE),
        group_act,
        small_term,
        head_blocks,
        branch_part.reshape(8 * rows, WIDTH),
        qkv_pieces,
        tokens[0],
        d_middle,
        gain_first,
    )
    gathered, half_got, side_got = lax.optimization_barrier((gathered, half_got, side_got))
    expert_own = jnp.concatenate(
        [
            part_of(half_sum, side).astype(F32) + half_got.astype(F32),
            part_of(side_sum, half).astype(F32) + side_got.astype(F32),
        ],
        axis=1,
    )
    d_w_qkv, d_w_out, rest = assemble(gathered, w_qkv)
    d_gain_first = rest[:, experts_count + 1] / gain_attn.astype(BF).astype(F32)
    return (
        output_rows[None],
        d_tokens[None],
        d_gain_first,
        d_w_qkv,
        d_w_out,
        rest[:, experts_count],
        rest[:, :experts_count],
        expert_own[0][None],
        expert_own[1][None],
        expert_own[2].T[None],
    )


def solution(mesh):
    placed = (
        P("wsh", "ctx", None),
        P(),
        P(),
        P("wsh", "ctx", None),
        P("wsh"),
        P("wsh", None),
        P("wsh", None),
        P("wsh"),
        P("wsh", None),
        P("ctx", "wsh", None),
        P("ctx", "wsh", None),
        P("ctx", None, "wsh"),
        P("wsh", "ctx", None),
    )
    return jax.shard_map(
        body,
        mesh=mesh,
        in_specs=placed,
        out_specs=(
            P("wsh", "ctx", None),
            P("wsh", "ctx", None),
            P("wsh"),
            P("wsh", None),
            P("wsh", None),
            P("wsh"),
            P("wsh", None),
            P("ctx", "wsh", None),
            P("ctx", "wsh", None),
            P("ctx", None, "wsh"),
        ),
        check_vma=False,
    )
```

```python
import functools

import jax
import jax.numpy as jnp
from jax import lax
from jax.experimental import pallas as pl
from jax.experimental.pallas import tpu as pltpu
from jax.sharding import PartitionSpec as P

QUERY_HEADS = 24
KEY_VALUE_HEADS = 8
HEAD_SIZE = 64
GROUP = QUERY_HEADS // KEY_VALUE_HEADS
TOP = 2
BLOCK = 64
WIDTH = GROUP * HEAD_SIZE
HEAD_COLUMNS = WIDTH + 2 * HEAD_SIZE
CHUNK = 512
LANES = 3
TURN = 256

EPSILON = 1e-05
NEG_BIG = -1e30
BF = jnp.bfloat16
F32 = jnp.float32

def turned(index):
    return index % 4 * 8 + index // 4 % 2 * 4 + index // 8


ROW = [[turned(y * 8 + r) for r in range(8)] for y in range(4)]
OWNERS = [[(2 * e + k) * 4 + w for k in range(2) for w in range(4)] for e in range(16)]
OTHER_HALF = [(c, c ^ 1) for c in range(32)]
OTHER_SIDE = [(w, w ^ 2) for w in range(4)]
OTHER_CORE = [(w, w ^ 1) for w in range(4)]
NEXT_Z = [(c * 4 + w, (c ^ 4) * 4 + (w ^ 2)) for c in range(32) for w in range(4)]

def dot(a, b, dims=((1,), (0,))):
    return lax.dot_general(a, b, (dims, ((), ())), preferred_element_type=F32)


NT = ((1,), (1,))
TN = ((0,), (0,))


def block_range(meta, b):
    base = meta[BLOCK + b] * BLOCK
    lane = lax.broadcasted_iota(jnp.int32, (1, WIDTH), 1)
    query = base + (lane & (BLOCK - 1))
    start = jnp.zeros((1, WIDTH), jnp.int32)
    first = jnp.int32(0)
    for i in range(3):
        bound = meta[80 + i]
        start = jnp.where(query >= bound, bound, start)
        first = jnp.where(base >= bound, bound, first)
    first = (first // 128) * 128
    count = (base + BLOCK - first + CHUNK - 1) // CHUNK
    return query, start, first, count


def list_work(meta, blocks, block_s, key_s):
    def one(b, n):
        _, _, first, count = block_range(meta, b)

        def put(i, n):
            block_s[n] = b
            key_s[n] = first + i * CHUNK
            return n + 1

        return lax.fori_loop(0, count, put, n)

    total = lax.fori_loop(0, blocks, one, jnp.int32(0))
    for i in range(LANES):
        block_s[total + i] = blocks
        key_s[total + i] = 0
    return (total + LANES - 1) // LANES


def allowed_of(key_start, query, start):
    key = key_start + lax.broadcasted_iota(jnp.int32, (CHUNK, WIDTH), 0)
    return (key <= query) & (key >= start)


def stack_heads(rows):
    return jnp.concatenate([rows[:, g * HEAD_SIZE : (g + 1) * HEAD_SIZE] for g in range(GROUP)], axis=0)


def sort_blocks(meta, kv_ref, sorted_ref):
    total = kv_ref.shape[0]

    def one(p, carry):
        source = pl.multiple_of(meta[p] * BLOCK, BLOCK)
        target = pl.multiple_of(p * BLOCK, BLOCK)
        sorted_ref[pl.ds(target, BLOCK), :] = kv_ref[pl.ds(source, BLOCK), :]
        return carry

    lax.fori_loop(0, total // BLOCK, one, 0, unroll=8)
    sorted_ref[total:, :] = jnp.zeros((CHUNK, sorted_ref.shape[1]), sorted_ref.dtype)


def transpose_all(sorted_ref, turned_ref):
    steps = sorted_ref.shape[0] // TURN

    def one(i, carry):
        at = pl.multiple_of(i * TURN, TURN)
        turned_ref[:, pl.ds(at, TURN)] = sorted_ref[pl.ds(at, TURN), :].T
        return carry

    lax.fori_loop(0, steps, one, 0)


def attention_forward(
    meta, q_ref, kv_ref, o_ref, lse_ref,
    sorted_ref, turned_ref, pad_ref, query_ref, start_ref, top_ref, total_ref, acc_ref, block_s, key_s,
):
    blocks = q_ref.shape[0] // BLOCK
    sort_blocks(meta, kv_ref, sorted_ref)
    transpose_all(sorted_ref, turned_ref)
    share = list_work(meta, blocks, block_s, key_s)
    zeros = jnp.zeros((WIDTH, HEAD_SIZE), BF)
    top_ref[...] = jnp.full(top_ref.shape, NEG_BIG, F32)
    total_ref[...] = jnp.zeros_like(total_ref)
    acc_ref[...] = jnp.zeros_like(acc_ref)
    query_ref[blocks] = jnp.full((1, WIDTH), -1, jnp.int32)
    start_ref[blocks] = jnp.zeros((1, WIDTH), jnp.int32)
    pad_ref[blocks] = jnp.zeros((WIDTH, 2 * HEAD_SIZE), BF)

    def prepare_block(b, carry):
        query_ref[b], start_ref[b], _, _ = block_range(meta, b)
        at = pl.multiple_of(b * BLOCK, BLOCK)
        rows = stack_heads(q_ref[pl.ds(at, BLOCK), :]) * jnp.asarray(HEAD_SIZE**-0.5, BF)
        pad_ref[b] = jnp.concatenate([rows, zeros], axis=1)
        return carry

    lax.fori_loop(0, blocks, prepare_block, 0, unroll=4)

    def work(i, carry):
        blocks_now = [block_s[lane * share + i] for lane in range(LANES)]
        starts_now = [pl.multiple_of(key_s[lane * share + i], 128) for lane in range(LANES)]
        results = []
        for b, key_start in zip(blocks_now, starts_now):
            scores = dot(sorted_ref[pl.ds(key_start, CHUNK), :], pad_ref[b], NT)
            scores = jnp.where(allowed_of(key_start, query_ref[b], start_ref[b]), scores, NEG_BIG)
            top = top_ref[b]
            top_new = jnp.maximum(top, jnp.max(scores, axis=0, keepdims=True))
            weights = jnp.exp(scores - top_new)
            fade = jnp.exp(top - top_new)
            total = total_ref[b] * fade + jnp.sum(weights, axis=0, keepdims=True)
            values = turned_ref[HEAD_SIZE:, pl.ds(key_start, CHUNK)]
            results.append((top_new, total, acc_ref[b] * fade + dot(values, weights.astype(BF))))
        for b, (top, total, acc) in zip(blocks_now, results):
            top_ref[b] = top
            total_ref[b] = total
            acc_ref[b] = acc
        return carry

    lax.fori_loop(0, share, work, 0)

    def finish_block(b, carry):
        at = pl.multiple_of(b * BLOCK, BLOCK)
        total = total_ref[b]
        lse_ref[b] = top_ref[b] + jnp.log(total)
        result = (acc_ref[b] / total).T.astype(BF)
        o_ref[pl.ds(at, BLOCK), :] = jnp.concatenate(
            [result[g * BLOCK : (g + 1) * BLOCK] for g in range(GROUP)], axis=1
        )
        return carry

    lax.fori_loop(0, blocks, finish_block, 0, unroll=4)


def attention_backward(
    meta, q_ref, kv_ref, o_ref, lse_ref, do_ref, dq_ref, dkv_ref,
    sorted_ref, turned_ref, total_ref, both_ref, query_ref, start_ref, delta_ref, acc_ref, block_s, key_s,
):
    blocks = q_ref.shape[0] // BLOCK
    sort_blocks(meta, kv_ref, sorted_ref)
    transpose_all(sorted_ref, turned_ref)
    share = list_work(meta, blocks, block_s, key_s)
    total_ref[...] = jnp.zeros_like(total_ref)
    acc_ref[...] = jnp.zeros_like(acc_ref)
    query_ref[blocks] = jnp.full((1, WIDTH), -1, jnp.int32)
    start_ref[blocks] = jnp.zeros((1, WIDTH), jnp.int32)
    delta_ref[blocks] = jnp.zeros((1, WIDTH), F32)
    both_ref[blocks] = jnp.zeros((2 * WIDTH, 2 * HEAD_SIZE), BF)
    zeros = jnp.zeros((WIDTH, HEAD_SIZE), BF)
    scaling = HEAD_SIZE**-0.5

    def prepare_block(b, carry):
        query_ref[b], start_ref[b], _, _ = block_range(meta, b)
        at = pl.multiple_of(b * BLOCK, BLOCK)
        rows = stack_heads(q_ref[pl.ds(at, BLOCK), :]) * jnp.asarray(scaling, BF)
        grad = stack_heads(do_ref[pl.ds(at, BLOCK), :])
        value = stack_heads(o_ref[pl.ds(at, BLOCK), :])
        delta_ref[b] = jnp.sum((grad.astype(F32) * value.astype(F32)).T, axis=0, keepdims=True)
        both_ref[b, :WIDTH] = jnp.concatenate([rows, zeros], axis=1)
        both_ref[b, WIDTH:] = jnp.concatenate([zeros, grad], axis=1)
        return carry

    lax.fori_loop(0, blocks, prepare_block, 0, unroll=4)

    def work(i, carry):
        blocks_now = [block_s[lane * share + i] for lane in range(LANES)]
        starts_now = [pl.multiple_of(key_s[lane * share + i], 128) for lane in range(LANES)]
        results = []
        for b, key_start in zip(blocks_now, starts_now):
            keys = sorted_ref[pl.ds(key_start, CHUNK), :]
            scores = dot(keys, both_ref[b, :WIDTH], NT)
            d_probs = dot(keys, both_ref[b, WIDTH:], NT)
            allowed = allowed_of(key_start, query_ref[b], start_ref[b])
            probs = jnp.where(allowed, jnp.exp(scores - lse_ref[b]), 0.0)
            d_scores = (probs * (d_probs - delta_ref[b])).astype(BF)
            joined = jnp.concatenate([d_scores, probs.astype(BF)], axis=1)
            turned = turned_ref[:HEAD_SIZE, pl.ds(key_start, CHUNK)]
            results.append((acc_ref[b] + dot(turned, d_scores), dot(joined, both_ref[b])))
        for b, key_start, (acc, d_keys) in zip(blocks_now, starts_now, results):
            acc_ref[b] = acc
            total_ref[pl.ds(key_start, CHUNK), :] += d_keys
        return carry

    lax.fori_loop(0, share, work, 0)

    def finish_block(b, carry):
        at = pl.multiple_of(b * BLOCK, BLOCK)
        result = (acc_ref[b] * scaling).T.astype(BF)
        dq_ref[pl.ds(at, BLOCK), :] = jnp.concatenate(
            [result[g * BLOCK : (g + 1) * BLOCK] for g in range(GROUP)], axis=1
        )
        return carry

    lax.fori_loop(0, blocks, finish_block, 0, unroll=4)

    def back(p, carry):
        target = pl.multiple_of(meta[p] * BLOCK, BLOCK)
        source = pl.multiple_of(p * BLOCK, BLOCK)
        dkv_ref[pl.ds(target, BLOCK), :] = total_ref[pl.ds(source, BLOCK), :].astype(BF)
        return carry

    lax.fori_loop(0, kv_ref.shape[0] // BLOCK, back, 0, unroll=8)


def local_call(kernel, outs, n_vmem, scratch, name):
    return pl.pallas_call(
        kernel,
        out_shape=outs,
        in_specs=[pl.BlockSpec(memory_space=pltpu.SMEM)] + [pl.BlockSpec(memory_space=pltpu.VMEM)] * n_vmem,
        out_specs=tuple(pl.BlockSpec(memory_space=pltpu.VMEM) for _ in outs),
        scratch_shapes=scratch,
        compiler_params=pltpu.CompilerParams(vmem_limit_bytes=40 * 2**20),
        cost_estimate=pl.CostEstimate(flops=4 * 10**9, bytes_accessed=10**7, transcendentals=4 * 10**6),
        name=name,
    )


def work_scratch(rows, keys):
    blocks = rows // BLOCK
    most = blocks * (keys // CHUNK + 1) + LANES
    return [pltpu.SMEM((most,), jnp.int32), pltpu.SMEM((most,), jnp.int32)]


def run_forward(meta, q, kv):
    rows, keys = q.shape[0], kv.shape[0]
    blocks = rows // BLOCK
    line = (blocks + 1, 1, WIDTH)
    return local_call(
        attention_forward,
        (jax.ShapeDtypeStruct((rows, WIDTH), BF), jax.ShapeDtypeStruct(line, F32)),
        2,
        [
            pltpu.VMEM((keys + CHUNK, 2 * HEAD_SIZE), BF),
            pltpu.VMEM((2 * HEAD_SIZE, keys + CHUNK), BF),
            pltpu.VMEM((blocks + 1, WIDTH, 2 * HEAD_SIZE), BF),
            pltpu.VMEM(line, jnp.int32),
            pltpu.VMEM(line, jnp.int32),
            pltpu.VMEM(line, F32),
            pltpu.VMEM(line, F32),
            pltpu.VMEM((blocks + 1, HEAD_SIZE, WIDTH), F32),
        ]
        + work_scratch(rows, keys),
        "attention_forward",
    )(meta, q, kv)


def run_backward(meta, q, kv, o, lse, d_o):
    rows, keys = q.shape[0], kv.shape[0]
    blocks = rows // BLOCK
    line = (blocks + 1, 1, WIDTH)
    return local_call(
        attention_backward,
        (jax.ShapeDtypeStruct((rows, WIDTH), BF), jax.ShapeDtypeStruct((keys, 2 * HEAD_SIZE), BF)),
        5,
        [
            pltpu.VMEM((keys + CHUNK, 2 * HEAD_SIZE), BF),
            pltpu.VMEM((2 * HEAD_SIZE, keys + CHUNK), BF),
            pltpu.VMEM((keys + CHUNK, 2 * HEAD_SIZE), F32),
            pltpu.VMEM((blocks + 1, 2 * WIDTH, 2 * HEAD_SIZE), BF),
            pltpu.VMEM(line, jnp.int32),
            pltpu.VMEM(line, jnp.int32),
            pltpu.VMEM(line, F32),
            pltpu.VMEM((blocks + 1, HEAD_SIZE, WIDTH), F32),
        ]
        + work_scratch(rows, keys),
        "attention_backward",
    )(meta, q, kv, o, lse, d_o)


def assemble_kernel(pieces_ref, weight_ref, qkv_ref, out_ref, rest_ref):
    parts = [pieces_ref[0, i].astype(F32) for i in range(8)]
    ends = (0, WIDTH, WIDTH + HEAD_SIZE, HEAD_COLUMNS)
    d_qkv = jnp.concatenate([t[:, a:b] for a, b in zip(ends[:-1], ends[1:]) for t in parts], axis=1)
    qkv_ref[...] = d_qkv
    gain_part = jnp.sum(d_qkv * weight_ref[...].astype(BF).astype(F32), axis=1, keepdims=True)
    out_ref[...] = jnp.concatenate([t[:, 384:] for t in parts], axis=1)
    tail = parts[0]
    for t in parts[1:]:
        tail = tail + t
    lane = lax.broadcasted_iota(jnp.int32, rest_ref.shape, 1)
    rest_ref[...] = jnp.where(lane == 17, gain_part, tail[:, HEAD_COLUMNS:384])


def assemble(gathered, weight):
    _, _, piece, columns = gathered.shape

    def by_rows(n):
        return pl.BlockSpec((piece, n), lambda i: (i, 0))

    return pl.pallas_call(
        assemble_kernel,
        out_shape=(
            jax.ShapeDtypeStruct((4 * piece, 8 * HEAD_COLUMNS), F32),
            jax.ShapeDtypeStruct((4 * piece, 8 * WIDTH), F32),
            jax.ShapeDtypeStruct((4 * piece, 64), F32),
        ),
        grid=(4,),
        in_specs=[pl.BlockSpec((1, 8, piece, columns), lambda i: (i, 0, 0, 0)), by_rows(weight.shape[1])],
        out_specs=(by_rows(8 * HEAD_COLUMNS), by_rows(8 * WIDTH), by_rows(64)),
        compiler_params=pltpu.CompilerParams(vmem_limit_bytes=40 * 2**20),
        name="assemble",
    )(gathered, weight)


MESH = pl.DeviceIdType.MESH
ANY = pl.BlockSpec(memory_space=pl.ANY)


class Copies:
    def __init__(self, send, recv, local):
        self.send, self.recv, self.local = send, recv, local
        self.remote_count = self.local_count = 0
        self.started, self.kept, self.left = [], [], []

    def to(self, source, target, device):
        k = self.remote_count
        self.remote_count += 1
        copy = pltpu.make_async_remote_copy(
            source, target, self.send.at[k], self.recv.at[k], device_id=device, device_id_type=MESH
        )
        copy.start()
        self.started.append(copy)
        return copy

    def keep(self, source, middle, target):
        k = self.local_count
        self.local_count += 2
        first = pltpu.make_async_copy(source, middle, self.local.at[k])
        first.start()
        self.kept.append((first, pltpu.make_async_copy(middle, target, self.local.at[k + 1])))

    def move_kept(self):
        for first, second in self.kept:
            first.wait()
            second.start()

    def sent(self, several):
        for copy in several:
            copy.wait_send()
            self.left.append(copy)

    def finish(self, arrived):
        for copy in self.started:
            if not any(copy is other for other in self.left):
                copy.wait_send()
            if not any(copy is other for other in arrived):
                copy.wait_recv()
        for _, second in self.kept:
            second.wait()


def meet(devices):
    barrier = pltpu.get_barrier_semaphore()
    for device in devices:
        pl.semaphore_signal(barrier, inc=1, device_id=device, device_id_type=MESH)
    pl.semaphore_wait(barrier, len(devices))


def gather_rows_kernel(
    tok_ref, wp_ref, gain_ref, wo_ref, tok_out, wp_out, gain_out, wo_out, v_tok, v_wp, v_gain, v_wo, send, recv, local
):
    index, stream = lax.axis_index("ctx"), lax.axis_index("wsh")
    place, parity = turned(index), index % 2
    beside = {"ctx": index + 1 - 2 * parity}
    x, z = place % 4, (place // 4) % 2
    right, left = {"ctx": turned(place - x + (x + 1) % 4)}, {"ctx": turned(place - x + (x + 3) % 4)}
    across = place + 4 - 8 * z
    other = {"wsh": stream + 1 - 2 * (stream % 2)}
    far = {"ctx": turned(across), "wsh": (stream + 2) % 4}
    meet([right, left, {"ctx": turned(across)}, other, far, beside])
    copies = Copies(send, recv, local)
    half = tok_ref.shape[0] // 2
    own, own_z = z * 4 + x, (1 - z) * 4 + x
    left_id, right_id = z * 4 + (x + 3) % 4, z * 4 + (x + 1) % 4
    left_z, right_z = (1 - z) * 4 + (x + 3) % 4, (1 - z) * 4 + (x + 1) % 4

    def rows(ref, h):
        return ref.at[pl.ds(h * half, half)]

    def spot(block, h):
        return tok_out.at[block, pl.ds(h * half, half)]

    head = place % 8
    far_wp = copies.to(wp_ref.at[across % 8], wp_out.at[stream], far)
    far_gain = copies.to(gain_ref, gain_out.at[stream], far)
    cross = [copies.to(rows(tok_ref, h), spot(own, h), {"ctx": turned(across)}) for h in range(2)]
    to_right = [copies.to(rows(tok_ref, h), spot(own, h), right) for h in (0, 1)]
    to_left = [copies.to(rows(tok_ref, h), spot(own, h), left) for h in (1, 0)]
    copies.to(wp_ref.at[head], wp_out.at[stream], other)
    copies.to(gain_ref, gain_out.at[stream], other)
    part = wo_ref.shape[0] // 4

    def half_of(side):
        return [pl.ds(pl.multiple_of((2 * side + i) * part, part), part) for i in range(2)]

    parts, rest = half_of(parity), half_of(1 - parity)
    far_wo = [copies.to(wo_ref.at[p], wo_out.at[stream, p], far) for p in parts]
    copies.to(wo_ref, wo_out.at[stream], other)
    copies.keep(tok_ref, v_tok, tok_out.at[own])
    copies.keep(wp_ref.at[head], v_wp, wp_out.at[stream])
    copies.keep(gain_ref, v_gain, gain_out.at[stream])
    copies.keep(wo_ref, v_wo, wo_out.at[stream])
    copies.move_kept()

    arrived = []

    def arrive(copy):
        copy.wait_recv()
        arrived.append(copy)

    far_stream = (stream + 2) % 4
    arrive(far_wp)
    copies.to(wp_out.at[far_stream], wp_out.at[far_stream], other)
    arrive(far_gain)
    copies.to(gain_out.at[far_stream], gain_out.at[far_stream], other)
    arrive(to_right[0])
    copies.to(spot(left_id, 0), spot(left_id, 0), right)
    arrive(to_left[0])
    copies.to(spot(right_id, 1), spot(right_id, 1), left)
    arrive(cross[0])
    arrive(cross[1])
    z_right = [copies.to(spot(own_z, h), spot(own_z, h), right) for h in (0, 1)]
    z_left = [copies.to(spot(own_z, h), spot(own_z, h), left) for h in (1, 0)]
    beside_wo = []

    def hand_on(i):
        at = wo_out.at[far_stream, parts[i]]
        arrive(far_wo[i])
        beside_wo.append(copies.to(at, at, beside))
        copies.to(at, at, other)

    hand_on(0)
    arrive(z_right[0])
    copies.to(spot(left_z, 0), spot(left_z, 0), right)
    arrive(z_left[0])
    copies.to(spot(right_z, 1), spot(right_z, 1), left)
    hand_on(1)
    for p, copy in zip(rest, beside_wo):
        arrive(copy)
        copies.to(wo_out.at[far_stream, p], wo_out.at[far_stream, p], other)
    copies.finish(arrived)


def gather_rows(tok, wp, gain, wo):
    return pl.pallas_call(
        gather_rows_kernel,
        out_shape=(
            jax.ShapeDtypeStruct((8,) + tok.shape, BF),
            jax.ShapeDtypeStruct((4,) + wp.shape[1:], BF),
            jax.ShapeDtypeStruct((4,) + gain.shape, BF),
            jax.ShapeDtypeStruct((4,) + wo.shape, BF),
        ),
        in_specs=[ANY] * 4,
        out_specs=(ANY,) * 4,
        scratch_shapes=[
            pltpu.VMEM(tok.shape, BF),
            pltpu.VMEM(wp.shape[1:], BF),
            pltpu.VMEM(gain.shape, BF),
            pltpu.VMEM(wo.shape, BF),
            pltpu.SemaphoreType.DMA((29,)),
            pltpu.SemaphoreType.DMA((29,)),
            pltpu.SemaphoreType.DMA((8,)),
        ],
        compiler_params=pltpu.CompilerParams(collective_id=1, has_side_effects=True, vmem_limit_bytes=40 * 2**20),
        name="gather_rows",
    )(tok, wp, gain, wo)


def gather_keys_kernel(kv_ref, kv_out, v_kv, send, recv, local):
    place = turned(lax.axis_index("ctx"))
    y = place // 8
    up, down = {"ctx": turned((place + 8) % 32)}, {"ctx": turned((place + 24) % 32)}
    meet([up, down])
    copies = Copies(send, recv, local)
    half = kv_ref.shape[0] // 2

    def rows(h):
        return kv_ref.at[pl.ds(h * half, half)]

    def spot(block, h):
        return kv_out.at[block, pl.ds(h * half, half)]

    to_up = [copies.to(rows(h), spot(y, h), up) for h in (0, 1)]
    to_down = [copies.to(rows(h), spot(y, h), down) for h in (1, 0)]
    copies.keep(kv_ref, v_kv, kv_out.at[y])
    copies.move_kept()
    to_up[0].wait_recv()
    copies.to(spot((y + 3) % 4, 0), spot((y + 3) % 4, 0), up)
    to_down[0].wait_recv()
    copies.to(spot((y + 1) % 4, 1), spot((y + 1) % 4, 1), down)
    copies.finish([to_up[0], to_down[0]])


def gather_keys(kv):
    return pl.pallas_call(
        gather_keys_kernel,
        out_shape=jax.ShapeDtypeStruct((4,) + kv.shape, BF),
        in_specs=[ANY],
        out_specs=ANY,
        scratch_shapes=[
            pltpu.VMEM(kv.shape, BF),
            pltpu.SemaphoreType.DMA((6,)),
            pltpu.SemaphoreType.DMA((6,)),
            pltpu.SemaphoreType.DMA((2,)),
        ],
        compiler_params=pltpu.CompilerParams(collective_id=2, has_side_effects=True, vmem_limit_bytes=40 * 2**20),
        name="gather_keys",
    )(kv)


FF_STEP = 256


def middle_kernel(
    attn_ref, x_ref, cot_ref, wo_ref, head_ref, gain_ref, choice_ref, slot_ref, slot_t_ref, w_ref,
    out_ref, d_mid_ref, small_ref, d_attn_to, branch_to, half_out, side_out,
    attn_v, wo_v, w_v, x_v, g_v, turned_x, turned_g, out_v, d_in_v, back_v, returned_v, acc_v, gate_v, up_v,
    hidden_v, d_gate_v, d_up_v, got_v, half_got, side_got, mid_v, act_v, d_attn_v, branch_v, send, recv, local,
):
    index, stream = lax.axis_index("ctx"), lax.axis_index("wsh")
    place, mine = turned(index), index // 2
    y, r = place // 8, place % 8
    inner = (index % 4 + 1) // 2 % 2

    def device(p):
        return {"ctx": p // 2 * 4 + (1 - inner) * (3 * (p % 2)) + inner * (1 + p % 2)}

    peers = [(mine + k) % 16 for k in range(1, 16)]
    in_row = [(r + k) % 8 for k in range(1, 8)]
    core, half, side = stream % 2, index % 2, stream // 2
    other = {"wsh": stream + 1 - 2 * core}
    other_half, other_side = {"ctx": index + 1 - 2 * half}, {"wsh": (stream + 2) % 4}
    meet([device(p) for p in peers] + [other, other_half, other_side])
    copies = Copies(send, recv, local)
    width, rows = turned_x.shape
    tokens = x_ref.shape[0]
    quarter = width // 4
    own, arrived = [], []

    def here(source, target):
        copy = pltpu.make_async_copy(source, target, local.at[len(own)])
        copy.start()
        own.append(copy)
        return copy

    def arrive(several):
        for copy in several:
            copy.wait_recv()
            arrived.append(copy)

    attn_came = [copies.to(attn_ref.at[pr], attn_v.at[r], {"ctx": turned(8 * y + pr)}) for pr in in_row]
    own_attn = here(attn_ref.at[r], attn_v.at[r])
    own_wo = here(wo_ref, wo_v)
    weights = [
        here(w_ref.at[4 * k + q, m], w_v.at[k, m, pl.ds(q * quarter, quarter)])
        for k in range(2)
        for q in range(4)
        for m in range(3)
    ]
    lanes = lax.broadcasted_iota(jnp.int32, (tokens, 64), 1)
    chosen = [choice_ref[:, j : j + 1] == lanes for j in range(TOP)]
    slot_rows = lax.broadcasted_iota(jnp.int32, (rows, tokens), 0)
    to_slot = [jnp.where(slot_t_ref[j : j + 1, :] == slot_rows, 1.0, 0.0).astype(BF) for j in range(TOP)]
    own_attn.wait()
    own_wo.wait()
    arrive(attn_came)
    middle = x_ref[...].astype(F32)
    for i in range(4):
        pair = jnp.concatenate([attn_v[2 * i], attn_v[2 * i + 1]], axis=1)
        middle += dot(pair, wo_v[i * quarter : (i + 1) * quarter, :])
    mid_v[...] = middle
    scale = rms_scale(middle)
    act = (middle * scale * gain_ref[...]).astype(BF)
    act_v[...] = act
    out_v[...] = dot(to_slot[0] + to_slot[1], act).astype(BF).reshape(out_v.shape)
    came = [copies.to(out_v.at[p], x_v.at[mine], device(p)) for p in peers]
    own_x = here(out_v.at[mine], x_v.at[mine])
    logits = dot(act, head_ref[:, HEAD_COLUMNS:])
    picked = [jnp.sum(jnp.where(c, logits, 0.0), axis=-1, keepdims=True) for c in chosen]
    top = jnp.maximum(picked[0], picked[1])
    powers = [jnp.exp(p - top) for p in picked]
    gates = [p / (powers[0] + powers[1]) for p in powers]
    gated = jnp.concatenate([(g * cot_ref[...].astype(F32)).astype(BF) for g in gates], axis=0)
    d_in_v[...] = dot(jnp.concatenate(to_slot, axis=1), gated).astype(BF).reshape(d_in_v.shape)
    came_g = [copies.to(d_in_v.at[p], g_v.at[mine], device(p)) for p in peers]
    own_g = here(d_in_v.at[mine], g_v.at[mine])

    for copy in weights:
        copy.wait()
    arrive(came)
    own_x.wait()
    steps = w_v.shape[3] // FF_STEP
    acc_v[...] = jnp.zeros_like(acc_v)

    def forward(i, carry):
        k, at = i // steps, pl.ds(pl.multiple_of(i % steps * FF_STEP, FF_STEP), FF_STEP)
        inputs = x_v[...].reshape(rows, width)
        gate = dot(inputs, w_v[k, 0, :, at])
        up = dot(inputs, w_v[k, 1, :, at])
        hidden = (gate * jax.nn.sigmoid(gate) * up).astype(BF)
        gate_v[i] = gate
        up_v[i] = up
        hidden_v[k, :, at] = hidden
        acc_v[...] += dot(hidden, w_v[k, 2, :, at], NT)
        return carry

    lax.fori_loop(0, 2 * steps, forward, 0)
    copies.sent(came)
    out_v[...] = acc_v[...].astype(BF).reshape(out_v.shape)
    outs = [copies.to(out_v.at[p], back_v.at[mine], device(p)) for p in peers]
    own_back = here(out_v.at[mine], back_v.at[mine])
    for q in range(4):
        at = slice(q * quarter, (q + 1) * quarter)
        turned_x[at, :] = x_v[:, :, at].reshape(rows, quarter).T
    acc_v[...] = jnp.zeros_like(acc_v)
    arrive(came_g)
    own_g.wait()

    def backward(i, carry):
        k, at = i // steps, pl.ds(pl.multiple_of(i % steps * FF_STEP, FF_STEP), FF_STEP)
        d_hidden = dot(g_v[...].reshape(rows, width), w_v[k, 2, :, at])
        gate, up = gate_v[i], up_v[i]
        sigmoid = jax.nn.sigmoid(gate)
        d_gate = (d_hidden * up * sigmoid * (1.0 + gate * (1.0 - sigmoid))).astype(BF)
        d_up = (d_hidden * (gate * sigmoid)).astype(BF)
        d_gate_v[k, :, at] = d_gate
        d_up_v[k, :, at] = d_up
        acc_v[...] += dot(d_gate, w_v[k, 0, :, at], NT) + dot(d_up, w_v[k, 1, :, at], NT)
        return carry

    lax.fori_loop(0, 2 * steps, backward, 0)
    copies.sent(came_g)
    d_in_v[...] = acc_v[...].astype(BF).reshape(d_in_v.shape)
    returns = [copies.to(d_in_v.at[p], returned_v.at[mine], device(p)) for p in peers]
    own_returned = here(d_in_v.at[mine], returned_v.at[mine])
    for q in range(4):
        at = slice(q * quarter, (q + 1) * quarter)
        turned_g[at, :] = g_v[:, :, at].reshape(rows, quarter).T

    def terms(k, z, c):
        at = pl.ds(pl.multiple_of((2 * z + c) * quarter, quarter), quarter)
        part = turned_x[at, :]
        return (
            dot(part, d_gate_v[k]),
            dot(part, d_up_v[k]),
            dot(turned_g[at, :], hidden_v[k]),
        )

    crossing = []
    for dz in (1, 0):
        z = side + dz - 2 * side * dz

        def other_term(k, carry, z=z, dz=dz):
            at = pl.ds(pl.multiple_of((2 * dz + k) * quarter, quarter), quarter)
            for m, term in enumerate(terms(k, z, 1 - core)):
                w_v[0, m, at] = term.astype(BF)
            return carry

        lax.fori_loop(0, 2, other_term, 0)
        at = pl.ds(2 * dz * quarter, 2 * quarter)
        crossing.append(copies.to(w_v.at[0, :, at], got_v.at[:, at], other))
    halfway = quarter // 2
    for dz, copy in zip((1, 0), crossing):
        z = side + dz - 2 * side * dz
        arrive([copy])
        for dk in (1, 0):
            k = half + dk - 2 * half * dk
            got_at = pl.ds(pl.multiple_of((2 * dz + k) * quarter, quarter), quarter)
            z_at = pl.ds(pl.multiple_of(z * halfway, halfway), halfway)
            k_at = pl.ds(pl.multiple_of(quarter + k * halfway, halfway), halfway)
            for m, term in enumerate(terms(k, z, core)):
                total = (term + got_v[m, got_at].astype(F32)).astype(BF)
                if dk:
                    w_v[1, m, z_at] = total[:halfway]
                else:
                    half_out[m, z] = total[:halfway]
                if dz:
                    w_v[1, m, k_at] = total[halfway:]
                else:
                    side_out[m, k] = total[halfway:]
    first = copies.to(w_v.at[1, :, pl.ds(0, quarter)], half_got, other_half)
    second = copies.to(w_v.at[1, :, pl.ds(quarter, quarter)], side_got, other_side)

    slot_lanes = lax.broadcasted_iota(jnp.int32, (tokens, rows), 1)
    of_slot = [jnp.where(slot_ref[:, j : j + 1] == slot_lanes, 1.0, 0.0).astype(BF) for j in range(TOP)]
    own_back.wait()
    arrive(outs)
    back = back_v[...].reshape(rows, width)
    d_out = cot_ref[...].astype(F32)
    total = mid_v[...]
    d_gates = []
    for j in range(TOP):
        both = dot(of_slot[j], back)
        total += gates[j] * both
        d_gates.append(jnp.sum(d_out * both, axis=-1, keepdims=True))
    out_ref[...] = total.astype(BF)
    inner_sum = gates[0] * d_gates[0] + gates[1] * d_gates[1]
    d_logits = 0.0
    for j in range(TOP):
        d_logits += jnp.where(chosen[j], gates[j] * (d_gates[j] - inner_sum), 0.0)
    d_logits = d_logits.astype(BF)
    own_returned.wait()
    arrive(returns)
    d_act = dot(of_slot[0] + of_slot[1], returned_v[...].reshape(rows, width))
    d_act += dot(d_logits, head_ref[:, HEAD_COLUMNS:], NT)
    middle = mid_v[...]
    normed = middle * scale
    spot = jnp.where(lanes == 16, 1.0, 0.0).astype(BF)
    small_ref[...] = (dot(act_v[...].T, d_logits) + dot((d_act * normed).astype(BF).T, spot)).astype(BF)
    scaled = d_act * gain_ref[...]
    d_mid = d_out + scale * (scaled - normed * scale * jnp.mean(scaled * middle, axis=-1, keepdims=True))
    d_mid_ref[...] = d_mid
    d_branch = d_mid.astype(BF)
    for i in range(8):
        branch_v[i] = d_branch[:, i * WIDTH : (i + 1) * WIDTH]
    to_row = [copies.to(branch_v.at[pr], branch_to.at[r], {"ctx": turned(8 * y + pr)}) for pr in in_row]
    for i in range(4):
        pair = dot(d_branch, wo_v[i * quarter : (i + 1) * quarter, :], NT).astype(BF)
        d_attn_v[2 * i] = pair[:, :WIDTH]
        d_attn_v[2 * i + 1] = pair[:, WIDTH:]
    to_row += [copies.to(d_attn_v.at[pr], d_attn_to.at[r], {"ctx": turned(8 * y + pr)}) for pr in in_row]
    own_row = [here(branch_v.at[r], branch_to.at[r]), here(d_attn_v.at[r], d_attn_to.at[r])]
    arrive([first, second])
    for m in range(3):
        for i in range(2):
            at = slice(i * halfway, (i + 1) * halfway)
            half_out[m, i] = (half_out[m, i].astype(F32) + half_got[m, at].astype(F32)).astype(BF)
            side_out[m, i] = (side_out[m, i].astype(F32) + side_got[m, at].astype(F32)).astype(BF)
    copies.finish(arrived)
    own_back = own_row
    for copy in own_back:
        copy.wait()


def run_middle(attn, x, cotangent, w_out, head_full, gain, choice, slots, weights):
    _, tokens, _ = attn.shape
    width = x.shape[1]
    groups, capacity = 16, 2 * TOP * tokens // 16
    rows, half, quarter = groups * capacity, weights.shape[3], width // 4
    steps = 2 * half // FF_STEP
    vmem = pltpu.VMEM
    whole = pl.BlockSpec(memory_space=pltpu.VMEM)
    slot_rows = vmem((groups, capacity, width), BF)
    wide, low = vmem((steps, rows, FF_STEP), F32), vmem((2, rows, half), BF)
    part = jax.ShapeDtypeStruct((3, 2, quarter // 2, half), BF)
    return pl.pallas_call(
        middle_kernel,
        out_shape=(
            jax.ShapeDtypeStruct(x.shape, BF),
            jax.ShapeDtypeStruct(x.shape, F32),
            jax.ShapeDtypeStruct((width, 64), BF),
            jax.ShapeDtypeStruct(attn.shape, BF),
            jax.ShapeDtypeStruct(attn.shape, BF),
            part,
            part,
        ),
        in_specs=[ANY, whole, whole, ANY, whole, whole, whole, whole, whole, ANY],
        out_specs=(whole, whole, whole, ANY, ANY, whole, whole),
        scratch_shapes=[
            vmem(attn.shape, BF),
            vmem(w_out.shape, BF),
            vmem((2, 3, width, half), BF),
            slot_rows,
            slot_rows,
            vmem((width, rows), BF),
            vmem((width, rows), BF),
            slot_rows,
            slot_rows,
            slot_rows,
            slot_rows,
            vmem((rows, width), F32),
            wide,
            wide,
            low,
            low,
            low,
            vmem((3, width, half), BF),
            vmem((3, quarter, half), BF),
            vmem((3, quarter, half), BF),
            vmem(x.shape, F32),
            vmem(x.shape, BF),
            vmem(attn.shape, BF),
            vmem(attn.shape, BF),
            pltpu.SemaphoreType.DMA((85,)),
            pltpu.SemaphoreType.DMA((85,)),
            pltpu.SemaphoreType.DMA((32,)),
        ],
        compiler_params=pltpu.CompilerParams(collective_id=6, has_side_effects=True, vmem_limit_bytes=60 * 2**20),
        cost_estimate=pl.CostEstimate(flops=15 * 10**9, bytes_accessed=10**8, transcendentals=10**6),
        name="middle",
    )(attn, x, cotangent, w_out, head_full, gain.reshape(1, width), choice, slots, slots.T, weights)


def prepare_kernel(qkv_ref, router_ref, wo_ref, gate_ref, up_ref, down_ref, wp_out, wo_out, expert_out):
    rows = qkv_ref.shape[0]
    experts = router_ref.shape[1]
    wo_out[...] = wo_ref[...].astype(BF)
    expert_out[0] = gate_ref[0].astype(BF)
    expert_out[1] = up_ref[0].astype(BF)
    expert_out[2] = down_ref[0].T.astype(BF)
    router = router_ref[...].astype(BF)
    tail = jnp.zeros((rows, wp_out.shape[2] - HEAD_COLUMNS - experts), BF)
    k_at, v_at = QUERY_HEADS * HEAD_SIZE, (QUERY_HEADS + KEY_VALUE_HEADS) * HEAD_SIZE
    for h in range(KEY_VALUE_HEADS):
        wp_out[h] = jnp.concatenate(
            [
                qkv_ref[:, h * WIDTH : (h + 1) * WIDTH].astype(BF),
                qkv_ref[:, k_at + h * HEAD_SIZE : k_at + (h + 1) * HEAD_SIZE].astype(BF),
                qkv_ref[:, v_at + h * HEAD_SIZE : v_at + (h + 1) * HEAD_SIZE].astype(BF),
                router,
                tail,
            ],
            axis=1,
        )


def prepare(w_qkv, w_router, w_out, w_gate, w_up, w_down):
    shard, half = w_gate.shape[1:]
    step = shard // 3

    def block(n):
        return pl.BlockSpec((step, n), lambda i: (i, 0))

    return pl.pallas_call(
        prepare_kernel,
        out_shape=(
            jax.ShapeDtypeStruct((KEY_VALUE_HEADS, shard, 384), BF),
            jax.ShapeDtypeStruct(w_out.shape, BF),
            jax.ShapeDtypeStruct((3, shard, half), BF),
        ),
        grid=(3,),
        in_specs=[
            block(w_qkv.shape[1]),
            block(w_router.shape[1]),
            block(w_out.shape[1]),
            pl.BlockSpec((1, step, half), lambda i: (0, i, 0)),
            pl.BlockSpec((1, step, half), lambda i: (0, i, 0)),
            pl.BlockSpec((1, half, step), lambda i: (0, 0, i)),
        ],
        out_specs=(
            pl.BlockSpec((KEY_VALUE_HEADS, step, 384), lambda i: (0, i, 0)),
            block(w_out.shape[1]),
            pl.BlockSpec((3, step, half), lambda i: (0, i, 0)),
        ),
        compiler_params=pltpu.CompilerParams(vmem_limit_bytes=40 * 2**20),
        name="prepare",
    )(w_qkv, w_router, w_out, w_gate, w_up, w_down)


def finish_kernel(
    dq_ref, kv_ref, act_ref, small_ref, attn_ref, branch_ref, p0, p1, p2, p3, x_ref, d_mid_ref, gain_ref,
    d_tokens_ref, all_out, kv_v, grad_v, grad_to, term_v, term_to, out_v, out_to, attn_v, act_t, own_v, w_v, acc_v,
    send, recv, local,
):
    place, stream = turned(lax.axis_index("ctx")), lax.axis_index("wsh")
    y, r = place // 8, place % 8
    x, z = r % 4, r // 4

    def at_place(p):
        return {"ctx": turned(p)}

    right, left = at_place(place - x + (x + 1) % 4), at_place(place - x + (x + 3) % 4)
    across = at_place(place + 4 - 8 * z)
    up, down, beyond = (at_place((place + 8 * k) % 32) for k in (1, 3, 2))
    others = [((y + k // 4) % 4, (stream + k % 4) % 4) for k in range(1, 16)]
    in_row = [(r + k) % 8 for k in range(1, 8)]
    meet([{"ctx": turned(r + 8 * py), "wsh": pw} for py, pw in others] + [at_place(8 * y + pr) for pr in in_row])
    copies = Copies(send, recv, local)
    rows, width = act_ref.shape
    shard, piece = width // 4, own_v.shape[0]
    arrived = []

    def arrive(*which):
        for copy in which:
            copy.wait_recv()
            arrived.append(copy)

    own = []

    def here(source, target):
        copy = pltpu.make_async_copy(source, target, local.at[len(own)])
        copy.start()
        own.append(copy)
        return copy

    kv_came = [
        copies.to(kv_ref.at[(y + k) % 4], kv_v.at[y], at_place((place + 8 * k) % 32)) for k in (2, 1, 3)
    ]
    own_kv = here(kv_ref.at[y], kv_v.at[y])
    r_z = (1 - z) * 4 + x
    r_left, r_right = z * 4 + (x + 3) % 4, z * 4 + (x + 1) % 4
    z_left, z_right = (1 - z) * 4 + (x + 3) % 4, (1 - z) * 4 + (x + 1) % 4
    front, rear = pl.ds(0, 4), pl.ds(4, 4)

    def pass_on(device, *at):
        return copies.to(attn_v.at[at], attn_v.at[at], device)

    attn_cross = copies.to(attn_ref, attn_v.at[r], across)
    attn_right = copies.to(attn_ref, attn_v.at[r], right)
    attn_left = copies.to(attn_ref, attn_v.at[r], left)
    own_attn = here(attn_ref, attn_v.at[r])
    weights = [here(p, w_v.at[j]) for j, p in enumerate((p0, p1, p2, p3))]
    dq = dq_ref[...]
    for q in range(4):
        act_t[q * shard : (q + 1) * shard, :] = act_ref[:, q * shard : (q + 1) * shard].T
    for q in range(4):
        term = dot(act_t[q * shard : (q + 1) * shard, :], dq).astype(BF)
        for i in range(4):
            term_v[i, q, :, :WIDTH] = term[i * piece : (i + 1) * piece]
            at = q * shard + i * piece
            term_v[i, q, :, HEAD_COLUMNS:] = small_ref[at : at + piece, :]
    arrive(attn_cross)
    attn_far = [pass_on(right, r_z), pass_on(left, r_z)]
    arrive(attn_right)
    attn_on = [pass_on(right, r_left, front)]
    arrive(attn_left)
    attn_on.append(pass_on(left, r_right, rear))
    own_kv.wait()
    arrive(*kv_came)
    total = kv_v[0].astype(F32)
    for i in range(1, 4):
        total = total + kv_v[i].astype(F32)
    kv = total.astype(BF)
    grad_v[...] = jnp.concatenate([dq, kv, jnp.zeros((rows, 64), BF)], axis=1).reshape(grad_v.shape)
    grads = [copies.to(grad_v.at[pr], grad_to.at[r], at_place(8 * y + pr)) for pr in in_row]
    own_grad = here(grad_v.at[r], grad_to.at[r])
    terms = []
    for dw in (2, 3, 1, 0):
        pw = (stream + dw) % 4
        part = act_t[pl.ds(pl.multiple_of(pw * shard, shard), shard), :]
        term = dot(part, kv).astype(BF)
        for i in range(4):
            term_v[i, pw, :, WIDTH:HEAD_COLUMNS] = term[i * piece : (i + 1) * piece]
        for dy in (2, 1, 3, 0):
            py = (y + dy) % 4
            if dw or dy:
                device = {"ctx": turned(r + 8 * py), "wsh": pw}
                terms.append(copies.to(term_v.at[py, pw], term_to.at[y, stream], device))
    own_term = here(term_v.at[y, stream], term_to.at[y, stream])
    arrive(attn_far[0])
    attn_on.append(pass_on(right, z_left, front))
    arrive(attn_far[1])
    attn_on.append(pass_on(left, z_right, rear))
    own_attn.wait()
    arrive(*attn_on)
    branch = branch_ref[...]
    for h in range(8):
        term = dot(attn_v[h].reshape(rows, WIDTH).T, branch).astype(BF)
        for i in range(2):
            n = 2 * h + i
            out_v[n % 4, n // 4] = term[i * piece : (i + 1) * piece]
    outs = []
    for k in (8, 4, 12, 10, 6, 14, 2, 9, 5, 13, 1, 11, 7, 15, 3):
        py, pw = others[k - 1]
        outs.append(copies.to(out_v.at[py, pw], out_to.at[y, stream], {"ctx": turned(r + 8 * py), "wsh": pw}))
    own_out = here(out_v.at[y, stream], out_to.at[y, stream])
    own_term.wait()
    arrive(*terms)
    total = term_to[0, 0].astype(F32)
    for i in range(1, 16):
        total = total + term_to[i // 4, i % 4].astype(F32)
    own_v[:, :384] = total.astype(BF)
    own_out.wait()
    arrive(*outs)
    total = out_to[0, 0].astype(F32)
    for i in range(1, 16):
        total = total + out_to[i // 4, i % 4].astype(F32)
    own_v[:, 384:] = total.astype(BF)

    half = piece // 2
    first, last = pl.ds(0, half), pl.ds(half, half)

    def on(device, *at):
        return copies.to(all_out.at[at], all_out.at[at], device)

    a_cross = copies.to(own_v.at[first], all_out.at[y, r, first], across)
    a_right = copies.to(own_v.at[first], all_out.at[y, r, first], right)
    a_left = copies.to(own_v.at[first], all_out.at[y, r, first], left)
    b_up = copies.to(own_v.at[last], all_out.at[y, r, last], up)
    b_down = copies.to(own_v.at[last], all_out.at[y, r, last], down)
    b_beyond = copies.to(own_v.at[last], all_out.at[y, r, last], beyond)
    keep = here(own_v, all_out.at[y, r])

    for copy in weights:
        copy.wait()
    own_grad.wait()
    arrive(*grads)
    acc_v[...] = jnp.zeros_like(acc_v)
    shards = (stream, stream + 1 - 2 * (stream % 2), (stream + 2) % 4, 3 - stream)

    def heads(start, count):
        def one(h, carry):
            grad = grad_to[h][:, :HEAD_COLUMNS]
            for j in range(4):
                acc_v[shards[j]] += dot(grad, w_v[j, h][:, :HEAD_COLUMNS], NT)
            return carry

        lax.fori_loop(start, start + count, one, 0)

    heads(0, 2)
    keep.wait()
    arrive(a_cross)
    a_z_right = on(right, y, r_z, first)
    a_z_left = on(left, y, r_z, first)
    arrive(a_right)
    a_on = on(right, y, r_left, first)
    arrive(b_up, b_down, b_beyond)
    lower, upper, every = pl.ds(0, 2), pl.ds(2, 2), pl.ds(0, 4)
    b_right = on(right, every, r, last)
    b_left = on(left, every, r, last)
    b_cross = on(across, every, r, last)
    heads(2, 2)
    arrive(a_z_left, a_left)
    a_z_on = on(left, y, z_right, first)
    arrive(a_z_right, a_on, a_z_on)
    low_r, high_r = pl.ds(0, 4), pl.ds(4, 4)
    c_up = [on(up, y, low_r, first), on(up, y, high_r, first)]
    c_down = [on(down, y, high_r, first), on(down, y, low_r, first)]
    heads(4, 2)
    arrive(b_right)
    on(right, lower, r_left, last)
    arrive(b_left)
    on(left, upper, r_right, last)
    arrive(b_cross)
    b_z_right = on(right, every, r_z, last)
    b_z_left = on(left, every, r_z, last)
    arrive(c_up[0])
    on(up, (y + 3) % 4, low_r, first)
    arrive(c_down[0])
    on(down, (y + 1) % 4, high_r, first)
    heads(6, 2)
    arrive(b_z_right)
    on(right, lower, z_left, last)
    arrive(b_z_left)
    on(left, upper, z_right, last)
    values = x_ref[...].astype(F32)
    scale = rms_scale(values)
    inner = 0.0
    for q in range(4):
        at = slice(q * shard, (q + 1) * shard)
        inner += jnp.sum(acc_v[q] * gain_ref[:, at] * values[:, at], axis=-1, keepdims=True)
    inner = inner * (1.0 / width)
    for q in range(4):
        at = slice(q * shard, (q + 1) * shard)
        d_tokens_ref[:, at] = (
            d_mid_ref[:, at] + scale * (acc_v[q] * gain_ref[:, at]) - values[:, at] * scale**3 * inner
        ).astype(BF)
    copies.finish(arrived)


def finish(dq, kv, act, small, attn, branch, pieces, x, d_middle, gain):
    rows, width = act.shape
    piece = width // 16
    vmem = pl.BlockSpec(memory_space=pltpu.VMEM)
    scratch = pltpu.VMEM
    return pl.pallas_call(
        finish_kernel,
        out_shape=(
            jax.ShapeDtypeStruct(x.shape, BF),
            jax.ShapeDtypeStruct((4, 8, piece, 384 + WIDTH), BF),
        ),
        in_specs=[vmem, ANY, vmem, vmem, ANY, vmem] + [ANY] * 4 + [vmem] * 3,
        out_specs=(vmem, ANY),
        scratch_shapes=[
            scratch(kv.shape, BF),
            scratch((8, rows // 8, 384), BF),
            scratch((8, rows // 8, 384), BF),
            scratch((4, 4, piece, 384), BF),
            scratch((4, 4, piece, 384), BF),
            scratch((4, 4, piece, WIDTH), BF),
            scratch((4, 4, piece, WIDTH), BF),
            scratch((8,) + attn.shape, BF),
            scratch((width, rows), BF),
            scratch((piece, 384 + WIDTH), BF),
            scratch((4,) + pieces[0].shape, BF),
            scratch((4, rows // 8, width // 4), F32),
            pltpu.SemaphoreType.DMA((74,)),
            pltpu.SemaphoreType.DMA((74,)),
            pltpu.SemaphoreType.DMA((10,)),
        ],
        compiler_params=pltpu.CompilerParams(collective_id=3, has_side_effects=True, vmem_limit_bytes=52 * 2**20),
        cost_estimate=pl.CostEstimate(flops=3 * 10**9, bytes_accessed=10**8, transcendentals=0),
        name="finish",
    )(dq, kv, act, small, attn, branch, *pieces, x, d_middle, gain.reshape(1, width))


def swap(x, groups, axis="ctx"):
    return lax.all_to_all(x, axis, 0, 0, axis_index_groups=groups, tiled=True)


def rms_scale(values):
    return lax.rsqrt(jnp.mean(values * values, axis=-1, keepdims=True) + EPSILON)


def body(
    tokens,
    lengths,
    deal,
    expert_ids,
    gain_attn,
    w_qkv,
    w_out,
    gain_moe,
    w_router,
    w_gate,
    w_up,
    w_down,
    cotangent,
):
    stream = lax.axis_index("wsh")
    index = lax.axis_index("ctx")
    place = turned(index)
    rows, width = tokens.shape[1], tokens.shape[2]
    shard = w_qkv.shape[0]
    experts_count = w_router.shape[1]
    capacity = 2 * rows * TOP // experts_count
    head = place % 8
    head_row = place // 8
    lengths_row = lax.dynamic_index_in_dim(lengths, stream, 0, keepdims=False)
    deal_row = lax.dynamic_index_in_dim(deal, stream, 0, keepdims=False)
    blocks = deal_row.shape[0]
    deal_row = deal_row.reshape(4, 2, 4, 2).transpose(2, 1, 0, 3).reshape(blocks)
    block_ids = jnp.arange(blocks, dtype=jnp.int32)
    inverse = jnp.sum(jnp.where(deal_row[None, :] == block_ids[:, None], block_ids[None, :], 0), axis=1)
    own_blocks = lax.dynamic_slice_in_dim(deal_row, head_row * 16, 16)
    meta = jnp.concatenate([inverse, own_blocks, jnp.cumsum(lengths_row)]).astype(jnp.int32)

    q_columns = QUERY_HEADS * HEAD_SIZE
    by_head, own_out, expert_shard = prepare(w_qkv, w_router, w_out, w_gate, w_up, w_down)
    own_gains = jnp.concatenate(
        [gain_attn.astype(BF)[None], gain_moe.astype(BF)[None], jnp.zeros((14, shard), BF)], axis=0
    )
    group_tokens, head_full, gains, full_out = gather_rows(tokens[0], by_head, own_gains, own_out)
    head_full = head_full.reshape(width, -1)
    head_weight = head_full[:, :HEAD_COLUMNS]
    full_router = head_full[:, HEAD_COLUMNS : HEAD_COLUMNS + experts_count]
    gain_first = gains[:, 0].reshape(width).astype(F32)
    gain_second = gains[:, 1].reshape(width).astype(F32)
    full_out = full_out.reshape(q_columns, width)

    expert_shard, gains = lax.optimization_barrier((expert_shard, gains))
    expert_all = lax.all_gather(expert_shard, ("ctx", "wsh"), axis_index_groups=OWNERS)

    group_x = group_tokens.reshape(8 * rows, width).astype(F32)
    group_act = (group_x * rms_scale(group_x) * gain_first).astype(BF)
    head_qkv = dot(group_act, head_weight).astype(BF)
    kv_all = gather_keys(head_qkv[:, WIDTH:]).reshape(32 * rows, 2 * HEAD_SIZE)
    head_q = head_qkv[:, :WIDTH]
    head_attn, lse = run_forward(meta, head_q, kv_all)
    by_head, head_attn = lax.optimization_barrier((by_head, head_attn))
    far_qkv = lax.ppermute(by_head, ("ctx", "wsh"), NEXT_Z)
    near_qkv = lax.ppermute(by_head, "wsh", OTHER_CORE)
    head_blocks = head_attn.reshape(8, rows, WIDTH)
    flat_ids = expert_ids[0].reshape(-1)
    expert_range = jnp.arange(experts_count, dtype=jnp.int32)
    assign_hot = (flat_ids[:, None] == expert_range[None, :]).astype(jnp.int32)
    ranks = jnp.sum((jnp.cumsum(assign_hot, axis=0) - 1) * assign_hot, axis=1)
    slots = (flat_ids * capacity + ranks).reshape(rows, TOP)
    output_rows, d_middle, small_term, head_d_attn, branch_part, half_sum, side_sum = run_middle(
        head_blocks, tokens[0], cotangent[0], full_out, head_full, gain_second, expert_ids[0], slots, expert_all
    )
    head_d_attn = head_d_attn.reshape(8 * rows, WIDTH)
    head_d_attn, far_qkv, near_qkv = lax.optimization_barrier((head_d_attn, far_qkv, near_qkv))
    qkv_pieces = [by_head, near_qkv, far_qkv, lax.ppermute(far_qkv, "wsh", OTHER_CORE)]

    half, side = index % 2, stream // 2

    def part_of(terms, which):
        return lax.dynamic_index_in_dim(terms, which, 1, keepdims=False)

    half_got = lax.ppermute(part_of(half_sum, 1 - side), "wsh", OTHER_SIDE)
    side_got = lax.ppermute(part_of(side_sum, 1 - half), "ctx", OTHER_HALF)
    d_q, d_kv = run_backward(meta, head_q, kv_all, head_attn, lse, head_d_attn)
    d_tokens, gathered = finish(
        d_q,
        d_kv.reshape(4, 8 * rows, 2 * HEAD_SIZE),
        group_act,
        small_term,
        head_blocks,
        branch_part.reshape(8 * rows, WIDTH),
        qkv_pieces,
        tokens[0],
        d_middle,
        gain_first,
    )
    gathered, half_got, side_got = lax.optimization_barrier((gathered, half_got, side_got))
    expert_own = jnp.concatenate(
        [
            part_of(half_sum, side).astype(F32) + half_got.astype(F32),
            part_of(side_sum, half).astype(F32) + side_got.astype(F32),
        ],
        axis=1,
    )
    d_w_qkv, d_w_out, rest = assemble(gathered, w_qkv)
    d_gain_first = rest[:, experts_count + 1] / gain_attn.astype(BF).astype(F32)
    return (
        output_rows[None],
        d_tokens[None],
        d_gain_first,
        d_w_qkv,
        d_w_out,
        rest[:, experts_count],
        rest[:, :experts_count],
        expert_own[0][None],
        expert_own[1][None],
        expert_own[2].T[None],
    )


def solution(mesh):
    placed = (
        P("wsh", "ctx", None),
        P(),
        P(),
        P("wsh", "ctx", None),
        P("wsh"),
        P("wsh", None),
        P("wsh", None),
        P("wsh"),
        P("wsh", None),
        P("ctx", "wsh", None),
        P("ctx", "wsh", None),
        P("ctx", None, "wsh"),
        P("wsh", "ctx", None),
    )
    return jax.shard_map(
        body,
        mesh=mesh,
        in_specs=placed,
        out_specs=(
            P("wsh", "ctx", None),
            P("wsh", "ctx", None),
            P("wsh"),
            P("wsh", None),
            P("wsh", None),
            P("wsh"),
            P("wsh", None),
            P("ctx", "wsh", None),
            P("ctx", "wsh", None),
            P("ctx", None, "wsh"),
        ),
        check_vma=False,
    )
```
